32 devices in a mesh: az: 4 (over y, x), rad: 8 (over z, core).
Axes of the slice: x: 2, y: 2, z: 4, core: 2. Of those that a mesh axis runs over, the one named last changes fastest.
Arguments:
- source_field: float32 [4096, 32, 128], P('az', 'rad'), may hold values from -6 to 6
- helmholtz: float32 [32], replicated, may hold values from 0.01 to 0.05
- azimuth_coef: float32 [32], replicated, may hold values from 0.2 to 0.5
- vertical_coef: float32 [32], replicated, may hold values from 1 to 4
- radial_coef: float32 [32], replicated, may hold values from 0.5 to 5
Outputs:
- pressure: float32 [4096, 32, 128], P('az', 'rad')
The draws below stay inside these ranges and needn't reach their ends.
All inputs are finite; a program needn't handle non-finite values.
Results may differ from the reference program's by a relative error of at most 0.00012.
Values sent between devices are 32-bit elements; how exact they have to be, the bound alone decides.
No kernel may reach another device: no remote copies, remote signals or barrier semaphores. Data moves between devices by JAX's collectives and lax.ppermute only.
A program may use at most 128 MiB of HBM per device.

```python
import math
import jax
import jax.numpy as jnp
from jax import lax

NT = 4096
NZ = 128
NR = 32


def spread_log(key, entries, lower_end, upper_end):
    uniform_values = jax.random.uniform(key, (entries,), jnp.float32)
    return jnp.exp(math.log(lower_end) + uniform_values * (math.log(upper_end) - math.log(lower_end)))


def plant_ends(values, lower_end, upper_end, seed_key):
    entries = values.shape[0]
    first_cell = jax.random.randint(seed_key, (), 0, entries)
    second_cell = (first_cell + entries // 2) % entries
    cell_ids = jnp.arange(entries, dtype=jnp.int32)
    values = jnp.where(cell_ids == first_cell, jnp.float32(lower_end), values)
    values = jnp.where(cell_ids == second_cell, jnp.float32(upper_end), values)
    return values


def draw_helmholtz(key, part):
    value_key = jax.random.fold_in(key, 11)
    place_key = jax.random.fold_in(key, 12)
    values = spread_log(value_key, NR, 0.01, 0.05)
    return plant_ends(values, 0.01, 0.05, place_key)


def draw_azimuth_coef(key, part):
    value_key = jax.random.fold_in(key, 21)
    place_key = jax.random.fold_in(key, 22)
    values = spread_log(value_key, NR, 0.2, 0.5)
    return plant_ends(values, 0.2, 0.5, place_key)


def draw_vertical_coef(key, part):
    value_key = jax.random.fold_in(key, 31)
    place_key = jax.random.fold_in(key, 32)
    values = spread_log(value_key, NR, 1.0, 4.0)
    return plant_ends(values, 1.0, 4.0, place_key)


def steps_of(rng, dims, cuts, low, high):
    loudness = 1.0
    for position, blocks in cuts:
        heights = jax.random.uniform(jax.random.fold_in(jax.random.fold_in(rng, 6), position), (blocks,), jnp.float32, low / len(cuts), high / len(cuts))
        loudness = loudness * jnp.repeat(jnp.exp(heights), dims[position] // blocks).reshape((-1,) + (1,) * (len(dims) - 1 - position))
    return loudness


def gaussian(stream_key, extent, scale, reach, shards=(), kind=jnp.bfloat16):
    array = jax.random.normal(stream_key, extent, jnp.float32) * scale
    if len(shards) > 0:
        array = steps_of(stream_key, extent, shards, -0.22, 0.18) * array
    return jnp.clip(array, min=-reach, max=reach).astype(kind)


def setup_inputs(seed: int = 0) -> dict:
    splits = jax.random.split(jax.random.key(seed), 6)
    source_field = gaussian(splits[0], (NT, NR, NZ), 1.0, 6.0, ((0, 4), (1, 8)), jnp.float32)
    helmholtz = draw_helmholtz(jax.random.fold_in(splits[5], 71), 0)
    azimuth_coef = draw_azimuth_coef(jax.random.fold_in(splits[5], 71), 0)
    vertical_coef = draw_vertical_coef(jax.random.fold_in(splits[5], 71), 0)
    radial_coef = jnp.clip(jnp.exp(jax.random.uniform(splits[4], (NR,), jnp.float32, math.log(0.5), math.log(5.0))), 0.5, 5.0)
    return {"source_field": source_field, "helmholtz": helmholtz, "azimuth_coef": azimuth_coef, "vertical_coef": vertical_coef, "radial_coef": radial_coef}


def cosine_matrix(depth):
    row_ids = jnp.arange(depth, dtype=jnp.int32)
    phases = (2 * row_ids[:, None] + 1) * row_ids[None, :] % (4 * depth)
    angles = math.pi / (2 * depth) * phases.astype(jnp.float32)
    scales = jnp.where(row_ids == 0, math.sqrt(1.0 / depth), math.sqrt(2.0 / depth)).astype(jnp.float32)
    return jnp.cos(angles) * scales[None, :]

def reference(source_field, helmholtz, azimuth_coef, vertical_coef, radial_coef):
    total_az, total_rad, depth = source_field.shape
    basis = cosine_matrix(depth).astype(source_field.dtype)
    layered = jnp.matmul(source_field, basis, precision=lax.Precision.HIGHEST)
    spectrum = jnp.fft.fft(layered, axis=0)
    stacked = jnp.stack([jnp.real(spectrum), jnp.imag(spectrum)], axis=-1)
    radius = jnp.arange(total_rad, dtype=jnp.int32)
    coupling = jnp.where(radius < total_rad - 1, radial_coef, jnp.zeros_like(radial_coef))
    previous = jnp.concatenate([jnp.zeros((1,), coupling.dtype), coupling[:-1]])
    level_ids = jnp.arange(depth, dtype=jnp.int32)
    vert_eig = 2.0 - 2.0 * jnp.cos(math.pi / depth * level_ids.astype(helmholtz.dtype))
    mode_ids = jnp.arange(total_az, dtype=jnp.int32)
    azim_eig = 2.0 - 2.0 * jnp.cos(2.0 * math.pi / total_az * mode_ids.astype(helmholtz.dtype))
    group_size = min(64, total_az)
    group_count = total_az // group_size
    stacked = stacked.reshape(group_count, group_size, total_rad, depth, 2)
    eig_groups = azim_eig.reshape(group_count, group_size)

    def solve_group(pieces):
        right_side, eigen = pieces
        diagonal = (helmholtz + coupling + previous)[None, None, :] + eigen[:, None, None] * azimuth_coef[None, None, :] + vert_eig[None, :, None] * vertical_coef[None, None, :]
        lower = jnp.broadcast_to(-previous, diagonal.shape)
        upper = jnp.broadcast_to(-coupling, diagonal.shape)
        system = jnp.transpose(right_side, (0, 2, 1, 3))
        answer = lax.linalg.tridiagonal_solve(lower, diagonal, upper, system)
        return jnp.transpose(answer, (0, 2, 1, 3))
    solved = lax.map(solve_group, (stacked, eig_groups)).reshape(total_az, total_rad, depth, 2)
    field = lax.complex(solved[..., 0], solved[..., 1])
    back = jnp.real(jnp.fft.ifft(field, axis=0))
    return jnp.matmul(back, basis.T, precision=lax.Precision.HIGHEST)
```

```python
import functools
import math

import jax
import jax.numpy as jnp
import ml_dtypes
import numpy as np
from jax import lax
from jax.experimental import pallas as pl
from jax.experimental.pallas import tpu as pltpu
from jax.sharding import PartitionSpec as P

F32 = jnp.float32
BF16 = jnp.bfloat16
CELLS = 4
SLABS = 4
LANES = 128
VMEM_LIMIT = 56 * 2**20


def two_halves(table):
    high = table.astype(np.float32).astype(ml_dtypes.bfloat16)
    low = (table - high.astype(np.float64)).astype(np.float32).astype(ml_dtypes.bfloat16)
    return high, low


def cosine_basis(depth):
    rows = np.arange(depth)
    phases = (2 * rows[:, None] + 1) * rows[None, :] % (4 * depth)
    scales = np.where(rows == 0, math.sqrt(1.0 / depth), math.sqrt(2.0 / depth))
    return np.cos(math.pi / (2 * depth) * phases) * scales[None, :]


def wide_basis(basis):
    high, low = two_halves(basis)
    top = np.concatenate([high, low], axis=1)
    bottom = np.concatenate([high, np.zeros_like(high)], axis=1)
    return np.concatenate([top, bottom], axis=0)


def slab_tables(length):
    quarter = length // 8
    half = quarter // 2
    offsets = np.arange(quarter) + 0.5
    stage = np.zeros((4, 2 * quarter, 2 * quarter))
    modes = np.zeros((4, 2 * quarter), np.int64)

    def angle(mode):
        return 2 * np.pi * (mode[:, None] * offsets[None, :] % length) / length

    def scale(mode):
        single = (mode == 0) | (mode == length // 2)
        return np.where(single, np.sqrt(1 / length), np.sqrt(2 / length))[:, None]

    steps = np.arange(half)
    for first, mode, column, wave in (
        (0, 8 * steps, 0, np.cos),
        (half, 8 * steps + 4, quarter, np.cos),
        (quarter, 8 * (steps + 1), 0, np.sin),
        (quarter + half, 8 * steps + 4, quarter, np.sin),
    ):
        stage[0, first : first + half, column : column + quarter] = scale(mode) * wave(angle(mode))
        modes[0, first : first + half] = mode
    for slot in (1, 2, 3):
        mode = slot + 8 * np.arange(quarter)
        cosine, sine = scale(mode) * np.cos(angle(mode)), scale(mode) * np.sin(angle(mode))
        stage[slot] = np.block([[cosine, sine], [sine, -cosine]])
        modes[slot] = np.concatenate([mode, mode])
    modes = modes.reshape(-1)
    parity = np.tile(np.repeat([1, -1], quarter), 4)
    single = (modes == 0) | (modes == length // 2)
    size = np.where(single, np.sqrt(1 / length), np.sqrt(2 / length))
    ends = size * np.where(parity > 0, np.cos(np.pi * modes / length), np.sin(np.pi * modes / length))
    eigen = 2.0 - 2.0 * np.cos(2 * np.pi * modes / length)
    return stage, eigen, ends, parity


def spread(column):
    return np.broadcast_to(column[..., None], column.shape + (LANES,)).astype(np.float32)


def split(values):
    high = values.astype(BF16)
    low = (values - high.astype(F32)).astype(BF16)
    return high, low


def dot(left, right):
    return jnp.dot(left, right, preferred_element_type=F32)


def times_basis(values, wide):
    high, low = split(values)
    both = dot(jnp.concatenate([high, low], axis=1), wide)
    depth = values.shape[1]
    return both[:, :depth] + both[:, depth:]


class Radial:
    def __init__(self, helmholtz, azimuth, vertical, radial, total):
        self.refs = (helmholtz, azimuth, vertical, radial)
        self.total = total

    def coupling(self, cell):
        cell = jnp.asarray(cell, jnp.int32)
        return jnp.where(cell < self.total - 1, self.refs[3][cell], 0.0)

    def previous(self, cell):
        cell = jnp.asarray(cell, jnp.int32)
        return jnp.where(cell > 0, self.refs[3][jnp.maximum(cell - 1, 0)], 0.0)

    def diagonal(self, cell, lam, mu):
        base = self.refs[0][cell] + self.coupling(cell) + self.previous(cell)
        return lam * self.refs[1][cell] + (mu * self.refs[2][cell] + base)


def inverse(values):
    return pl.reciprocal(values, approx=False)


def solve_block(radial, first, lam, mu, right, add_first=None, add_last=None):
    rows = []
    factor = values = None
    for place in range(CELLS):
        cell = first + place
        diagonal = radial.diagonal(cell, lam, mu)
        if place == 0 and add_first is not None:
            diagonal = diagonal - add_first
        if place == CELLS - 1 and add_last is not None:
            diagonal = diagonal - add_last
        if place > 0:
            before = radial.previous(cell)
            pivot = inverse(diagonal - before * factor)
            values = (right[place] + before * values) * pivot
        else:
            pivot = inverse(diagonal)
            values = right[place] * pivot
        factor = radial.coupling(cell) * pivot
        rows.append((values, factor))
    answer = [rows[-1][0]]
    for values, factor in rows[-2::-1]:
        answer.insert(0, values + factor * answer[0])
    return answer


def block_ports(radial, first, lam, mu):
    diagonals = [radial.diagonal(first + place, lam, mu) for place in range(CELLS)]
    pivot = inverse(diagonals[0])
    forward = [pivot]
    for place in range(1, CELLS):
        before = radial.previous(first + place)
        pivot = inverse(diagonals[place] - before * before * pivot)
        forward.append(pivot)
    last = forward[-1]
    cross = last
    for place in range(CELLS - 2, -1, -1):
        cross = radial.coupling(first + place) * forward[place] * cross
    backward = inverse(diagonals[-1])
    for place in range(CELLS - 2, -1, -1):
        after = radial.coupling(first + place)
        backward = inverse(diagonals[place] - after * after * backward)
    entry, leave = radial.previous(first), radial.coupling(first + CELLS - 1)
    return backward * entry, cross * leave, cross * entry, last * leave


def chip_ports(radial, first, lam, mu):
    b1, g1, b2, g2 = block_ports(radial, first, lam, mu)
    c1, h1, c2, h2 = block_ports(radial, first + CELLS, lam, mu)
    mid = inverse(1.0 - g2 * c1)
    low = c1 * b2 * mid
    high = h1 * mid
    whole = (
        b1 + g1 * low,
        g1 * high,
        c2 * (b2 + g2 * low),
        h2 + c2 * g2 * high,
    )
    return (b1, g1, b2, g2), (c1, h1, c2, h2), mid, whole


def forward_kernel(total, source, wide, stage_high, stage_low, lam, mu, *rest):
    radial = Radial(*rest[:4], total)
    spectrum, keep, send, high, low = rest[4:]
    length = source.shape[0]
    quarter = length // 8
    root = math.sqrt(0.5)
    core = lax.rem(lax.axis_index("rad"), 2)
    first = lax.axis_index("rad") * CELLS
    for cell in range(CELLS):
        x = [source[n * quarter : (n + 1) * quarter, cell, :] for n in range(8)]
        s = [x[n] + x[n + 4] for n in range(4)]
        d = [x[n] - x[n + 4] for n in range(4)]
        even, odd = s[0] + s[2], s[1] + s[3]
        minus, plus = root * (d[1] - d[3]), root * (d[1] + d[3])
        parts = (
            even + odd,
            even - odd,
            d[0] + minus,
            -plus - d[2],
            s[0] - s[2],
            s[3] - s[1],
            d[0] - minus,
            d[2] - plus,
        )
        for place, part in enumerate(parts):
            one, two = split(times_basis(part, wide[...]))
            slot, half = place // 2, place % 2
            rows = slice(half * quarter, (half + 1) * quarter)
            columns = slice(cell * LANES, (cell + 1) * LANES)
            high[slot, rows, columns] = one
            low[slot, rows, columns] = two
    for slot in range(4):
        result = (
            dot(stage_high[slot], high[slot])
            + dot(stage_high[slot], low[slot])
            + dot(stage_low[slot], high[slot])
        )
        for cell in range(CELLS):
            spectrum[cell, slot * 2 * quarter : (slot + 1) * 2 * quarter, :] = result[
                :, cell * LANES : (cell + 1) * LANES
            ]
    chunk = 32
    half = length // 2
    level = mu[...][:1]

    def step(index, _):
        ends = []
        for part in range(2):
            rows = pl.ds(pl.multiple_of(part * half + index * chunk, chunk), chunk)
            right = [spectrum[cell, rows, :] for cell in range(CELLS)]
            answer = solve_block(radial, first, lam[rows, :], level, right)
            ends.append((answer[0], answer[-1]))
        rows = pl.ds(pl.multiple_of(index * chunk, chunk), chunk)
        for place in range(2):
            keep[place, rows, :] = jnp.where(core == 0, ends[0][place], ends[1][place])
            send[place, rows, :] = jnp.where(core == 0, ends[1][place], ends[0][place])
        return 0

    lax.fori_loop(0, half // chunk, step, 0)


def pair_ports_kernel(total, lam, mu, *rest):
    radial = Radial(*rest[:4], total)
    (out,) = rest[4:]
    half = out.shape[1]
    core = lax.rem(lax.axis_index("rad"), 2)
    first = lax.axis_index("rad") // 2 * (2 * CELLS)
    level = mu[...][:1]
    chunk = 32

    def step(index, _):
        rows = pl.ds(pl.multiple_of(index * chunk, chunk), chunk)
        spot = pl.ds(pl.multiple_of(core * half + index * chunk, chunk), chunk)
        (b1, g1, b2, g2), (c1, h1, c2, h2), mid, _whole = chip_ports(
            radial, first, lam[spot, :], level
        )
        for place, value in enumerate((g1, b2, g2, c1, h1, c2, mid)):
            out[place, rows, :] = value
        return 0

    lax.fori_loop(0, half // chunk, step, 0)


def merge_kernel(chips, keep, got, ports, *rest):
    outs, whole = rest[:-1], rest[-1]
    half = keep.shape[1]
    core = lax.rem(lax.axis_index("rad"), 2)
    chip = lax.axis_index("rad") // 2
    chunk = 32

    def step(index, _):
        rows = pl.ds(pl.multiple_of(index * chunk, chunk), chunk)
        g1, b2, g2, c1, h1, c2, mid = (ports[place, rows, :] for place in range(7))
        mine = [keep[place, rows, :] for place in range(2)]
        other = [got[place, rows, :] for place in range(2)]
        low = [jnp.where(core == 0, m, o) for m, o in zip(mine, other)]
        high = [jnp.where(core == 0, o, m) for m, o in zip(mine, other)]
        upper = (high[0] + c1 * low[1]) * mid
        whole[0, rows, :] = low[0] + g1 * upper
        whole[1, rows, :] = high[1] + c2 * (low[1] + g2 * upper)
        return 0

    lax.fori_loop(0, half // chunk, step, 0)
    piece = half // chips
    for distance, out in enumerate(outs):
        target = lax.rem(chip + distance, chips)
        out[...] = whole[:, pl.ds(pl.multiple_of(target * piece, piece), piece), :]


def chain_ports_kernel(total, chips, lam, mu, *rest):
    radial = Radial(*rest[:4], total)
    (out,) = rest[4:]
    length = lam.shape[0]
    half = length // 2
    piece = half // chips
    core = lax.rem(lax.axis_index("rad"), 2)
    chip = lax.axis_index("rad") // 2
    level = mu[...][:1]
    chunk = min(64, piece)

    def step(index, _):
        rows = pl.ds(pl.multiple_of(index * chunk, chunk), chunk)
        start = core * half + chip * piece + index * chunk
        values = lam[pl.ds(pl.multiple_of(start, chunk), chunk), :]

        def link(place, carry):
            _one, _two, _mid, (b1, g1, b2, g2) = chip_ports(
                radial, place * (2 * CELLS), values, level
            )
            pivot = inverse(1.0 - b1 * carry)
            out[place, 0, rows, :] = b1
            out[place, 1, rows, :] = b2
            out[place, 2, rows, :] = pivot
            out[place, 3, rows, :] = g1 * pivot
            out[place, 4, rows, :] = carry
            return g2 + b2 * carry * g1 * pivot

        lax.fori_loop(0, chips, link, jnp.zeros((chunk, LANES), F32))
        return 0

    lax.fori_loop(0, piece // chunk, step, 0)


def chain_kernel(chips, ports, *rest):
    pieces, outs = rest[:chips], rest[chips : 2 * chips]
    ends, sides, before, start = rest[2 * chips :]
    chip = lax.axis_index("rad") // 2
    for distance, piece in enumerate(pieces):
        ends[lax.rem(chip + chips - distance, chips)] = piece[...]
    size = ports.shape[2]
    chunk = min(32, size)

    def step(index, _):
        rows = pl.ds(pl.multiple_of(index * chunk, chunk), chunk)
        value = jnp.zeros((chunk, LANES), F32)
        for place in range(chips):
            b1, b2, pivot = (ports[place, kind, rows, :] for kind in range(3))
            carry = ports[place, 4, rows, :]
            before[place] = value
            origin = (ends[place, 0, rows, :] + b1 * value) * pivot
            start[place] = origin
            value = ends[place, 1, rows, :] + b2 * (value + carry * origin)
        after = jnp.zeros((chunk, LANES), F32)
        for place in range(chips - 1, -1, -1):
            origin = start[place] + ports[place, 3, rows, :] * after
            sides[place, 0, rows, :] = before[place] + ports[place, 4, rows, :] * origin
            sides[place, 1, rows, :] = after
            after = origin
        return 0

    lax.fori_loop(0, size // chunk, step, 0)
    for distance, out in enumerate(outs):
        out[...] = sides[lax.rem(chip + distance, chips)]


def parts_kernel(chips, keep, got, ports, *rest):
    pieces = rest[:chips]
    own, send, sides = rest[chips:]
    half = keep.shape[1]
    piece_rows = half // chips
    core = lax.rem(lax.axis_index("rad"), 2)
    chip = lax.axis_index("rad") // 2
    for distance, piece in enumerate(pieces):
        target = lax.rem(chip + chips - distance, chips)
        sides[:, pl.ds(pl.multiple_of(target * piece_rows, piece_rows), piece_rows), :] = piece[...]
    chunk = 32

    def step(index, _):
        rows = pl.ds(pl.multiple_of(index * chunk, chunk), chunk)
        _g1, b2, g2, c1, h1, _c2, mid = (ports[place, rows, :] for place in range(7))
        left, right = sides[0, rows, :], sides[1, rows, :]
        last = jnp.where(core == 0, keep[1, rows, :], got[1, rows, :]) + b2 * left
        opening = jnp.where(core == 0, got[0, rows, :], keep[0, rows, :]) + h1 * right
        upper = (opening + c1 * last) * mid
        lower = last + g2 * upper
        own[0, rows, :] = jnp.where(core == 0, left, lower)
        own[1, rows, :] = jnp.where(core == 0, upper, right)
        send[0, rows, :] = jnp.where(core == 0, lower, left)
        send[1, rows, :] = jnp.where(core == 0, right, upper)
        return 0

    lax.fori_loop(0, half // chunk, step, 0)


def fold_rows(values):
    total = values[:8]
    for start in range(8, values.shape[0], 8):
        total = total + values[start : start + 8]
    return total


def ratios(radial, first, lam, mu, left_store, right_store):
    total = radial.total
    shape = lam.shape

    def leftward(cell, factor):
        pivot = inverse(radial.diagonal(cell, lam, mu) - radial.previous(cell) * factor)
        factor = radial.coupling(cell) * pivot
        left_store[cell] = factor
        return factor

    def rightward(step, factor):
        cell = total - 1 - step
        pivot = inverse(radial.diagonal(cell, lam, mu) - radial.coupling(cell) * factor)
        factor = radial.previous(cell) * pivot
        right_store[cell] = factor
        return factor

    zero = jnp.zeros(shape, F32)
    left = lax.fori_loop(0, first, leftward, zero)
    right = lax.fori_loop(0, total - CELLS - first, rightward, zero)
    return left, right


def ends_kernel(total, spectrum, lam, ends, mu, *rest):
    radial = Radial(*rest[:4], total)
    out, store, sums = rest[4:]
    first = lax.axis_index("rad") * CELLS
    level = mu[...][:1]
    chunk = spectrum.shape[1] // 8
    sums[...] = jnp.zeros_like(sums)

    def step(index, _):
        kind = lax.rem(index, 2)
        rows = pl.ds(pl.multiple_of(index * chunk, chunk), chunk)
        values = lam[rows, :]
        left, right = ratios(radial, first, values, level, store, store)
        weight = 2.0 * ends[rows, :]
        answer = solve_block(
            radial,
            first,
            values,
            level,
            [weight * spectrum[cell, rows, :] for cell in range(CELLS)],
            radial.previous(first) * left,
            radial.coupling(first + CELLS - 1) * right,
        )
        for place in range(CELLS):
            sums[kind, first + place] += fold_rows(answer[place])

        def outward_left(move, value):
            cell = first - 1 - move
            value = store[cell] * value
            sums[kind, cell] += fold_rows(value)
            return value

        def outward_right(cell, value):
            value = store[cell] * value
            sums[kind, cell] += fold_rows(value)
            return value

        lax.fori_loop(0, first, outward_left, answer[0])
        lax.fori_loop(first + CELLS, total, outward_right, answer[-1])
        return 0

    lax.fori_loop(0, 8, step, 0)
    for kind in range(2):
        for cell in range(total):
            out[kind, cell : cell + 1, :] = jnp.sum(sums[kind, cell], axis=0, keepdims=True)


def response_kernel(total, lam, weight, mu, *rest):
    radial = Radial(*rest[:4], total)
    out, store, sums = rest[4:]
    first = lax.axis_index("rad") * CELLS
    level = mu[pl.ds(lax.axis_index("az"), 1), :]
    group = LANES // SLABS
    chunk = lam.shape[1] // 2
    sums[...] = jnp.zeros_like(sums)

    def step(index, _):
        kind = index // 2
        rows = pl.ds(pl.multiple_of(lax.rem(index, 2) * chunk, chunk), chunk)
        values = lam[kind, rows, :]
        left, right = ratios(radial, first, values, level, store, store)
        source = weight[kind, rows, :]
        zero = jnp.zeros_like(source)
        openings, closings = [], []
        for place in range(CELLS):
            answer = solve_block(
                radial,
                first,
                values,
                level,
                [source if cell == place else zero for cell in range(CELLS)],
                radial.previous(first) * left,
                radial.coupling(first + CELLS - 1) * right,
            )
            for cell in range(CELLS):
                sums[kind, place, first + cell] += fold_rows(answer[cell])
            openings.append(answer[0])
            closings.append(answer[-1])

        def outward(cell, factor, edges):
            factor = store[cell] * factor
            for place in range(CELLS):
                sums[kind, place, cell] += fold_rows(factor * edges[place])
            return factor

        one = jnp.ones_like(source)
        lax.fori_loop(
            0, first, lambda move, factor: outward(first - 1 - move, factor, openings), one
        )
        lax.fori_loop(
            first + CELLS, total, lambda cell, factor: outward(cell, factor, closings), one
        )
        return 0

    lax.fori_loop(0, 4, step, 0)
    lane = lax.broadcasted_iota(jnp.int32, (1, LANES), 1) // group

    def close(cell, _):
        for kind in range(2):
            result = jnp.zeros((1, LANES), F32)
            for place in range(CELLS):
                row = jnp.sum(sums[kind, place, cell], axis=0, keepdims=True)
                row = row + pltpu.roll(row, 2 * group, 1)
                row = row + pltpu.roll(row, group, 1)
                result = jnp.where(lane == place, row, result)
            out[kind, pl.ds(cell, 1), :] = result
        return 0

    lax.fori_loop(0, total, close, 0)


def invert(matrix, total):
    rows = lax.broadcasted_iota(jnp.int32, (total, LANES), 0)

    def step(pivot, _):
        mark = rows == pivot
        scale = 1.0 / matrix[pivot, pl.ds(pivot, 1), :]
        line = jnp.where(mark, 1.0, matrix[pivot]) * scale

        def row(index, _):
            factor = matrix[index, pl.ds(pivot, 1), :]
            matrix[index] = jnp.where(mark, 0.0, matrix[index]) - factor * line
            return 0

        lax.fori_loop(0, total, row, 0, unroll=8)
        matrix[pivot] = line
        return 0

    lax.fori_loop(0, total, step, 0)


def capacity_kernel(total, chips, azimuth, *rest):
    pieces = rest[:chips]
    first_out, second_out, sum_matrix = rest[chips:]
    chip = lax.axis_index("rad") // 2
    core = lax.rem(lax.axis_index("rad"), 2)
    group = LANES // SLABS
    lane = lax.broadcasted_iota(jnp.int32, (1, LANES), 1) // group
    cells = lax.broadcasted_iota(jnp.int32, (total, LANES), 0)
    for distance, piece in enumerate(pieces):
        origin = lax.rem(chip + chips - distance, chips)
        for side in range(2):
            block = 2 * origin + lax.rem(core + side, 2)
            for kind in range(2):
                packed = piece[side, kind]
                for place in range(CELLS):
                    row = jnp.where(lane == place, packed, 0.0)
                    row = row + pltpu.roll(row, 2 * group, 1)
                    row = row + pltpu.roll(row, group, 1)
                    cell = block * CELLS + place
                    own = jnp.where(cells == cell, 0.5 / azimuth[cell], 0.0)
                    if kind == 0:
                        sum_matrix[cell] = own + row
                    else:
                        first_out[cell] = own - row
    invert(first_out, total)
    weight = jnp.where(lane < 2, 0.25, 0.0)

    def column(cell, value):
        return jnp.where(cells == cell, 1.0 / azimuth[cell], value)

    scale = lax.fori_loop(0, total, column, jnp.zeros((total, LANES), F32)) * weight

    def add(cell, _):
        second_out[cell] = sum_matrix[cell] + first_out[cell] * scale * (1.0 / azimuth[cell])
        return 0

    lax.fori_loop(0, total, add, 0)
    invert(second_out, total)


def apply_matrix(matrix, vector):
    total = vector.shape[0]
    result = matrix[0] * vector[0:1, :]
    for cell in range(1, total):
        result = result + matrix[cell] * vector[cell : cell + 1, :]
    return result


def times_i(values):
    group = LANES // SLABS
    lane = lax.broadcasted_iota(jnp.int32, (1, LANES), 1) // group
    ahead = pltpu.roll(values, group, 1)
    behind = pltpu.roll(values, LANES - group, 1)
    return jnp.where(lane == 0, -behind, jnp.where(lane == 1, ahead, 0.0))


def slabs_kernel(total, azimuth, first_matrix, second_matrix, *rest):
    pieces, outs = rest[:SLABS], rest[SLABS : 2 * SLABS]
    values, results = rest[2 * SLABS :]
    slab = lax.axis_index("az")
    group = LANES // SLABS
    lane = lax.broadcasted_iota(jnp.int32, (1, LANES), 1) // group
    cells = lax.broadcasted_iota(jnp.int32, (total, LANES), 0)
    for distance, piece in enumerate(pieces):
        values[slab ^ distance] = piece[...]

    def channels(kind):
        u = [values[place, kind] for place in range(SLABS)]
        mixed = (u[0] - u[2], u[3] - u[1], (u[0] + u[2]) - (u[1] + u[3]))
        result = jnp.zeros((total, LANES), F32)
        for channel, value in enumerate(mixed):
            shift = lax.rem(channel - slab + SLABS, SLABS) * group
            result = jnp.where(lane == channel, pltpu.roll(value, shift, 1), result)
        return result

    def column(cell, value):
        return jnp.where(cells == cell, 0.5 / azimuth[cell], value)

    scale = lax.fori_loop(0, total, column, jnp.zeros((total, LANES), F32))
    sums, differences = channels(0), channels(1)
    lead = apply_matrix(first_matrix, differences)
    plus = apply_matrix(second_matrix, times_i(lead) * scale - sums)
    plus = jnp.where(lane < 3, plus, 0.0)
    minus = lead + apply_matrix(first_matrix, times_i(plus) * scale)
    minus = jnp.where(lane < 3, minus, 0.0)
    for kind, value in enumerate((plus, minus)):
        parts = []
        for channel in range(3):
            shift = lax.rem(slab - channel + SLABS, SLABS) * group
            part = pltpu.roll(value, shift, 1)
            parts.append(jnp.where(lane == slab, part, 0.0))
        real, imag, alternate = parts
        results[0, kind] = 0.25 * (2.0 * real + alternate)
        results[1, kind] = 0.25 * (-2.0 * imag - alternate)
        results[2, kind] = 0.25 * (alternate - 2.0 * real)
        results[3, kind] = 0.25 * (2.0 * imag - alternate)
    for distance, out in enumerate(outs):
        out[...] = results[slab ^ distance]


def sides_kernel(total, lam, ends, mu, *rest):
    radial = Radial(*rest[:4], total)
    pieces = rest[4 : 4 + SLABS]
    sources, out = rest[4 + SLABS :]
    sources[...] = (pieces[0][...] + pieces[1][...]) + (pieces[2][...] + pieces[3][...])
    first = lax.axis_index("rad") * CELLS
    level = mu[...][:1]
    chunk = lam.shape[0] // 8

    def step(index, _):
        kind = lax.rem(index, 2)
        rows = pl.ds(pl.multiple_of(index * chunk, chunk), chunk)
        values = lam[rows, :]
        zero = jnp.zeros((chunk, LANES), F32)

        def leftward(cell, carry):
            factor, value = carry
            before = radial.previous(cell)
            pivot = inverse(radial.diagonal(cell, values, level) - before * factor)
            value = (sources[kind, pl.ds(cell, 1), :] + before * value) * pivot
            return radial.coupling(cell) * pivot, value

        def rightward(move, carry):
            cell = total - 1 - move
            factor, value = carry
            after = radial.coupling(cell)
            pivot = inverse(radial.diagonal(cell, values, level) - after * factor)
            value = (sources[kind, pl.ds(cell, 1), :] + after * value) * pivot
            return radial.previous(cell) * pivot, value

        left, left_value = lax.fori_loop(0, first, leftward, (zero, zero))
        right, right_value = lax.fori_loop(0, total - CELLS - first, rightward, (zero, zero))
        entry, leave = radial.previous(first), radial.coupling(first + CELLS - 1)
        own = [sources[kind, pl.ds(first + place, 1), :] for place in range(CELLS)]
        own[0] = own[0] + entry * left_value
        own[-1] = own[-1] + leave * right_value
        answer = solve_block(radial, first, values, level, own, entry * left, leave * right)
        weight = ends[rows, :]
        out[0, rows, :] = weight * (left_value + left * answer[0])
        out[1, rows, :] = weight * (right_value + right * answer[-1])
        return 0

    lax.fori_loop(0, 8, step, 0)


def backward_kernel(total, spectrum, own, got, extra, sources, wide, stage_high, stage_low, *rest):
    lam, ends, mu = rest[:3]
    radial = Radial(*rest[3:7], total)
    out, high, low, middle = rest[7:]
    length = spectrum.shape[1]
    quarter = length // 8
    half = length // 2
    root = math.sqrt(0.5)
    core = lax.rem(lax.axis_index("rad"), 2)
    first = lax.axis_index("rad") * CELLS
    level = mu[...][:1]
    chunk = 32
    entry, leave = radial.previous(first), radial.coupling(first + CELLS - 1)

    for slot in range(4):

        def step(index, _):
            kind = index // (quarter // chunk)
            spot = pl.ds(pl.multiple_of(index * chunk, chunk), chunk)
            rows = pl.ds(pl.multiple_of(slot * 2 * quarter + index * chunk, chunk), chunk)
            near = pl.ds(pl.multiple_of(slot % 2 * 2 * quarter + index * chunk, chunk), chunk)
            mine = core == slot // 2
            side = [
                jnp.where(mine, own[place, near, :], got[place, near, :]) + extra[place, rows, :]
                for place in range(2)
            ]
            weight = ends[rows, :]
            right = [
                spectrum[cell, rows, :] + weight * sources[kind, pl.ds(first + cell, 1), :]
                for cell in range(CELLS)
            ]
            right[0] = right[0] + entry * side[0]
            right[-1] = right[-1] + leave * side[1]
            answer = solve_block(radial, first, lam[rows, :], level, right)
            for cell in range(CELLS):
                one, two = split(answer[cell])
                columns = slice(cell * LANES, (cell + 1) * LANES)
                high[slot, spot, columns] = one
                low[slot, spot, columns] = two
            return 0

        lax.fori_loop(0, 2 * quarter // chunk, step, 0)
        middle[slot] = (
            dot(stage_high[slot], high[slot])
            + dot(stage_high[slot], low[slot])
            + dot(stage_low[slot], high[slot])
        )
    for cell in range(CELLS):
        columns = slice(cell * LANES, (cell + 1) * LANES)
        y = [
            middle[place // 2, place % 2 * quarter : (place % 2 + 1) * quarter, columns]
            for place in range(8)
        ]
        plus, minus = y[0] + y[1], y[0] - y[1]
        s = (plus + y[4], minus - y[5], plus - y[4], minus + y[5])
        real, imag = root * (y[2] - y[6]), root * (y[3] + y[7])
        d = (y[2] + y[6], real - imag, y[7] - y[3], -real - imag)
        for n in range(4):
            for sign in range(2):
                value = s[n] + d[n] if sign == 0 else s[n] - d[n]
                place = n + 4 * sign
                out[place * quarter : (place + 1) * quarter, cell, :] = times_basis(
                    value, wide[...]
                )


def call(kernel, out_shapes, args, scalars=(), scratch=(), flops=0, name=None):
    specs = [
        pl.BlockSpec(memory_space=pltpu.SMEM if place in scalars else pltpu.VMEM)
        for place in range(len(args))
    ]
    outs = [jax.ShapeDtypeStruct(shape, F32) for shape in out_shapes]
    moved = sum(math.prod(shape) for shape in out_shapes) + sum(math.prod(a.shape) for a in args)
    return pl.pallas_call(
        kernel,
        out_shape=outs,
        in_specs=specs,
        out_specs=[pl.BlockSpec(memory_space=pltpu.VMEM)] * len(outs),
        scratch_shapes=list(scratch),
        compiler_params=pltpu.CompilerParams(vmem_limit_bytes=VMEM_LIMIT),
        cost_estimate=pl.CostEstimate(flops=flops, bytes_accessed=4 * moved, transcendentals=0),
        name=name,
    )(*args)


def other_core(values):
    count = lax.axis_size("rad")
    return lax.ppermute(values, "rad", [(index, index ^ 1) for index in range(count)])


def along_chips(values, distance):
    chips = lax.axis_size("rad") // 2
    route = [
        (2 * chip + core, 2 * ((chip + distance) % chips) + core)
        for chip in range(chips)
        for core in range(2)
    ]
    return lax.ppermute(values, "rad", route)


def across_slabs(values, distance):
    return lax.ppermute(values, "az", [(slab, slab ^ distance) for slab in range(SLABS)])


def on_device(source, helmholtz, azimuth, vertical, radial):
    length, cells, depth = source.shape
    blocks = lax.axis_size("rad")
    chips = blocks // 2
    total = blocks * cells
    assert cells == CELLS and depth == LANES and lax.axis_size("az") == SLABS
    half = length // 2
    piece = half // chips
    quarter = length // 8
    scalars4 = (helmholtz, azimuth, vertical, radial)

    basis = cosine_basis(depth)
    stage, eigen, end_weights, parity = slab_tables(length)
    stage_high, stage_low = two_halves(stage)
    back_high, back_low = two_halves(np.swapaxes(stage, 1, 2))
    lam = jnp.asarray(spread(eigen))
    ends = jnp.asarray(spread(end_weights))
    vertical_eigen = 2.0 - 2.0 * np.cos(math.pi / depth * np.arange(depth))
    mu = jnp.asarray(np.broadcast_to(vertical_eigen[None, :], (8, depth)).astype(np.float32))
    group = depth // SLABS
    mu_groups = jnp.asarray(
        np.tile(vertical_eigen.reshape(SLABS, group), (1, SLABS)).astype(np.float32)
    )

    def packed(column):
        table = np.stack([column[parity > 0], column[parity < 0]]).reshape(2, quarter, SLABS)
        return jnp.asarray(np.repeat(table, group, axis=2).astype(np.float32))

    lam_groups = packed(eigen)
    weight_groups = packed(2.0 * end_weights**2)

    def smem(start):
        return tuple(range(start, start + 4))

    spectrum, keep, send = call(
        functools.partial(forward_kernel, total),
        [(CELLS, length, LANES), (2, half, LANES), (2, half, LANES)],
        (source, jnp.asarray(wide_basis(basis)), jnp.asarray(stage_high), jnp.asarray(stage_low), lam, mu)
        + scalars4,
        smem(6),
        [pltpu.VMEM((4, 2 * quarter, CELLS * LANES), BF16)] * 2,
        name="forward",
    )
    got = other_core(send)
    (ports,) = call(
        functools.partial(pair_ports_kernel, total),
        [(7, half, LANES)],
        (lam, mu) + scalars4,
        smem(2),
        name="pair_ports",
    )
    merged = call(
        functools.partial(merge_kernel, chips),
        [(2, piece, LANES)] * chips,
        (keep, got, ports),
        (),
        [pltpu.VMEM((2, half, LANES), F32)],
        name="merge",
    )
    gathered = [merged[0]] + [along_chips(merged[d], d) for d in range(1, chips)]
    (chain_ports,) = call(
        functools.partial(chain_ports_kernel, total, chips),
        [(chips, 5, piece, LANES)],
        (lam, mu) + scalars4,
        smem(2),
        name="chain_ports",
    )
    chain_chunk = min(32, piece)
    sides = call(
        functools.partial(chain_kernel, chips),
        [(2, piece, LANES)] * chips,
        (chain_ports, *gathered),
        (),
        [pltpu.VMEM((chips, 2, piece, LANES), F32)] * 2
        + [pltpu.VMEM((chips, chain_chunk, LANES), F32)] * 2,
        name="chain",
    )
    returned = [sides[0]] + [along_chips(sides[d], d) for d in range(1, chips)]
    own_sides, send_sides = call(
        functools.partial(parts_kernel, chips),
        [(2, half, LANES)] * 2,
        (keep, got, ports, *returned),
        (),
        [pltpu.VMEM((2, half, LANES), F32)],
        name="parts",
    )
    got_sides = other_core(send_sides)

    (response,) = call(
        functools.partial(response_kernel, total),
        [(2, total, LANES)],
        (lam_groups, weight_groups, mu_groups) + scalars4,
        smem(3),
        [
            pltpu.VMEM((total, quarter // 2, LANES), F32),
            pltpu.VMEM((2, CELLS, total, 8, LANES), F32),
        ],
        name="response",
    )
    both = jnp.stack([response, other_core(response)])
    responses = [both] + [along_chips(both, d) for d in range(1, chips)]
    first_matrix, second_matrix = call(
        functools.partial(capacity_kernel, total, chips),
        [(total, total, LANES)] * 2,
        (azimuth, *responses),
        (0,),
        [pltpu.VMEM((total, total, LANES), F32)],
        name="capacity",
    )

    (partial_ends,) = call(
        functools.partial(ends_kernel, total),
        [(2, total, LANES)],
        (spectrum, lam, ends, mu) + scalars4,
        smem(4),
        [
            pltpu.VMEM((total, quarter, LANES), F32),
            pltpu.VMEM((2, total, 8, LANES), F32),
        ],
        name="ends",
    )
    pair_ends = partial_ends + other_core(partial_ends)
    slab_ends = pair_ends + sum(along_chips(pair_ends, d) for d in range(1, chips))
    all_ends = [slab_ends] + [across_slabs(slab_ends, d) for d in range(1, SLABS)]
    end_sources = call(
        functools.partial(slabs_kernel, total),
        [(2, total, LANES)] * SLABS,
        (azimuth, first_matrix, second_matrix, *all_ends),
        (0,),
        [pltpu.VMEM((SLABS, 2, total, LANES), F32)] * 2,
        name="slabs",
    )
    sources = [end_sources[0]] + [across_slabs(end_sources[d], d) for d in range(1, SLABS)]
    all_sources, extra = call(
        functools.partial(sides_kernel, total),
        [(2, total, LANES), (2, length, LANES)],
        (lam, ends, mu) + scalars4 + tuple(sources),
        smem(3),
        name="sides",
    )
    (pressure,) = call(
        functools.partial(backward_kernel, total),
        [(length, CELLS, LANES)],
        (
            spectrum,
            own_sides,
            got_sides,
            extra,
            all_sources,
            jnp.asarray(wide_basis(basis.T)),
            jnp.asarray(back_high),
            jnp.asarray(back_low),
            lam,
            ends,
            mu,
        )
        + scalars4,
        smem(11),
        [pltpu.VMEM((4, 2 * quarter, CELLS * LANES), BF16)] * 2
        + [pltpu.VMEM((4, 2 * quarter, CELLS * LANES), F32)],
        name="backward",
    )
    return pressure


def solution(mesh):
    in_specs = (P("az", "rad", None), P(), P(), P(), P())
    return jax.shard_map(
        on_device,
        mesh=mesh,
        in_specs=in_specs,
        out_specs=P("az", "rad", None),
        check_vma=False,
    )
```

```python
import functools
import math

import jax
import jax.numpy as jnp
import ml_dtypes
import numpy as np
from jax import lax
from jax.experimental import pallas as pl
from jax.experimental.pallas import tpu as pltpu
from jax.sharding import PartitionSpec as P

F32 = jnp.float32
BF16 = jnp.bfloat16
CELLS = 4
SLABS = 4
LANES = 128


def two_halves(table):
    high = table.astype(np.float32).astype(ml_dtypes.bfloat16)
    low = (table - high.astype(np.float64)).astype(np.float32).astype(ml_dtypes.bfloat16)
    return high, low


def cosine_basis(depth):
    rows = np.arange(depth)
    phases = (2 * rows[:, None] + 1) * rows[None, :] % (4 * depth)
    scales = np.where(rows == 0, math.sqrt(1.0 / depth), math.sqrt(2.0 / depth))
    return np.cos(math.pi / (2 * depth) * phases) * scales[None, :]


def wide_basis(basis):
    high, low = two_halves(basis)
    top = np.concatenate([high, low], axis=1)
    bottom = np.concatenate([high, np.zeros_like(high)], axis=1)
    return np.concatenate([top, bottom], axis=0)


def slab_tables(length):
    quarter = length // 8
    half = quarter // 2
    offsets = np.arange(quarter) + 0.5
    stage = np.zeros((4, 2 * quarter, 2 * quarter))
    modes = np.zeros((4, 2 * quarter), np.int64)

    def angle(mode):
        return 2 * np.pi * (mode[:, None] * offsets[None, :] % length) / length

    def scale(mode):
        single = (mode == 0) | (mode == length // 2)
        return np.where(single, np.sqrt(1 / length), np.sqrt(2 / length))[:, None]

    steps = np.arange(half)
    for first, mode, column, wave in (
        (0, 8 * steps, 0, np.cos),
        (half, 8 * steps + 4, quarter, np.cos),
        (quarter, 8 * (steps + 1), 0, np.sin),
        (quarter + half, 8 * steps + 4, quarter, np.sin),
    ):
        stage[0, first : first + half, column : column + quarter] = scale(mode) * wave(angle(mode))
        modes[0, first : first + half] = mode
    for slot in (1, 2, 3):
        mode = slot + 8 * np.arange(quarter)
        cosine, sine = scale(mode) * np.cos(angle(mode)), scale(mode) * np.sin(angle(mode))
        stage[slot] = np.block([[cosine, sine], [sine, -cosine]])
        modes[slot] = np.concatenate([mode, mode])
    modes = modes.reshape(-1)
    parity = np.tile(np.repeat([1, -1], quarter), 4)
    single = (modes == 0) | (modes == length // 2)
    size = np.where(single, np.sqrt(1 / length), np.sqrt(2 / length))
    ends = size * np.where(parity > 0, np.cos(np.pi * modes / length), np.sin(np.pi * modes / length))
    eigen = 2.0 - 2.0 * np.cos(2 * np.pi * modes / length)
    return stage, eigen, ends, parity


def spread(column):
    return np.broadcast_to(column[..., None], column.shape + (LANES,)).astype(np.float32)


def split(values):
    high = values.astype(BF16)
    low = (values - high.astype(F32)).astype(BF16)
    return high, low


def dot(left, right):
    return jnp.dot(left, right, preferred_element_type=F32)


def times_basis(values, wide):
    high, low = split(values)
    both = dot(jnp.concatenate([high, low], axis=1), wide)
    depth = values.shape[1]
    return both[:, :depth] + both[:, depth:]


class Radial:
    def __init__(self, helmholtz, azimuth, vertical, radial, total):
        self.refs = (helmholtz, azimuth, vertical, radial)
        self.total = total

    def coupling(self, cell):
        cell = jnp.asarray(cell, jnp.int32)
        return jnp.where(cell < self.total - 1, self.refs[3][cell], 0.0)

    def previous(self, cell):
        cell = jnp.asarray(cell, jnp.int32)
        return jnp.where(cell > 0, self.refs[3][jnp.maximum(cell - 1, 0)], 0.0)

    def diagonal(self, cell, lam, mu):
        base = self.refs[0][cell] + self.coupling(cell) + self.previous(cell)
        return lam * self.refs[1][cell] + (mu * self.refs[2][cell] + base)


def inverse(values):
    return pl.reciprocal(values, approx=False)


def solve_block(radial, first, lam, mu, right, add_first=None, add_last=None):
    rows = []
    factor = values = None
    for place in range(CELLS):
        cell = first + place
        diagonal = radial.diagonal(cell, lam, mu)
        if place == 0 and add_first is not None:
            diagonal = diagonal - add_first
        if place == CELLS - 1 and add_last is not None:
            diagonal = diagonal - add_last
        if place > 0:
            before = radial.previous(cell)
            pivot = inverse(diagonal - before * factor)
            values = (right[place] + before * values) * pivot
        else:
            pivot = inverse(diagonal)
            values = right[place] * pivot
        factor = radial.coupling(cell) * pivot
        rows.append((values, factor))
    answer = [rows[-1][0]]
    for values, factor in rows[-2::-1]:
        answer.insert(0, values + factor * answer[0])
    return answer


def block_ports(radial, first, lam, mu):
    diagonals = [radial.diagonal(first + place, lam, mu) for place in range(CELLS)]
    pivot = inverse(diagonals[0])
    forward = [pivot]
    for place in range(1, CELLS):
        before = radial.previous(first + place)
        pivot = inverse(diagonals[place] - before * before * pivot)
        forward.append(pivot)
    last = forward[-1]
    cross = last
    for place in range(CELLS - 2, -1, -1):
        cross = radial.coupling(first + place) * forward[place] * cross
    backward = inverse(diagonals[-1])
    for place in range(CELLS - 2, -1, -1):
        after = radial.coupling(first + place)
        backward = inverse(diagonals[place] - after * after * backward)
    entry, leave = radial.previous(first), radial.coupling(first + CELLS - 1)
    return backward * entry, cross * leave, cross * entry, last * leave


def chip_ports(radial, first, lam, mu):
    b1, g1, b2, g2 = block_ports(radial, first, lam, mu)
    c1, h1, c2, h2 = block_ports(radial, first + CELLS, lam, mu)
    mid = inverse(1.0 - g2 * c1)
    low = c1 * b2 * mid
    high = h1 * mid
    whole = (
        b1 + g1 * low,
        g1 * high,
        c2 * (b2 + g2 * low),
        h2 + c2 * g2 * high,
    )
    return (b1, g1, b2, g2), (c1, h1, c2, h2), mid, whole


def spread_parts(x):
    root = math.sqrt(0.5)
    s = [x[n] + x[n + 4] for n in range(4)]
    d = [x[n] - x[n + 4] for n in range(4)]
    even, odd = s[0] + s[2], s[1] + s[3]
    minus, plus = root * (d[1] - d[3]), root * (d[1] + d[3])
    return (
        even + odd,
        even - odd,
        d[0] + minus,
        -plus - d[2],
        s[0] - s[2],
        s[3] - s[1],
        d[0] - minus,
        d[2] - plus,
    )


def gather_parts(y):
    root = math.sqrt(0.5)
    plus, minus = y[0] + y[1], y[0] - y[1]
    s = (plus + y[4], minus - y[5], plus - y[4], minus + y[5])
    real, imag = root * (y[2] - y[6]), root * (y[3] + y[7])
    d = (y[2] + y[6], real - imag, y[7] - y[3], -real - imag)
    return [s[n] + d[n] for n in range(4)] + [s[n] - d[n] for n in range(4)]


def forward_kernel(total, source_in, tables_in, stages_in, *rest):
    scalars_in = rest[:4]
    spectrum, keep, send = rest[4:7]
    source, tables, stages, s0, s1, s2, s3, wide_rows, high, low, sems = rest[7:]
    scalars = (s0, s1, s2, s3)
    pairs = [(source_in, source), (stages_in, stages), (tables_in, tables)]
    pairs += list(zip(scalars_in, scalars))
    copies = [
        pltpu.make_async_copy(origin, target, sems.at[place])
        for place, (origin, target) in enumerate(pairs)
    ]
    for copy in copies:
        copy.start()
    radial = Radial(*scalars, total)
    length = source.shape[0] // CELLS
    quarter = length // 8
    core = lax.rem(lax.axis_index("rad"), 2)
    first = lax.axis_index("rad") * CELLS
    chunk = 16
    copies[0].wait()
    for cell in range(CELLS):
        for start in range(0, quarter, chunk):
            x = [
                source[pl.ds((n * quarter + start) * CELLS + cell, chunk, stride=CELLS), :]
                for n in range(8)
            ]
            for place, part in enumerate(spread_parts(x)):
                one, two = split(part)
                row = cell * length + place * quarter + start
                wide_rows[row : row + chunk, :LANES] = one
                wide_rows[row : row + chunk, LANES:] = two
    copies[1].wait()
    wide = stages[8 * 2 * quarter : 8 * 2 * quarter + 2 * LANES, :]
    for cell in range(CELLS):
        for slot in range(4):
            row = cell * length + slot * 2 * quarter
            both = dot(wide_rows[row : row + 2 * quarter, :], wide)
            one, two = split(both[:, :LANES] + both[:, LANES:])
            columns = slice(cell * LANES, (cell + 1) * LANES)
            high[slot, :, columns] = one
            low[slot, :, columns] = two
    for slot in range(4):
        upper = stages[slot * 2 * quarter : (slot + 1) * 2 * quarter, :]
        lower = stages[(4 + slot) * 2 * quarter : (5 + slot) * 2 * quarter, :]
        result = dot(upper, high[slot]) + dot(upper, low[slot]) + dot(lower, high[slot])
        for cell in range(CELLS):
            spectrum[cell, slot * 2 * quarter : (slot + 1) * 2 * quarter, :] = result[
                :, cell * LANES : (cell + 1) * LANES
            ]
    for copy in copies[2:]:
        copy.wait()
    chunk = 64
    half = length // 2
    level = tables[length : length + 1, :]

    def step(index, _):
        ends = []
        for part in range(2):
            rows = pl.ds(pl.multiple_of(part * half + index * chunk, chunk), chunk)
            right = [spectrum[cell, rows, :] for cell in range(CELLS)]
            answer = solve_block(radial, first, tables[rows, :], level, right)
            ends.append((answer[0], answer[-1]))
        rows = pl.ds(pl.multiple_of(index * chunk, chunk), chunk)
        for place in range(2):
            keep[place, rows, :] = jnp.where(core == 0, ends[0][place], ends[1][place])
            send[place, rows, :] = jnp.where(core == 0, ends[1][place], ends[0][place])
        return 0

    lax.fori_loop(0, half // chunk, step, 0)


def shared_row(slot, kind, quarter):
    return pl.multiple_of(jnp.where(slot == 0, kind, slot + 1) * quarter, quarter)


def pair_ports_kernel(total, lam, mu, edges, *rest):
    radial = Radial(*rest[:4], total)
    (out,) = rest[4:]
    half = out.shape[1]
    quarter = half // 4
    chips = total // (2 * CELLS)
    core = lax.rem(lax.axis_index("rad"), 2)
    chip = lax.axis_index("rad") // 2
    left_side = chip < chips // 2
    first = chip * (2 * CELLS)
    level = mu[...][:1]
    chunk = min(64, quarter)

    def step(index, _):
        rows = pl.ds(pl.multiple_of(index * chunk, chunk), chunk)
        spot = pl.ds(pl.multiple_of(core * half + index * chunk, chunk), chunk)
        block = index * chunk // quarter
        start = shared_row(core * 2 + block // 2, lax.rem(block, 2), quarter)
        spot5 = pl.ds(pl.multiple_of(start + lax.rem(index * chunk, quarter), chunk), chunk)
        (b1, g1, b2, g2), (c1, h1, c2, h2), mid, (w1, w2, w3, w4) = chip_ports(
            radial, first, lam[spot, :], level
        )
        for place, value in enumerate((g1, b2, g2, c1, h1, c2, mid)):
            out[place, rows, :] = value
        left, right = edges[0, spot5, :], edges[1, spot5, :]
        far, near = jnp.where(left_side, left, right), jnp.where(left_side, right, left)
        rff, rnn = jnp.where(left_side, w1, w4), jnp.where(left_side, w4, w1)
        rfn, rnf = jnp.where(left_side, w2, w3), jnp.where(left_side, w3, w2)
        pivot = inverse(1.0 - rff * far)
        onward = rnn + rnf * far * rfn * pivot
        for place, value in enumerate(
            (rff, pivot, rfn * pivot, rnf, far, near, inverse(1.0 - near * onward))
        ):
            out[7 + place, rows, :] = value
        return 0

    lax.fori_loop(0, half // chunk, step, 0)


def merge_kernel(chips, keep, got, ports, whole, out):
    half = keep.shape[1]
    core = lax.rem(lax.axis_index("rad"), 2)
    left_side = lax.axis_index("rad") // 2 < chips // 2
    chunk = 32

    def step(index, _):
        rows = pl.ds(pl.multiple_of(index * chunk, chunk), chunk)
        g1, b2, g2, c1, h1, c2, mid = (ports[place, rows, :] for place in range(7))
        mine = [keep[place, rows, :] for place in range(2)]
        other = [got[place, rows, :] for place in range(2)]
        low = [jnp.where(core == 0, m, o) for m, o in zip(mine, other)]
        high = [jnp.where(core == 0, o, m) for m, o in zip(mine, other)]
        upper = (high[0] + c1 * low[1]) * mid
        first = low[0] + g1 * upper
        last = high[1] + c2 * (low[1] + g2 * upper)
        near = jnp.where(left_side, last, first)
        whole[0, rows, :] = jnp.where(left_side, first, last)
        whole[1, rows, :] = near
        out[rows, :] = near
        return 0

    lax.fori_loop(0, half // chunk, step, 0)


def inward_kernel(whole, incoming, ports, out):
    half = out.shape[0]
    chunk = 32

    def step(index, _):
        rows = pl.ds(pl.multiple_of(index * chunk, chunk), chunk)
        rff, pivot, _rfn, rnf, far = (ports[7 + place, rows, :] for place in range(5))
        value = incoming[rows, :]
        origin = (whole[0, rows, :] + rff * value) * pivot
        out[rows, :] = whole[1, rows, :] + rnf * (value + far * origin)
        return 0

    lax.fori_loop(0, half // chunk, step, 0)


def middle_kernel(chips, whole, incoming, own, other, ports, near_out, far_out):
    half = far_out.shape[0]
    chip = lax.axis_index("rad") // 2
    inner = (chip == chips // 2) | (chip == chips // 2 - 1)
    chunk = 32

    def step(index, _):
        rows = pl.ds(pl.multiple_of(index * chunk, chunk), chunk)
        rff, pivot, hold, _rnf, _far, near, close = (
            ports[7 + place, rows, :] for place in range(7)
        )
        value = (other[rows, :] + near * own[rows, :]) * close
        value = jnp.where(inner, value, 0.0)
        origin = (whole[0, rows, :] + rff * incoming[rows, :]) * pivot
        near_out[rows, :] = value
        far_out[rows, :] = origin + hold * value
        return 0

    lax.fori_loop(0, half // chunk, step, 0)


def outward_kernel(whole, incoming, near_in, ports, far_out):
    half = far_out.shape[0]
    chunk = 32

    def step(index, _):
        rows = pl.ds(pl.multiple_of(index * chunk, chunk), chunk)
        rff, pivot, hold = (ports[7 + place, rows, :] for place in range(3))
        origin = (whole[0, rows, :] + rff * incoming[rows, :]) * pivot
        far_out[rows, :] = origin + hold * near_in[rows, :]
        return 0

    lax.fori_loop(0, half // chunk, step, 0)


def parts_kernel(chips, keep, got, ports, whole, incoming, near_one, near_two, own, send):
    half = keep.shape[1]
    core = lax.rem(lax.axis_index("rad"), 2)
    left_side = lax.axis_index("rad") // 2 < chips // 2
    chunk = 32

    def step(index, _):
        rows = pl.ds(pl.multiple_of(index * chunk, chunk), chunk)
        _g1, b2, g2, c1, h1, _c2, mid = (ports[place, rows, :] for place in range(7))
        rff, pivot, hold, _rnf, far = (ports[7 + place, rows, :] for place in range(5))
        near = near_one[rows, :] + near_two[rows, :]
        value = incoming[rows, :]
        outer = value + far * ((whole[0, rows, :] + rff * value) * pivot + hold * near)
        left, right = jnp.where(left_side, outer, near), jnp.where(left_side, near, outer)
        last = jnp.where(core == 0, keep[1, rows, :], got[1, rows, :]) + b2 * left
        opening = jnp.where(core == 0, got[0, rows, :], keep[0, rows, :]) + h1 * right
        upper = (opening + c1 * last) * mid
        lower = last + g2 * upper
        own[0, rows, :] = jnp.where(core == 0, left, lower)
        own[1, rows, :] = jnp.where(core == 0, upper, right)
        send[0, rows, :] = jnp.where(core == 0, lower, left)
        send[1, rows, :] = jnp.where(core == 0, right, upper)
        return 0

    lax.fori_loop(0, half // chunk, step, 0)


def fold_rows(values):
    parts = [values[start : start + 8] for start in range(0, values.shape[0], 8)]
    while len(parts) > 1:
        parts = [a + b for a, b in zip(parts[::2], parts[1::2])]
    return parts[0]


def by_blocks(count, body, carry):
    def block(index, carry):
        for place in range(CELLS):
            carry = body(index * CELLS + place, carry)
        return carry

    return lax.fori_loop(0, lax.div(count, CELLS), block, carry)


def ratios(radial, first, lam, mu, left_store, right_store):
    total = radial.total
    shape = lam.shape

    def leftward(cell, factor):
        pivot = inverse(radial.diagonal(cell, lam, mu) - radial.previous(cell) * factor)
        factor = radial.coupling(cell) * pivot
        left_store[cell] = factor
        return factor

    def rightward(step, factor):
        cell = total - 1 - step
        pivot = inverse(radial.diagonal(cell, lam, mu) - radial.coupling(cell) * factor)
        factor = radial.previous(cell) * pivot
        right_store[cell] = factor
        return factor

    zero = jnp.zeros(shape, F32)
    left = by_blocks(first, leftward, zero)
    right = by_blocks(total - CELLS - first, rightward, zero)
    return left, right


def ratios_kernel(total, kept, lam, mu, *rest):
    radial = Radial(*rest[:4], total)
    edges, store = rest[4:]
    first = lax.axis_index("rad") * CELLS
    opening = lax.axis_index("rad") // 2 * (2 * CELLS)
    level = mu[...][:1]
    chunk = lam.shape[0] // 5

    def step(index, _):
        rows = pl.ds(pl.multiple_of(index * chunk, chunk), chunk)
        view = store.at[:, rows, :] if kept else store
        ratios(radial, first, lam[rows, :], level, view, view)
        left = view[jnp.maximum(opening - 1, 0)]
        right = view[jnp.minimum(opening + 2 * CELLS, total - 1)]
        edges[0, rows, :] = jnp.where(opening > 0, left, 0.0)
        edges[1, rows, :] = jnp.where(opening + 2 * CELLS < total, right, 0.0)
        return 0

    lax.fori_loop(0, 5, step, 0)


def outside(view, first, total):
    left = jnp.where(first > 0, view[jnp.maximum(first - 1, 0)], 0.0)
    right = view[jnp.minimum(first + CELLS, total - 1)]
    return left, jnp.where(first + CELLS < total, right, 0.0)


def stored_view(store, index, chunk):
    start = shared_row(index // 2, lax.rem(index, 2), chunk)
    return store.at[:, pl.ds(start, chunk), :]


def ends_kernel(total, kept, response, spectrum, lam, ends, mu, *rest):
    radial = Radial(*rest[:4], total)
    if kept:
        store, out, sums = rest[4:]
    else:
        out, sums, store = rest[4:]
    first = lax.axis_index("rad") * CELLS
    level = mu[...][:1]
    chunk = spectrum.shape[1] // 8
    sums[...] = jnp.zeros_like(sums)

    def step(index, _):
        kind = lax.rem(index, 2)
        rows = pl.ds(pl.multiple_of(index * chunk, chunk), chunk)
        values = lam[rows, :]
        if kept:
            view = stored_view(store, index, chunk)
            left, right = outside(view, first, total)
        else:
            view = store
            left, right = ratios(radial, first, values, level, store, store)
        weight = 2.0 * ends[rows, :]
        answer = solve_block(
            radial,
            first,
            values,
            level,
            [weight * spectrum[cell, rows, :] for cell in range(CELLS)],
            radial.previous(first) * left,
            radial.coupling(first + CELLS - 1) * right,
        )
        for place in range(CELLS):
            sums[kind, first + place] += fold_rows(answer[place])

        def outward_left(move, value):
            cell = first - 1 - move
            value = view[cell] * value
            sums[kind, cell] += fold_rows(value)
            return value

        def outward_right(move, value):
            cell = first + CELLS + move
            value = view[cell] * value
            sums[kind, cell] += fold_rows(value)
            return value

        by_blocks(first, outward_left, answer[0])
        by_blocks(total - CELLS - first, outward_right, answer[-1])
        return 0

    lax.fori_loop(0, 8, step, 0)
    for kind in range(2):
        for cell in range(total):
            out[kind, cell : cell + 1, :] = jnp.sum(sums[kind, cell], axis=0, keepdims=True)
    out[2:4] = response[...]


def join_kernel(own, other, out):
    out[0:2] = own[0:2] + other[0:2]
    out[2:4] = own[2:4]
    out[4:6] = other[2:4]


def total_kernel(*rest):
    pieces, out = rest[:-1], rest[-1]
    value = pieces[0][0:2]
    for piece in pieces[1:]:
        value = value + piece[0:2]
    out[...] = value


def response_kernel(total, lam, weight, mu, *rest):
    radial = Radial(*rest[:4], total)
    out, store, sums, lines = rest[4:]
    first = lax.axis_index("rad") * CELLS
    level = mu[pl.ds(lax.axis_index("az"), 1), :]
    group = LANES // SLABS
    chunk = lam.shape[1]
    sums[...] = jnp.zeros_like(sums)

    def step(index, _):
        kind = index
        values = lam[kind]
        left, right = ratios(radial, first, values, level, store, store)
        source = weight[kind]
        zero = jnp.zeros_like(source)
        openings, closings = [], []
        for place in range(CELLS):
            answer = solve_block(
                radial,
                first,
                values,
                level,
                [source if cell == place else zero for cell in range(CELLS)],
                radial.previous(first) * left,
                radial.coupling(first + CELLS - 1) * right,
            )
            for cell in range(CELLS):
                sums[kind, place, first + cell] += fold_rows(answer[cell])
            openings.append(answer[0])
            closings.append(answer[-1])

        def outward(cell, factor, edges):
            factor = store[cell] * factor
            for place in range(CELLS):
                sums[kind, place, cell] += fold_rows(factor * edges[place])
            return factor

        one = jnp.ones_like(source)
        by_blocks(first, lambda move, factor: outward(first - 1 - move, factor, openings), one)
        by_blocks(
            total - CELLS - first,
            lambda move, factor: outward(first + CELLS + move, factor, closings),
            one,
        )
        return 0

    lax.fori_loop(0, 2, step, 0)
    lane = lax.broadcasted_iota(jnp.int32, (1, LANES), 1) // group

    def close(cell, _):
        for kind in range(2):
            for place in range(CELLS):
                lines[kind, place, pl.ds(cell, 1), :] = jnp.sum(
                    sums[kind, place, cell], axis=0, keepdims=True
                )
        return 0

    lax.fori_loop(0, total, close, 0, unroll=8)
    for kind in range(2):
        result = jnp.zeros((total, LANES), F32)
        for place in range(CELLS):
            line = lines[kind, place]
            line = line + pltpu.roll(line, 2 * group, 1)
            line = line + pltpu.roll(line, group, 1)
            result = jnp.where(lane == place, line, result)
        out[kind] = result


def lane_groups():
    return lax.broadcasted_iota(jnp.int32, (1, LANES), 1) // (LANES // SLABS)


def to_all_groups(values, group):
    width = LANES // SLABS
    values = jnp.where(lane_groups() == group, values, 0.0)
    values = values + pltpu.roll(values, 2 * width, 1)
    return values + pltpu.roll(values, width, 1)


def fold_cells(values):
    width = values.shape[0] // SLABS
    result = values[:width]
    for group in range(1, SLABS):
        part = values[group * width : (group + 1) * width]
        result = jnp.where(lane_groups() == group, part, result)
    return result


def unfold_cells(values):
    return jnp.concatenate([to_all_groups(values, group) for group in range(SLABS)])


def invert(matrices, total):
    width = total // SLABS
    step_size = 8
    rows = lax.broadcasted_iota(jnp.int32, (width, LANES), 0)
    cells = rows + lane_groups() * width

    def step(panel, _):
        base = pl.multiple_of(panel * step_size, step_size)
        group = lax.div(base, width)
        spot_rows = pl.ds(pl.multiple_of(lax.rem(base, width), step_size), step_size)
        inside = (cells >= base) & (cells < base + step_size)
        state = []
        for matrix in matrices:
            lines = [matrix[base + place] for place in range(step_size)]
            corners = [
                to_all_groups(matrix[base + place, spot_rows, :], group)
                for place in range(step_size)
            ]
            state.append((lines, corners))
        for place in range(step_size):
            mark = cells == base + place
            spot = lax.broadcasted_iota(jnp.int32, (step_size, LANES), 0) == place
            for lines, corners in state:
                scale = inverse(corners[place][place : place + 1])
                line = jnp.where(mark, 1.0, lines[place]) * scale
                corner = jnp.where(spot, 1.0, corners[place]) * scale
                for row in range(step_size):
                    if row == place:
                        continue
                    factor = corners[row][place : place + 1]
                    lines[row] = jnp.where(mark, 0.0, lines[row]) - factor * line
                    corners[row] = jnp.where(spot, 0.0, corners[row]) - factor * corner
                lines[place], corners[place] = line, corner

        batch = 16

        def update(index, _):
            for matrix, (lines, _corners) in zip(matrices, state):
                spots = [index * batch + place for place in range(batch)]
                corners = [to_all_groups(matrix[spot, spot_rows, :], group) for spot in spots]
                values = [jnp.where(inside, 0.0, matrix[spot]) for spot in spots]
                for place in range(step_size):
                    values = [
                        value - corner[place : place + 1] * lines[place]
                        for value, corner in zip(values, corners)
                    ]
                for spot, value in zip(spots, values):
                    matrix[spot] = value
            return 0

        lax.fori_loop(0, total // batch, update, 0)
        for matrix, (lines, _corners) in zip(matrices, state):
            for place in range(step_size):
                matrix[base + place] = lines[place]
        return 0

    lax.fori_loop(0, total // step_size, step, 0)


def per_cell(total, azimuth, top):
    width = total // SLABS
    cells = lax.broadcasted_iota(jnp.int32, (width, LANES), 0) + lane_groups() * width

    def column(cell, value):
        return jnp.where(cells == cell, top / azimuth[cell], value)

    return lax.fori_loop(0, total, column, jnp.zeros((width, LANES), F32), unroll=8)


def capacity_kernel(total, chips, azimuth, *rest):
    pieces = rest[:chips]
    minus_out, alternate_out, pair_out = rest[chips:]
    chip = lax.axis_index("rad") // 2
    core = lax.rem(lax.axis_index("rad"), 2)
    width = total // SLABS
    shift = LANES // SLABS
    lane = lane_groups()
    cells = lax.broadcasted_iota(jnp.int32, (width, LANES), 0) + lane * width
    for distance, piece in enumerate(pieces):
        origin = lax.rem(chip + chips - distance, chips)
        for side in range(2):
            block = 2 * origin + lax.rem(core + side, 2)
            for kind in range(2):
                parts = [
                    piece[2 + 2 * side + kind, group * width : (group + 1) * width, :]
                    for group in range(SLABS)
                ]
                for place in range(CELLS):
                    row = jnp.zeros((width, LANES), F32)
                    for group, part in enumerate(parts):
                        turn = (group - place) % SLABS
                        part = pltpu.roll(part, turn * shift, 1) if turn else part
                        row = jnp.where(lane == group, part, row)
                    cell = block * CELLS + place
                    own = jnp.where(cells == cell, 0.5 / azimuth[cell], 0.0)
                    if kind == 0:
                        alternate_out[cell] = own + row
                        pair_out[cell] = own + row
                    else:
                        minus_out[cell] = own - row
    invert([minus_out, alternate_out], total)
    scale = per_cell(total, azimuth, 0.25)

    def add(cell, _):
        pair_out[cell] = pair_out[cell] + minus_out[cell] * scale * (1.0 / azimuth[cell])
        return 0

    lax.fori_loop(0, total, add, 0, unroll=8)
    invert([pair_out], total)


def apply_matrix(matrix, store, slots):
    total = matrix.shape[0]
    results = [[None] * 4 for _ in slots]
    for cell in range(total):
        line = matrix[cell]
        for place, slot in enumerate(slots):
            term = line * store[slot, cell : cell + 1, :]
            before = results[place][cell % 4]
            results[place][cell % 4] = term if before is None else before + term
    return [(r[0] + r[1]) + (r[2] + r[3]) for r in results]


def slabs_kernel(total, azimuth, minus_matrix, alternate_matrix, pair_matrix, *rest):
    pieces, outs = rest[:SLABS], rest[SLABS : 2 * SLABS]
    values, results, store = rest[2 * SLABS :]
    slab = lax.axis_index("az")
    width = total // SLABS
    shift = LANES // SLABS
    lane = lane_groups()
    for distance, piece in enumerate(pieces):
        values[slab ^ distance] = piece[...]

    def channels(kind):
        u = [values[place, kind] for place in range(SLABS)]
        mixed = (u[0] - u[2], u[3] - u[1], (u[0] + u[2]) - (u[1] + u[3]))
        return [to_all_groups(value, slab) for value in mixed]

    sums, differences = channels(0), channels(1)
    half = per_cell(total, azimuth, 0.5)
    for place in range(3):
        store[place] = differences[place]
    store[3] = -sums[2]
    lead_real, lead_imag, minus_alternate = apply_matrix(minus_matrix, store, (0, 1, 2))
    (plus_alternate,) = apply_matrix(alternate_matrix, store, (3,))
    store[4] = unfold_cells(-half * lead_imag - fold_cells(sums[0]))
    store[5] = unfold_cells(half * lead_real - fold_cells(sums[1]))
    plus_real, plus_imag = apply_matrix(pair_matrix, store, (4, 5))
    store[6] = unfold_cells(-half * plus_imag)
    store[7] = unfold_cells(half * plus_real)
    more_real, more_imag = apply_matrix(minus_matrix, store, (6, 7))
    found = (
        (plus_real, plus_imag, plus_alternate),
        (lead_real + more_real, lead_imag + more_imag, minus_alternate),
    )
    for kind, (real, imag, alternate) in enumerate(found):
        folded = (
            0.25 * (2.0 * real + alternate),
            0.25 * (-2.0 * imag - alternate),
            0.25 * (alternate - 2.0 * real),
            0.25 * (2.0 * imag - alternate),
        )
        for place, value in enumerate(folded):
            for group in range(SLABS):
                turn = lax.rem(slab - group + SLABS, SLABS) * shift
                rows = slice(group * width, (group + 1) * width)
                results[place, kind, rows, :] = jnp.where(
                    lane == slab, pltpu.roll(value, turn, 1), 0.0
                )
    for distance, out in enumerate(outs):
        out[...] = results[slab ^ distance]


def sides_kernel(total, kept, lam, ends, mu, *rest):
    radial = Radial(*rest[:4], total)
    pieces = rest[4 : 4 + SLABS]
    if kept:
        store, sources, out = rest[4 + SLABS :]
    else:
        sources, out, store = rest[4 + SLABS :]
    sources[...] = (pieces[0][...] + pieces[1][...]) + (pieces[2][...] + pieces[3][...])
    first = lax.axis_index("rad") * CELLS
    level = mu[...][:1]
    chunk = lam.shape[0] // 8

    def step(index, _):
        kind = lax.rem(index, 2)
        rows = pl.ds(pl.multiple_of(index * chunk, chunk), chunk)
        values = lam[rows, :]
        if kept:
            view = stored_view(store, index, chunk)
            left, right = outside(view, first, total)
        else:
            view = store
            left, right = ratios(radial, first, values, level, store, store)
        zero = jnp.zeros((chunk, LANES), F32)

        def passed(cell, value):
            return view[cell] * (sources[kind, pl.ds(cell, 1), :] + value)

        from_left = by_blocks(first, passed, zero)
        from_right = by_blocks(
            total - CELLS - first,
            lambda move, value: passed(total - 1 - move, value),
            zero,
        )
        entry, leave = radial.previous(first), radial.coupling(first + CELLS - 1)
        own = [sources[kind, pl.ds(first + place, 1), :] for place in range(CELLS)]
        own[0] = own[0] + from_left
        own[-1] = own[-1] + from_right
        answer = solve_block(radial, first, values, level, own, entry * left, leave * right)
        weight = ends[rows, :]
        out[0, rows, :] = weight * (from_left + entry * left * answer[0])
        out[1, rows, :] = weight * (from_right + leave * right * answer[-1])
        return 0

    lax.fori_loop(0, 8, step, 0)


def backward_kernel(total, spectrum, own, got, extra, sources, stages, lam, ends, mu, *rest):
    radial = Radial(*rest[:4], total)
    out, high, low, middle, wide_rows = rest[4:]
    length = spectrum.shape[1]
    quarter = length // 8
    core = lax.rem(lax.axis_index("rad"), 2)
    first = lax.axis_index("rad") * CELLS
    level = mu[...][:1]
    chunk = min(64, quarter)
    entry, leave = radial.previous(first), radial.coupling(first + CELLS - 1)

    for slot in range(4):

        def step(index, _):
            kind = index // (quarter // chunk)
            spot = pl.ds(pl.multiple_of(index * chunk, chunk), chunk)
            rows = pl.ds(pl.multiple_of(slot * 2 * quarter + index * chunk, chunk), chunk)
            near = pl.ds(pl.multiple_of(slot % 2 * 2 * quarter + index * chunk, chunk), chunk)
            mine = core == slot // 2
            side = [jnp.where(mine, own[place, near, :], got[place, near, :]) for place in range(2)]
            weight = ends[rows, :]
            right = [
                spectrum[cell, rows, :] + weight * sources[kind, pl.ds(first + cell, 1), :]
                for cell in range(CELLS)
            ]
            right[0] = right[0] + (entry * side[0] + extra[0, rows, :])
            right[-1] = right[-1] + (leave * side[1] + extra[1, rows, :])
            answer = solve_block(radial, first, lam[rows, :], level, right)
            for cell in range(CELLS):
                one, two = split(answer[cell])
                columns = slice(cell * LANES, (cell + 1) * LANES)
                high[slot, spot, columns] = one
                low[slot, spot, columns] = two
            return 0

        lax.fori_loop(0, 2 * quarter // chunk, step, 0)
        upper = stages[slot * 2 * quarter : (slot + 1) * 2 * quarter, :]
        lower = stages[(4 + slot) * 2 * quarter : (5 + slot) * 2 * quarter, :]
        middle[slot] = dot(upper, high[slot]) + dot(upper, low[slot]) + dot(lower, high[slot])
    chunk = 16
    wide = stages[8 * 2 * quarter : 8 * 2 * quarter + 2 * LANES, :]
    for cell in range(CELLS):
        columns = slice(cell * LANES, (cell + 1) * LANES)
        for start in range(0, quarter, chunk):
            y = [
                middle[place // 2, pl.ds(place % 2 * quarter + start, chunk), columns]
                for place in range(8)
            ]
            for place, value in enumerate(gather_parts(y)):
                one, two = split(value)
                row = place * quarter + start
                wide_rows[row : row + chunk, :LANES] = one
                wide_rows[row : row + chunk, LANES:] = two
        for start in range(0, length, 2 * quarter):
            both = dot(wide_rows[start : start + 2 * quarter, :], wide)
            out[pl.ds(start * CELLS + cell, 2 * quarter, stride=CELLS), :] = (
                both[:, :LANES] + both[:, LANES:]
            )


def call(kernel, out_shapes, args, scalars=(), scratch=(), cost=1, room=20, held=(), name=None):
    specs = []
    for place in range(len(args)):
        space = pltpu.SMEM if place in scalars else pltpu.HBM if place in held else pltpu.VMEM
        specs.append(pl.BlockSpec(memory_space=space))
    outs = [jax.ShapeDtypeStruct(shape, F32) for shape in out_shapes]
    return pl.pallas_call(
        kernel,
        out_shape=outs,
        in_specs=specs,
        out_specs=[pl.BlockSpec(memory_space=pltpu.VMEM)] * len(outs),
        scratch_shapes=list(scratch),
        compiler_params=pltpu.CompilerParams(vmem_limit_bytes=room * 2**20),
        cost_estimate=pl.CostEstimate(
            flops=0, bytes_accessed=int(cost * 3.69e6), transcendentals=0
        ),
        name=name,
    )(*args)


def other_core(values):
    count = lax.axis_size("rad")
    return lax.ppermute(values, "rad", [(index, index ^ 1) for index in range(count)])


def between_chips(values, pairs):
    route = [(2 * a + core, 2 * b + core) for a, b in pairs for core in range(2)]
    return lax.ppermute(values, "rad", route)


def along_chips(values, distance):
    chips = lax.axis_size("rad") // 2
    return between_chips(values, [(chip, (chip + distance) % chips) for chip in range(chips)])


def across_slabs(values, distance):
    return lax.ppermute(values, "az", [(slab, slab ^ distance) for slab in range(SLABS)])


def on_device(source, helmholtz, azimuth, vertical, radial):
    length, cells, depth = source.shape
    blocks = lax.axis_size("rad")
    chips = blocks // 2
    total = blocks * cells
    assert cells == CELLS and depth == LANES and lax.axis_size("az") == SLABS
    assert chips % 2 == 0
    half = length // 2
    quarter = length // 8
    scalars4 = (helmholtz, azimuth, vertical, radial)
    kept = total * 5 * quarter * LANES * 4 <= 12 * 2**20
    room = 20 if kept else 56

    basis = cosine_basis(depth)
    stage, eigen, end_weights, parity = slab_tables(length)

    def matrices(stages, last):
        high, low = two_halves(stages.reshape(-1, stages.shape[-1]))
        return jnp.asarray(np.concatenate([high, low, wide_basis(last)]))

    vertical_eigen = 2.0 - 2.0 * np.cos(math.pi / depth * np.arange(depth))
    levels = np.broadcast_to(vertical_eigen[None, :], (8, depth)).astype(np.float32)
    lam = jnp.asarray(spread(eigen))
    ends = jnp.asarray(spread(end_weights))
    mu = jnp.asarray(levels)
    tables = jnp.asarray(np.concatenate([spread(eigen), levels]))
    by_slot = eigen.reshape(4, 2, quarter)
    lam_shared = jnp.asarray(
        spread(np.concatenate([by_slot[0, 0], by_slot[0, 1], by_slot[1:, 0].reshape(-1)]))
    )
    group = depth // SLABS
    mu_groups = jnp.asarray(
        np.tile(vertical_eigen.reshape(SLABS, group), (1, SLABS)).astype(np.float32)
    )

    def packed(column):
        table = np.stack([column[parity > 0], column[parity < 0]]).reshape(2, quarter, SLABS)
        return jnp.asarray(np.repeat(table, group, axis=2).astype(np.float32))

    lam_groups = packed(eigen)
    weight_groups = packed(2.0 * end_weights**2)

    def smem(start):
        return tuple(range(start, start + 4))

    wide_shape = (2 * quarter, CELLS * LANES)
    stages = matrices(stage, basis)
    spectrum, keep, send = call(
        functools.partial(forward_kernel, total),
        [(CELLS, length, LANES), (2, half, LANES), (2, half, LANES)],
        (source.reshape(length * CELLS, LANES), tables, stages) + scalars4,
        (),
        [
            pltpu.VMEM((length * CELLS, LANES), F32),
            pltpu.VMEM(tables.shape, F32),
            pltpu.VMEM(stages.shape, BF16),
        ]
        + [pltpu.SMEM((total,), F32)] * 4
        + [pltpu.VMEM((length * CELLS, 2 * LANES), BF16)]
        + [pltpu.VMEM((4,) + wide_shape, BF16)] * 2
        + [pltpu.SemaphoreType.DMA((7,))],
        cost=8,
        held=tuple(range(7)),
        room=57,
        name="forward",
    )
    got = other_core(send)

    store_shape = (total, (5 if kept else 1) * quarter, LANES)
    edge_shape = (2, 5 * quarter, LANES)
    ratios_out = call(
        functools.partial(ratios_kernel, total, kept),
        [edge_shape] + ([store_shape] if kept else []),
        (lam_shared, mu) + scalars4,
        smem(2),
        [] if kept else [pltpu.VMEM(store_shape, F32)],
        cost=5,
        room=room,
        name="ratios",
    )
    edges, store = ratios_out[0], tuple(ratios_out[1:])
    scratch_store = [] if kept else [pltpu.VMEM(store_shape, F32)]

    (ports,) = call(
        functools.partial(pair_ports_kernel, total),
        [(14, half, LANES)],
        (lam, mu, edges) + scalars4,
        smem(3),
        cost=2,
        room=room,
        name="pair_ports",
    )
    line = (half, LANES)
    whole, out = call(
        functools.partial(merge_kernel, chips),
        [(2, half, LANES), line],
        (keep, got, ports),
        cost=0.3,
        room=room,
        name="merge",
    )
    out, spectrum_late, helmholtz_late = lax.optimization_barrier((out, spectrum, helmholtz))
    scalars_late = (helmholtz_late,) + scalars4[1:]
    (response,) = call(
        functools.partial(response_kernel, total),
        [(2, total, LANES)],
        (lam_groups, weight_groups, mu_groups) + scalars_late,
        smem(3),
        [
            pltpu.VMEM((total, quarter, LANES), F32),
            pltpu.VMEM((2, CELLS, total, 8, LANES), F32),
            pltpu.VMEM((2, CELLS, total, LANES), F32),
        ],
        cost=5,
        room=room,
        name="response",
    )
    (packed_ends,) = call(
        functools.partial(ends_kernel, total, kept),
        [(4, total, LANES)],
        (response, spectrum_late, lam, ends, mu) + scalars4 + store,
        smem(5),
        [pltpu.VMEM((2, total, 8, LANES), F32)] + scratch_store,
        cost=3,
        room=room,
        name="ends",
    )
    incoming = None
    (joint,) = call(
        join_kernel,
        [(6, total, LANES)],
        (packed_ends, other_core(packed_ends)),
        cost=0.3,
        room=room,
        name="join",
    )
    whole_late, joint = lax.optimization_barrier((whole, joint))
    for edge in range(chips // 2 - 1):
        moved = between_chips(out, [(edge, edge + 1), (chips - 1 - edge, chips - 2 - edge)])
        incoming = moved if incoming is None else incoming + moved
        (out,) = call(
            inward_kernel,
            [line],
            (whole_late, incoming, ports),
            cost=0.3,
            room=room,
            name="inward",
        )
    joints = [joint] + [along_chips(joint, d) for d in range(1, chips)]
    (slab_ends,) = call(
        total_kernel, [(2, total, LANES)], tuple(joints), cost=0.3, room=room, name="total"
    )
    all_ends = [slab_ends] + [across_slabs(slab_ends, d) for d in range(1, SLABS)]
    matrices3 = call(
        functools.partial(capacity_kernel, total, chips),
        [(total, total // SLABS, LANES)] * 3,
        (azimuth, *joints),
        (0,),
        cost=6,
        room=room,
        name="capacity",
    )
    low, high = chips // 2 - 1, chips // 2
    other = between_chips(out, [(low, high), (high, low)])
    whole_last, _, _ = lax.optimization_barrier((whole, matrices3[0], tuple(all_ends)))
    near, far = call(
        functools.partial(middle_kernel, chips),
        [line, line],
        (whole_last, incoming, out, other, ports),
        cost=0.3,
        room=room,
        name="middle",
    )
    passed = None
    for edge in range(chips // 2 - 2, -1, -1):
        moved = between_chips(far, [(edge + 1, edge), (chips - 2 - edge, chips - 1 - edge)])
        passed = moved if passed is None else passed + moved
        if edge > 0:
            (far,) = call(
                outward_kernel,
                [line],
                (whole, incoming, passed, ports),
                cost=0.3,
                room=room,
                name="outward",
            )
    own_sides, send_sides = call(
        functools.partial(parts_kernel, chips),
        [(2, half, LANES)] * 2,
        (keep, got, ports, whole, incoming, near, passed),
        cost=0.4,
        room=room,
        name="parts",
    )
    got_sides = other_core(send_sides)
    end_sources = call(
        functools.partial(slabs_kernel, total),
        [(2, total, LANES)] * SLABS,
        (azimuth, *matrices3, *all_ends),
        (0,),
        [pltpu.VMEM((SLABS, 2, total, LANES), F32)] * 2 + [pltpu.VMEM((8, total, LANES), F32)],
        cost=2,
        room=room,
        name="slabs",
    )
    sources = [end_sources[0]] + [across_slabs(end_sources[d], d) for d in range(1, SLABS)]
    all_sources, extra = call(
        functools.partial(sides_kernel, total, kept),
        [(2, total, LANES), (2, length, LANES)],
        (lam, ends, mu) + scalars4 + tuple(sources) + store,
        smem(3),
        scratch_store,
        cost=3,
        room=room,
        name="sides",
    )
    (pressure,) = call(
        functools.partial(backward_kernel, total),
        [(length * CELLS, LANES)],
        (
            spectrum,
            own_sides,
            got_sides,
            extra,
            all_sources,
            matrices(np.swapaxes(stage, 1, 2), basis.T),
            lam,
            ends,
            mu,
        )
        + scalars4,
        smem(9),
        [pltpu.VMEM((4,) + wide_shape, BF16)] * 2
        + [pltpu.VMEM((4,) + wide_shape, F32), pltpu.VMEM((length, 2 * LANES), BF16)],
        cost=7,
        room=room,
        name="backward",
    )
    return pressure.reshape(length, CELLS, LANES)


def solution(mesh):
    in_specs = (P("az", "rad", None), P(), P(), P(), P())
    return jax.shard_map(
        on_device,
        mesh=mesh,
        in_specs=in_specs,
        out_specs=P("az", "rad", None),
        check_vma=False,
    )
```

```python
import functools
import math

import jax
import jax.numpy as jnp
import ml_dtypes
import numpy as np
from jax import lax
from jax.experimental import pallas as pl
from jax.experimental.pallas import tpu as pltpu
from jax.sharding import PartitionSpec as P

F32 = jnp.float32
BF16 = jnp.bfloat16
CELLS = 4
SLABS = 4
LANES = 128


def two_halves(table):
    high = table.astype(np.float32).astype(ml_dtypes.bfloat16)
    low = (table - high.astype(np.float64)).astype(np.float32).astype(ml_dtypes.bfloat16)
    return high, low


def cosine_basis(depth):
    rows = np.arange(depth)
    phases = (2 * rows[:, None] + 1) * rows[None, :] % (4 * depth)
    scales = np.where(rows == 0, math.sqrt(1.0 / depth), math.sqrt(2.0 / depth))
    return np.cos(math.pi / (2 * depth) * phases) * scales[None, :]


def wide_basis(basis):
    high, low = two_halves(basis)
    top = np.concatenate([high, low], axis=1)
    bottom = np.concatenate([high, np.zeros_like(high)], axis=1)
    return np.concatenate([top, bottom], axis=0)


def slab_tables(length):
    quarter = length // 8
    half = quarter // 2
    offsets = np.arange(quarter) + 0.5
    stage = np.zeros((4, 2 * quarter, 2 * quarter))
    modes = np.zeros((4, 2 * quarter), np.int64)

    def angle(mode):
        return 2 * np.pi * (mode[:, None] * offsets[None, :] % length) / length

    def scale(mode):
        single = (mode == 0) | (mode == length // 2)
        return np.where(single, np.sqrt(1 / length), np.sqrt(2 / length))[:, None]

    steps = np.arange(half)
    for first, mode, column, wave in (
        (0, 8 * steps, 0, np.cos),
        (half, 8 * steps + 4, quarter, np.cos),
        (quarter, 8 * (steps + 1), 0, np.sin),
        (quarter + half, 8 * steps + 4, quarter, np.sin),
    ):
        stage[0, first : first + half, column : column + quarter] = scale(mode) * wave(angle(mode))
        modes[0, first : first + half] = mode
    for slot in (1, 2, 3):
        mode = slot + 8 * np.arange(quarter)
        cosine, sine = scale(mode) * np.cos(angle(mode)), scale(mode) * np.sin(angle(mode))
        stage[slot] = np.block([[cosine, sine], [sine, -cosine]])
        modes[slot] = np.concatenate([mode, mode])
    modes = modes.reshape(-1)
    parity = np.tile(np.repeat([1, -1], quarter), 4)
    single = (modes == 0) | (modes == length // 2)
    size = np.where(single, np.sqrt(1 / length), np.sqrt(2 / length))
    ends = size * np.where(parity > 0, np.cos(np.pi * modes / length), np.sin(np.pi * modes / length))
    eigen = 2.0 - 2.0 * np.cos(2 * np.pi * modes / length)
    return stage, eigen, ends, parity


def spread(column):
    return np.broadcast_to(column[..., None], column.shape + (LANES,)).astype(np.float32)


def split(values):
    high = values.astype(BF16)
    low = (values - high.astype(F32)).astype(BF16)
    return high, low


def dot(left, right):
    return jnp.dot(left, right, preferred_element_type=F32)


def times_basis(values, wide):
    high, low = split(values)
    both = dot(jnp.concatenate([high, low], axis=1), wide)
    depth = values.shape[1]
    return both[:, :depth] + both[:, depth:]


class Radial:
    def __init__(self, helmholtz, azimuth, vertical, radial, total):
        self.refs = (helmholtz, azimuth, vertical, radial)
        self.total = total

    def coupling(self, cell):
        cell = jnp.asarray(cell, jnp.int32)
        return jnp.where(cell < self.total - 1, self.refs[3][cell], 0.0)

    def previous(self, cell):
        cell = jnp.asarray(cell, jnp.int32)
        return jnp.where(cell > 0, self.refs[3][jnp.maximum(cell - 1, 0)], 0.0)

    def diagonal(self, cell, lam, mu):
        base = self.refs[0][cell] + self.coupling(cell) + self.previous(cell)
        return lam * self.refs[1][cell] + (mu * self.refs[2][cell] + base)


def inverse(values):
    return pl.reciprocal(values, approx=False)


def solve_block(radial, first, lam, mu, right, add_first=None, add_last=None):
    rows = []
    factor = values = None
    for place in range(CELLS):
        cell = first + place
        diagonal = radial.diagonal(cell, lam, mu)
        if place == 0 and add_first is not None:
            diagonal = diagonal - add_first
        if place == CELLS - 1 and add_last is not None:
            diagonal = diagonal - add_last
        if place > 0:
            before = radial.previous(cell)
            pivot = inverse(diagonal - before * factor)
            values = (right[place] + before * values) * pivot
        else:
            pivot = inverse(diagonal)
            values = right[place] * pivot
        factor = radial.coupling(cell) * pivot
        rows.append((values, factor))
    answer = [rows[-1][0]]
    for values, factor in rows[-2::-1]:
        answer.insert(0, values + factor * answer[0])
    return answer


def block_ports(radial, first, lam, mu):
    diagonals = [radial.diagonal(first + place, lam, mu) for place in range(CELLS)]
    pivot = inverse(diagonals[0])
    forward = [pivot]
    for place in range(1, CELLS):
        before = radial.previous(first + place)
        pivot = inverse(diagonals[place] - before * before * pivot)
        forward.append(pivot)
    last = forward[-1]
    cross = last
    for place in range(CELLS - 2, -1, -1):
        cross = radial.coupling(first + place) * forward[place] * cross
    backward = inverse(diagonals[-1])
    for place in range(CELLS - 2, -1, -1):
        after = radial.coupling(first + place)
        backward = inverse(diagonals[place] - after * after * backward)
    entry, leave = radial.previous(first), radial.coupling(first + CELLS - 1)
    return backward * entry, cross * leave, cross * entry, last * leave


def chip_ports(radial, first, lam, mu):
    b1, g1, b2, g2 = block_ports(radial, first, lam, mu)
    c1, h1, c2, h2 = block_ports(radial, first + CELLS, lam, mu)
    mid = inverse(1.0 - g2 * c1)
    low = c1 * b2 * mid
    high = h1 * mid
    whole = (
        b1 + g1 * low,
        g1 * high,
        c2 * (b2 + g2 * low),
        h2 + c2 * g2 * high,
    )
    return (b1, g1, b2, g2), (c1, h1, c2, h2), mid, whole


def spread_parts(x):
    root = math.sqrt(0.5)
    s = [x[n] + x[n + 4] for n in range(4)]
    d = [x[n] - x[n + 4] for n in range(4)]
    even, odd = s[0] + s[2], s[1] + s[3]
    minus, plus = root * (d[1] - d[3]), root * (d[1] + d[3])
    return (
        even + odd,
        even - odd,
        d[0] + minus,
        -plus - d[2],
        s[0] - s[2],
        s[3] - s[1],
        d[0] - minus,
        d[2] - plus,
    )


def gather_parts(y):
    root = math.sqrt(0.5)
    plus, minus = y[0] + y[1], y[0] - y[1]
    s = (plus + y[4], minus - y[5], plus - y[4], minus + y[5])
    real, imag = root * (y[2] - y[6]), root * (y[3] + y[7])
    d = (y[2] + y[6], real - imag, y[7] - y[3], -real - imag)
    return [s[n] + d[n] for n in range(4)] + [s[n] - d[n] for n in range(4)]


def forward_kernel(total, source_in, tables_in, stages_in, *rest):
    scalars_in = rest[:4]
    spectrum_out, keep, send = rest[4:7]
    source, tables, stages, s0, s1, s2, s3, wide_rows, high, low, spectrum, sems = rest[7:]
    scalars = (s0, s1, s2, s3)
    length = source.shape[0] * source.shape[1] // CELLS
    quarter = length // 8
    eighth = quarter * CELLS
    pairs = []
    for part in range(2):
        rows = pl.ds(part * eighth // 2, eighth // 2)
        pairs.append((source_in.at[:, rows, :], source.at[:, rows, :]))
    pairs += [(stages_in, stages), (tables_in, tables)]
    pairs += list(zip(scalars_in, scalars))
    copies = [
        pltpu.make_async_copy(origin, target, sems.at[place])
        for place, (origin, target) in enumerate(pairs)
    ]
    for copy in copies:
        copy.start()
    radial = Radial(*scalars, total)
    core = lax.rem(lax.axis_index("rad"), 2)
    first = lax.axis_index("rad") * CELLS
    chunk = 16
    for start in range(0, quarter, chunk):
        if start * 2 % quarter == 0:
            copies[start * 2 // quarter].wait()
        for cell in range(CELLS):
            x = [
                source[n, pl.ds(start * CELLS + cell, chunk, stride=CELLS), :] for n in range(8)
            ]
            for place, part in enumerate(spread_parts(x)):
                one, two = split(part)
                row = cell * length + place * quarter + start
                wide_rows[row : row + chunk, :LANES] = one
                wide_rows[row : row + chunk, LANES:] = two
    copies[2].wait()
    wide = stages[8 * 2 * quarter : 8 * 2 * quarter + 2 * LANES, :]
    for cell in range(CELLS):
        for slot in range(4):
            row = cell * length + slot * 2 * quarter
            both = dot(wide_rows[row : row + 2 * quarter, :], wide)
            one, two = split(both[:, :LANES] + both[:, LANES:])
            columns = slice(cell * LANES, (cell + 1) * LANES)
            high[slot, :, columns] = one
            low[slot, :, columns] = two
    leaving = []
    for slot in range(4):
        upper = stages[slot * 2 * quarter : (slot + 1) * 2 * quarter, :]
        lower = stages[(4 + slot) * 2 * quarter : (5 + slot) * 2 * quarter, :]
        result = dot(upper, high[slot]) + dot(upper, low[slot]) + dot(lower, high[slot])
        for cell in range(CELLS):
            spectrum[cell, slot * 2 * quarter : (slot + 1) * 2 * quarter, :] = result[
                :, cell * LANES : (cell + 1) * LANES
            ]
        rows = pl.ds(slot * 2 * quarter, 2 * quarter)
        leaving.append(
            pltpu.make_async_copy(
                spectrum.at[:, rows, :], spectrum_out.at[:, rows, :], sems.at[8 + slot]
            )
        )
        leaving[-1].start()
    for copy in copies[3:]:
        copy.wait()
    chunk = 64
    half = length // 2
    level = tables[length : length + 1, :]

    def step(index, _):
        ends = []
        for part in range(2):
            rows = pl.ds(pl.multiple_of(part * half + index * chunk, chunk), chunk)
            right = [spectrum[cell, rows, :] for cell in range(CELLS)]
            answer = solve_block(radial, first, tables[rows, :], level, right)
            ends.append((answer[0], answer[-1]))
        rows = pl.ds(pl.multiple_of(index * chunk, chunk), chunk)
        for place in range(2):
            keep[place, rows, :] = jnp.where(core == 0, ends[0][place], ends[1][place])
            send[place, rows, :] = jnp.where(core == 0, ends[1][place], ends[0][place])
        return 0

    lax.fori_loop(0, half // chunk, step, 0)
    for copy in leaving:
        copy.wait()


def shared_row(slot, kind, quarter):
    return pl.multiple_of(jnp.where(slot == 0, kind, slot + 1) * quarter, quarter)


def pair_ports_kernel(total, lam, mu, *rest):
    radial = Radial(*rest[:4], total)
    (out,) = rest[4:]
    half = out.shape[1]
    quarter = half // 4
    chips = total // (2 * CELLS)
    core = lax.rem(lax.axis_index("rad"), 2)
    chip = lax.axis_index("rad") // 2
    left_side = chip < chips // 2
    first = chip * (2 * CELLS)
    level = mu[...][:1]
    chunk = min(64, quarter)

    def step(index, _):
        rows = pl.ds(pl.multiple_of(index * chunk, chunk), chunk)
        spot = pl.ds(pl.multiple_of(core * half + index * chunk, chunk), chunk)
        (b1, g1, b2, g2), (c1, h1, c2, h2), mid, (w1, w2, w3, w4) = chip_ports(
            radial, first, lam[spot, :], level
        )
        rff, rnn = jnp.where(left_side, w1, w4), jnp.where(left_side, w4, w1)
        rfn, rnf = jnp.where(left_side, w2, w3), jnp.where(left_side, w3, w2)
        for place, value in enumerate((g1, b2, g2, c1, h1, c2, mid, rff, rfn, rnf, rnn)):
            out[place, rows, :] = value
        return 0

    lax.fori_loop(0, half // chunk, step, 0)


def chain_links_kernel(chips, ports, edges, out):
    half = out.shape[1]
    quarter = half // 4
    core = lax.rem(lax.axis_index("rad"), 2)
    left_side = lax.axis_index("rad") // 2 < chips // 2
    chunk = min(64, quarter)

    def step(index, _):
        rows = pl.ds(pl.multiple_of(index * chunk, chunk), chunk)
        block = index * chunk // quarter
        start = shared_row(core * 2 + block // 2, lax.rem(block, 2), quarter)
        spot = pl.ds(pl.multiple_of(start + lax.rem(index * chunk, quarter), chunk), chunk)
        rff, rfn, rnf, rnn = (ports[7 + place, rows, :] for place in range(4))
        left, right = edges[0, spot, :], edges[1, spot, :]
        far, near = jnp.where(left_side, left, right), jnp.where(left_side, right, left)
        pivot = inverse(1.0 - rff * far)
        onward = rnn + rnf * far * rfn * pivot
        for place, value in enumerate(
            (rff, pivot, rfn * pivot, rnf, far, near, inverse(1.0 - near * onward))
        ):
            out[place, rows, :] = value
        return 0

    lax.fori_loop(0, half // chunk, step, 0)


def merge_kernel(chips, keep, got, ports, whole, out):
    half = keep.shape[1]
    core = lax.rem(lax.axis_index("rad"), 2)
    left_side = lax.axis_index("rad") // 2 < chips // 2
    chunk = 32

    def step(index, _):
        rows = pl.ds(pl.multiple_of(index * chunk, chunk), chunk)
        g1, b2, g2, c1, h1, c2, mid = (ports[place, rows, :] for place in range(7))
        mine = [keep[place, rows, :] for place in range(2)]
        other = [got[place, rows, :] for place in range(2)]
        low = [jnp.where(core == 0, m, o) for m, o in zip(mine, other)]
        high = [jnp.where(core == 0, o, m) for m, o in zip(mine, other)]
        upper = (high[0] + c1 * low[1]) * mid
        first = low[0] + g1 * upper
        last = high[1] + c2 * (low[1] + g2 * upper)
        near = jnp.where(left_side, last, first)
        whole[0, rows, :] = jnp.where(left_side, first, last)
        whole[1, rows, :] = near
        out[rows, :] = near
        return 0

    lax.fori_loop(0, half // chunk, step, 0)


def inward_kernel(whole, incoming, links, out):
    half = out.shape[0]
    chunk = 32

    def step(index, _):
        rows = pl.ds(pl.multiple_of(index * chunk, chunk), chunk)
        rff, pivot, _rfn, rnf, far = (links[place, rows, :] for place in range(5))
        value = incoming[rows, :]
        origin = (whole[0, rows, :] + rff * value) * pivot
        out[rows, :] = whole[1, rows, :] + rnf * (value + far * origin)
        return 0

    lax.fori_loop(0, half // chunk, step, 0)


def middle_kernel(chips, whole, incoming, own, other, links, near_out, far_out):
    half = far_out.shape[0]
    chip = lax.axis_index("rad") // 2
    inner = (chip == chips // 2) | (chip == chips // 2 - 1)
    chunk = 32

    def step(index, _):
        rows = pl.ds(pl.multiple_of(index * chunk, chunk), chunk)
        rff, pivot, hold, _rnf, _far, near, close = (
            links[place, rows, :] for place in range(7)
        )
        value = (other[rows, :] + near * own[rows, :]) * close
        value = jnp.where(inner, value, 0.0)
        origin = (whole[0, rows, :] + rff * incoming[rows, :]) * pivot
        near_out[rows, :] = value
        far_out[rows, :] = origin + hold * value
        return 0

    lax.fori_loop(0, half // chunk, step, 0)


def outward_kernel(whole, incoming, near_in, links, far_out):
    half = far_out.shape[0]
    chunk = 32

    def step(index, _):
        rows = pl.ds(pl.multiple_of(index * chunk, chunk), chunk)
        rff, pivot, hold = (links[place, rows, :] for place in range(3))
        origin = (whole[0, rows, :] + rff * incoming[rows, :]) * pivot
        far_out[rows, :] = origin + hold * near_in[rows, :]
        return 0

    lax.fori_loop(0, half // chunk, step, 0)


def parts_kernel(chips, keep, got, ports, links, whole, incoming, near_one, near_two, own, send):
    half = keep.shape[1]
    core = lax.rem(lax.axis_index("rad"), 2)
    left_side = lax.axis_index("rad") // 2 < chips // 2
    chunk = 32

    def step(index, _):
        rows = pl.ds(pl.multiple_of(index * chunk, chunk), chunk)
        _g1, b2, g2, c1, h1, _c2, mid = (ports[place, rows, :] for place in range(7))
        rff, pivot, hold, _rnf, far = (links[place, rows, :] for place in range(5))
        near = near_one[rows, :] + near_two[rows, :]
        value = incoming[rows, :]
        outer = value + far * ((whole[0, rows, :] + rff * value) * pivot + hold * near)
        left, right = jnp.where(left_side, outer, near), jnp.where(left_side, near, outer)
        last = jnp.where(core == 0, keep[1, rows, :], got[1, rows, :]) + b2 * left
        opening = jnp.where(core == 0, got[0, rows, :], keep[0, rows, :]) + h1 * right
        upper = (opening + c1 * last) * mid
        lower = last + g2 * upper
        own[0, rows, :] = jnp.where(core == 0, left, lower)
        own[1, rows, :] = jnp.where(core == 0, upper, right)
        send[0, rows, :] = jnp.where(core == 0, lower, left)
        send[1, rows, :] = jnp.where(core == 0, right, upper)
        return 0

    lax.fori_loop(0, half // chunk, step, 0)


def fold_rows(values):
    parts = [values[start : start + 8] for start in range(0, values.shape[0], 8)]
    while len(parts) > 1:
        parts = [a + b for a, b in zip(parts[::2], parts[1::2])]
    return parts[0]


def by_blocks(count, body, carry):
    def block(index, carry):
        for place in range(CELLS):
            carry = body(index * CELLS + place, carry)
        return carry

    return lax.fori_loop(0, lax.div(count, CELLS), block, carry)


def ratios(radial, first, lam, mu, left_store, right_store):
    total = radial.total
    shape = lam.shape

    def leftward(cell, factor):
        pivot = inverse(radial.diagonal(cell, lam, mu) - radial.previous(cell) * factor)
        factor = radial.coupling(cell) * pivot
        left_store[cell] = factor
        return factor

    def rightward(step, factor):
        cell = total - 1 - step
        pivot = inverse(radial.diagonal(cell, lam, mu) - radial.coupling(cell) * factor)
        factor = radial.previous(cell) * pivot
        right_store[cell] = factor
        return factor

    zero = jnp.zeros(shape, F32)
    left = by_blocks(first, leftward, zero)
    right = by_blocks(total - CELLS - first, rightward, zero)
    return left, right


def ratios_kernel(total, kept, lam, mu, *rest):
    radial = Radial(*rest[:4], total)
    edges, store = rest[4:]
    first = lax.axis_index("rad") * CELLS
    opening = lax.axis_index("rad") // 2 * (2 * CELLS)
    level = mu[...][:1]
    chunk = lam.shape[0] // (2 if kept else 5)

    def step(index, _):
        rows = pl.ds(pl.multiple_of(index * chunk, chunk), chunk)
        view = store.at[:, rows, :] if kept else store
        ratios(radial, first, lam[rows, :], level, view, view)
        left = view[jnp.maximum(opening - 1, 0)]
        right = view[jnp.minimum(opening + 2 * CELLS, total - 1)]
        edges[0, rows, :] = jnp.where(opening > 0, left, 0.0)
        edges[1, rows, :] = jnp.where(opening + 2 * CELLS < total, right, 0.0)
        return 0

    lax.fori_loop(0, lam.shape[0] // chunk, step, 0)


def outside(view, first, total):
    left = jnp.where(first > 0, view[jnp.maximum(first - 1, 0)], 0.0)
    right = view[jnp.minimum(first + CELLS, total - 1)]
    return left, jnp.where(first + CELLS < total, right, 0.0)


def stored_view(store, index, chunk):
    start = shared_row(index // 2, lax.rem(index, 2), chunk)
    return store.at[:, pl.ds(start, chunk), :]


def ends_kernel(total, kept, response, spectrum, lam, ends, mu, *rest):
    radial = Radial(*rest[:4], total)
    if kept:
        store, out, sums = rest[4:]
    else:
        out, sums, store = rest[4:]
    first = lax.axis_index("rad") * CELLS
    level = mu[...][:1]
    chunk = spectrum.shape[1] // 8
    sums[...] = jnp.zeros_like(sums)

    def step(index, _):
        kind = lax.rem(index, 2)
        rows = pl.ds(pl.multiple_of(index * chunk, chunk), chunk)
        values = lam[rows, :]
        if kept:
            view = stored_view(store, index, chunk)
            left, right = outside(view, first, total)
        else:
            view = store
            left, right = ratios(radial, first, values, level, store, store)
        weight = 2.0 * ends[rows, :]
        answer = solve_block(
            radial,
            first,
            values,
            level,
            [weight * spectrum[cell, rows, :] for cell in range(CELLS)],
            radial.previous(first) * left,
            radial.coupling(first + CELLS - 1) * right,
        )
        for place in range(CELLS):
            sums[kind, first + place] += fold_rows(answer[place])

        def outward_left(move, value):
            cell = first - 1 - move
            value = view[cell] * value
            sums[kind, cell] += fold_rows(value)
            return value

        def outward_right(move, value):
            cell = first + CELLS + move
            value = view[cell] * value
            sums[kind, cell] += fold_rows(value)
            return value

        by_blocks(first, outward_left, answer[0])
        by_blocks(total - CELLS - first, outward_right, answer[-1])
        return 0

    lax.fori_loop(0, 8, step, 0)
    for kind in range(2):
        for cell in range(total):
            out[kind, cell : cell + 1, :] = jnp.sum(sums[kind, cell], axis=0, keepdims=True)
    out[2:4] = response[...]


def join_kernel(axis, bit, common, own, other, out):
    high = lax.rem(lax.div(lax.axis_index(axis), 1 << bit), 2)
    count = own.shape[0] - common
    if common:
        out[0:common] = own[0:common] + other[0:common]
    out[pl.ds(common + high * count, count)] = own[common:]
    out[pl.ds(common + (1 - high) * count, count)] = other[common:]


def halve_kernel(axis, bit, own, other, keep, send):
    high = lax.rem(lax.div(lax.axis_index(axis), 1 << bit), 2)
    count = keep.shape[0]
    keep[...] = own[pl.ds(high * count, count)] + other[pl.ds(high * count, count)]
    there = pl.ds((1 - high) * count, count)
    send[...] = own[there] + other[there]


def response_kernel(total, lam, weight, mu, *rest):
    radial = Radial(*rest[:4], total)
    out, store, sums, lines = rest[4:]
    first = lax.axis_index("rad") * CELLS
    level = mu[pl.ds(lax.axis_index("az"), 1), :]
    group = LANES // SLABS
    chunk = lam.shape[0] // 2
    sums[...] = jnp.zeros_like(sums)
    lefts, rights = ratios(radial, first, lam[...], level, store, store)

    for kind in range(2):
        rows = slice(kind * chunk, (kind + 1) * chunk)
        source = weight[rows, :]
        zero = jnp.zeros_like(source)
        openings, closings = [], []
        for place in range(CELLS):
            answer = solve_block(
                radial,
                first,
                lam[rows, :],
                level,
                [source if cell == place else zero for cell in range(CELLS)],
                radial.previous(first) * lefts[rows],
                radial.coupling(first + CELLS - 1) * rights[rows],
            )
            for cell in range(CELLS):
                sums[kind, place, first + cell] += fold_rows(answer[cell])
            openings.append(answer[0])
            closings.append(answer[-1])

        def outward(cell, factor, edges):
            factor = store[cell, rows, :] * factor
            for place in range(CELLS):
                sums[kind, place, cell] += fold_rows(factor * edges[place])
            return factor

        one = jnp.ones_like(source)
        by_blocks(first, lambda move, factor: outward(first - 1 - move, factor, openings), one)
        by_blocks(
            total - CELLS - first,
            lambda move, factor: outward(first + CELLS + move, factor, closings),
            one,
        )

    lane = lax.broadcasted_iota(jnp.int32, (1, LANES), 1) // group

    def close(cell, _):
        for kind in range(2):
            for place in range(CELLS):
                lines[kind, place, pl.ds(cell, 1), :] = jnp.sum(
                    sums[kind, place, cell], axis=0, keepdims=True
                )
        return 0

    lax.fori_loop(0, total, close, 0, unroll=8)
    for kind in range(2):
        result = jnp.zeros((total, LANES), F32)
        for place in range(CELLS):
            line = lines[kind, place]
            line = line + pltpu.roll(line, 2 * group, 1)
            line = line + pltpu.roll(line, group, 1)
            result = jnp.where(lane == place, line, result)
        out[kind] = result


def lane_groups():
    return lax.broadcasted_iota(jnp.int32, (1, LANES), 1) // (LANES // SLABS)


def to_all_groups(values, group):
    width = LANES // SLABS
    values = jnp.where(lane_groups() == group, values, 0.0)
    values = values + pltpu.roll(values, 2 * width, 1)
    return values + pltpu.roll(values, width, 1)


def fold_cells(values):
    width = values.shape[0] // SLABS
    result = values[:width]
    for group in range(1, SLABS):
        part = values[group * width : (group + 1) * width]
        result = jnp.where(lane_groups() == group, part, result)
    return result


def unfold_cells(values):
    return jnp.concatenate([to_all_groups(values, group) for group in range(SLABS)])


def invert(matrices, total):
    width = total // SLABS
    step_size = 8
    rows = lax.broadcasted_iota(jnp.int32, (width, LANES), 0)
    cells = rows + lane_groups() * width

    def step(panel, _):
        base = pl.multiple_of(panel * step_size, step_size)
        group = lax.div(base, width)
        spot_rows = pl.ds(pl.multiple_of(lax.rem(base, width), step_size), step_size)
        inside = (cells >= base) & (cells < base + step_size)
        state = []
        for matrix in matrices:
            lines = [matrix[base + place] for place in range(step_size)]
            corners = [
                to_all_groups(matrix[base + place, spot_rows, :], group)
                for place in range(step_size)
            ]
            state.append((lines, corners))
        for place in range(step_size):
            mark = cells == base + place
            spot = lax.broadcasted_iota(jnp.int32, (step_size, LANES), 0) == place
            for lines, corners in state:
                scale = inverse(corners[place][place : place + 1])
                line = jnp.where(mark, 1.0, lines[place]) * scale
                corner = jnp.where(spot, 1.0, corners[place]) * scale
                for row in range(step_size):
                    if row == place:
                        continue
                    factor = corners[row][place : place + 1]
                    lines[row] = jnp.where(mark, 0.0, lines[row]) - factor * line
                    corners[row] = jnp.where(spot, 0.0, corners[row]) - factor * corner
                lines[place], corners[place] = line, corner

        batch = 16

        def update(index, _):
            for matrix, (lines, _corners) in zip(matrices, state):
                spots = [index * batch + place for place in range(batch)]
                corners = [to_all_groups(matrix[spot, spot_rows, :], group) for spot in spots]
                values = [jnp.where(inside, 0.0, matrix[spot]) for spot in spots]
                for place in range(step_size):
                    values = [
                        value - corner[place : place + 1] * lines[place]
                        for value, corner in zip(values, corners)
                    ]
                for spot, value in zip(spots, values):
                    matrix[spot] = value
            return 0

        lax.fori_loop(0, total // batch, update, 0)
        for matrix, (lines, _corners) in zip(matrices, state):
            for place in range(step_size):
                matrix[base + place] = lines[place]
        return 0

    lax.fori_loop(0, total // step_size, step, 0)


def per_cell(total, azimuth, top):
    width = total // SLABS
    cells = lax.broadcasted_iota(jnp.int32, (width, LANES), 0) + lane_groups() * width

    def column(cell, value):
        return jnp.where(cells == cell, azimuth[cell], value)

    return top * inverse(lax.fori_loop(0, total, column, jnp.ones((width, LANES), F32), unroll=8))


def capacity_kernel(total, azimuth, responses, *outs):
    minus_out, alternate_out, pair_out = outs
    chips = total // (2 * CELLS)
    width = total // SLABS
    shift = LANES // SLABS
    lane = lane_groups()
    cells = lax.broadcasted_iota(jnp.int32, (width, LANES), 0) + lane * width
    half = per_cell(total, azimuth, 0.5)
    for block in range(2 * chips):
        start = 2 + 2 * (block % 2 * chips + block // 2)
        for kind in range(2):
            parts = [
                responses[start + kind, group * width : (group + 1) * width, :]
                for group in range(SLABS)
            ]
            for place in range(CELLS):
                row = jnp.zeros((width, LANES), F32)
                for group, part in enumerate(parts):
                    turn = (group - place) % SLABS
                    part = pltpu.roll(part, turn * shift, 1) if turn else part
                    row = jnp.where(lane == group, part, row)
                cell = block * CELLS + place
                own = jnp.where(cells == cell, half, 0.0)
                if kind == 0:
                    alternate_out[cell] = own + row
                    pair_out[cell] = own + row
                else:
                    minus_out[cell] = own - row
    invert([minus_out, alternate_out], total)


def pair_kernel(total, azimuth, minus_matrix, plus_matrix, pair_out):
    scale = per_cell(total, azimuth, 0.25)

    def add(cell, _):
        own = inverse(jnp.full((1, LANES), azimuth[cell], F32))
        pair_out[cell] = plus_matrix[cell] + minus_matrix[cell] * (scale * own)
        return 0

    lax.fori_loop(0, total, add, 0, unroll=8)
    invert([pair_out], total)


def apply_matrix(matrix, store, slots):
    total = matrix.shape[0]
    results = [[None] * 4 for _ in slots]
    for cell in range(total):
        line = matrix[cell]
        for place, slot in enumerate(slots):
            term = line * store[slot, cell : cell + 1, :]
            before = results[place][cell % 4]
            results[place][cell % 4] = term if before is None else before + term
    return [(r[0] + r[1]) + (r[2] + r[3]) for r in results]


def slabs_kernel(total, azimuth, minus_matrix, alternate_matrix, pair_matrix, *rest):
    values, keep, send, results, store = rest
    slab = lax.axis_index("az")
    width = total // SLABS
    shift = LANES // SLABS
    lane = lane_groups()

    def channels(kind):
        u = [values[2 * place + kind] for place in range(SLABS)]
        mixed = (u[0] - u[2], u[3] - u[1], (u[0] + u[2]) - (u[1] + u[3]))
        return [to_all_groups(value, slab) for value in mixed]

    sums, differences = channels(0), channels(1)
    half = per_cell(total, azimuth, 0.5)
    for place in range(3):
        store[place] = differences[place]
    store[3] = -sums[2]
    lead_real, lead_imag, minus_alternate = apply_matrix(minus_matrix, store, (0, 1, 2))
    (plus_alternate,) = apply_matrix(alternate_matrix, store, (3,))
    store[4] = unfold_cells(-half * lead_imag - fold_cells(sums[0]))
    store[5] = unfold_cells(half * lead_real - fold_cells(sums[1]))
    plus_real, plus_imag = apply_matrix(pair_matrix, store, (4, 5))
    store[6] = unfold_cells(-half * plus_imag)
    store[7] = unfold_cells(half * plus_real)
    more_real, more_imag = apply_matrix(minus_matrix, store, (6, 7))
    found = (
        (plus_real, plus_imag, plus_alternate),
        (lead_real + more_real, lead_imag + more_imag, minus_alternate),
    )
    for kind, (real, imag, alternate) in enumerate(found):
        folded = (
            0.25 * (2.0 * real + alternate),
            0.25 * (-2.0 * imag - alternate),
            0.25 * (alternate - 2.0 * real),
            0.25 * (2.0 * imag - alternate),
        )
        for place, value in enumerate(folded):
            for group in range(SLABS):
                turn = lax.rem(slab - group + SLABS, SLABS) * shift
                rows = slice(group * width, (group + 1) * width)
                results[2 * place + kind, rows, :] = jnp.where(
                    lane == slab, pltpu.roll(value, turn, 1), 0.0
                )
    high = lax.div(slab, SLABS // 2)
    keep[...] = results[pl.ds(high * SLABS, SLABS)]
    send[...] = results[pl.ds((1 - high) * SLABS, SLABS)]


def sides_kernel(total, kept, lam, ends, mu, *rest):
    radial = Radial(*rest[:4], total)
    own_part, other_part = rest[4:6]
    if kept:
        store, sources, out = rest[6:]
    else:
        sources, out, store = rest[6:]
    sources[...] = own_part[...] + other_part[...]
    first = lax.axis_index("rad") * CELLS
    level = mu[...][:1]
    chunk = lam.shape[0] // 8

    def step(index, _):
        kind = lax.rem(index, 2)
        rows = pl.ds(pl.multiple_of(index * chunk, chunk), chunk)
        values = lam[rows, :]
        if kept:
            view = stored_view(store, index, chunk)
            left, right = outside(view, first, total)
        else:
            view = store
            left, right = ratios(radial, first, values, level, store, store)
        zero = jnp.zeros((chunk, LANES), F32)

        def passed(cell, value):
            return view[cell] * (sources[kind, pl.ds(cell, 1), :] + value)

        from_left = by_blocks(first, passed, zero)
        from_right = by_blocks(
            total - CELLS - first,
            lambda move, value: passed(total - 1 - move, value),
            zero,
        )
        entry, leave = radial.previous(first), radial.coupling(first + CELLS - 1)
        own = [sources[kind, pl.ds(first + place, 1), :] for place in range(CELLS)]
        own[0] = own[0] + from_left
        own[-1] = own[-1] + from_right
        answer = solve_block(radial, first, values, level, own, entry * left, leave * right)
        weight = ends[rows, :]
        out[0, rows, :] = weight * (from_left + entry * left * answer[0])
        out[1, rows, :] = weight * (from_right + leave * right * answer[-1])
        return 0

    lax.fori_loop(0, 8, step, 0)


def backward_kernel(total, spectrum, own, got, extra, sources, stages, lam, ends, mu, *rest):
    radial = Radial(*rest[:4], total)
    out, high, low, middle, wide_rows, field, sems = rest[4:]
    length = spectrum.shape[1]
    quarter = length // 8
    core = lax.rem(lax.axis_index("rad"), 2)
    first = lax.axis_index("rad") * CELLS
    level = mu[...][:1]
    chunk = min(64, quarter)
    entry, leave = radial.previous(first), radial.coupling(first + CELLS - 1)

    for slot in range(4):

        def step(index, _):
            kind = index // (quarter // chunk)
            spot = pl.ds(pl.multiple_of(index * chunk, chunk), chunk)
            rows = pl.ds(pl.multiple_of(slot * 2 * quarter + index * chunk, chunk), chunk)
            near = pl.ds(pl.multiple_of(slot % 2 * 2 * quarter + index * chunk, chunk), chunk)
            mine = core == slot // 2
            side = [jnp.where(mine, own[place, near, :], got[place, near, :]) for place in range(2)]
            weight = ends[rows, :]
            right = [
                spectrum[cell, rows, :] + weight * sources[kind, pl.ds(first + cell, 1), :]
                for cell in range(CELLS)
            ]
            right[0] = right[0] + (entry * side[0] + extra[0, rows, :])
            right[-1] = right[-1] + (leave * side[1] + extra[1, rows, :])
            answer = solve_block(radial, first, lam[rows, :], level, right)
            for cell in range(CELLS):
                one, two = split(answer[cell])
                columns = slice(cell * LANES, (cell + 1) * LANES)
                high[slot, spot, columns] = one
                low[slot, spot, columns] = two
            return 0

        lax.fori_loop(0, 2 * quarter // chunk, step, 0)
        upper = stages[slot * 2 * quarter : (slot + 1) * 2 * quarter, :]
        lower = stages[(4 + slot) * 2 * quarter : (5 + slot) * 2 * quarter, :]
        middle[slot] = dot(upper, high[slot]) + dot(upper, low[slot]) + dot(lower, high[slot])
    chunk = 16
    wide = stages[8 * 2 * quarter : 8 * 2 * quarter + 2 * LANES, :]
    for cell in range(CELLS):
        columns = slice(cell * LANES, (cell + 1) * LANES)
        for start in range(0, quarter, chunk):
            y = [
                middle[place // 2, pl.ds(place % 2 * quarter + start, chunk), columns]
                for place in range(8)
            ]
            for place, value in enumerate(gather_parts(y)):
                one, two = split(value)
                row = cell * length + place * quarter + start
                wide_rows[row : row + chunk, :LANES] = one
                wide_rows[row : row + chunk, LANES:] = two
    copies = []
    for part in range(4):
        start = part * 2 * quarter
        for cell in range(CELLS):
            row = cell * length + start
            both = dot(wide_rows[row : row + 2 * quarter, :], wide)
            field[pl.ds(start * CELLS + cell, 2 * quarter, stride=CELLS), :] = (
                both[:, :LANES] + both[:, LANES:]
            )
        rows = pl.ds(start * CELLS, 2 * quarter * CELLS)
        copies.append(pltpu.make_async_copy(field.at[rows], out.at[rows], sems.at[part]))
        copies[-1].start()
    for copy in copies:
        copy.wait()


def call(kernel, out_shapes, args, scalars=(), scratch=(), cost=1, room=20, held=(), out_held=(), name=None):
    specs = []
    for place in range(len(args)):
        space = pltpu.SMEM if place in scalars else pltpu.HBM if place in held else pltpu.VMEM
        specs.append(pl.BlockSpec(memory_space=space))
    outs = [jax.ShapeDtypeStruct(shape, F32) for shape in out_shapes]
    return pl.pallas_call(
        kernel,
        out_shape=outs,
        in_specs=specs,
        out_specs=[
            pl.BlockSpec(memory_space=pltpu.HBM if place in out_held else pltpu.VMEM)
            for place in range(len(outs))
        ],
        scratch_shapes=list(scratch),
        compiler_params=pltpu.CompilerParams(vmem_limit_bytes=room * 2**20),
        cost_estimate=pl.CostEstimate(
            flops=0, bytes_accessed=int(cost * 3.69e6), transcendentals=0
        ),
        name=name,
    )(*args)


def other_core(values):
    count = lax.axis_size("rad")
    return lax.ppermute(values, "rad", [(index, index ^ 1) for index in range(count)])


def between_chips(values, pairs):
    route = [(2 * a + core, 2 * b + core) for a, b in pairs for core in range(2)]
    return lax.ppermute(values, "rad", route)


def hop(axis, values, bit):
    count = lax.axis_size(axis)
    return lax.ppermute(values, axis, [(index, index ^ (1 << bit)) for index in range(count)])


def on_device(source, helmholtz, azimuth, vertical, radial):
    length, cells, depth = source.shape
    blocks = lax.axis_size("rad")
    chips = blocks // 2
    total = blocks * cells
    assert cells == CELLS and depth == LANES and lax.axis_size("az") == SLABS
    assert chips % 2 == 0
    half = length // 2
    quarter = length // 8
    scalars4 = (helmholtz, azimuth, vertical, radial)
    kept = total * 5 * quarter * LANES * 4 <= 12 * 2**20
    room = 20 if kept else 56

    basis = cosine_basis(depth)
    stage, eigen, end_weights, parity = slab_tables(length)

    def matrices(stages, last):
        high, low = two_halves(stages.reshape(-1, stages.shape[-1]))
        return jnp.asarray(np.concatenate([high, low, wide_basis(last)]))

    vertical_eigen = 2.0 - 2.0 * np.cos(math.pi / depth * np.arange(depth))
    levels = np.broadcast_to(vertical_eigen[None, :], (8, depth)).astype(np.float32)
    lam = jnp.asarray(spread(eigen))
    ends = jnp.asarray(spread(end_weights))
    mu = jnp.asarray(levels)
    tables = jnp.asarray(np.concatenate([spread(eigen), levels]))
    by_slot = eigen.reshape(4, 2, quarter)
    lam_shared = jnp.asarray(
        spread(np.concatenate([by_slot[0, 0], by_slot[0, 1], by_slot[1:, 0].reshape(-1)]))
    )
    group = depth // SLABS
    mu_groups = jnp.asarray(
        np.tile(vertical_eigen.reshape(SLABS, group), (1, SLABS)).astype(np.float32)
    )

    def packed(column):
        table = np.stack([column[parity > 0], column[parity < 0]]).reshape(2 * quarter, SLABS)
        return jnp.asarray(np.repeat(table, group, axis=1).astype(np.float32))

    lam_groups = packed(eigen)
    weight_groups = packed(2.0 * end_weights**2)

    def smem(start):
        return tuple(range(start, start + 4))

    wide_shape = (2 * quarter, CELLS * LANES)
    stages = matrices(stage, basis)
    spectrum, keep, send = call(
        functools.partial(forward_kernel, total),
        [(CELLS, length, LANES), (2, half, LANES), (2, half, LANES)],
        (source.reshape(8, quarter * CELLS, LANES), tables, stages)
        + scalars4,
        (),
        [
            pltpu.VMEM((8, quarter * CELLS, LANES), F32),
            pltpu.VMEM(tables.shape, F32),
            pltpu.VMEM(stages.shape, BF16),
        ]
        + [pltpu.SMEM((total,), F32)] * 4
        + [pltpu.VMEM((length * CELLS, 2 * LANES), BF16)]
        + [pltpu.VMEM((4,) + wide_shape, BF16)] * 2
        + [pltpu.VMEM((CELLS, length, LANES), F32), pltpu.SemaphoreType.DMA((12,))],
        cost=8,
        held=tuple(range(7)),
        out_held=(0,),
        room=57,
        name="forward",
    )
    got = other_core(send)
    azimuth_ports, _ = lax.optimization_barrier((azimuth, send))
    (ports,) = call(
        functools.partial(pair_ports_kernel, total),
        [(11, half, LANES)],
        (lam, mu, helmholtz, azimuth_ports, vertical, radial),
        smem(2),
        cost=2,
        room=room,
        name="pair_ports",
    )
    line = (half, LANES)
    whole, out = call(
        functools.partial(merge_kernel, chips),
        [(2, half, LANES), line],
        (keep, got, ports),
        cost=0.3,
        room=room,
        name="merge",
    )

    out, azimuth_ratios = lax.optimization_barrier((out, azimuth))
    store_shape = (total, (5 if kept else 1) * quarter, LANES)
    edge_shape = (2, 5 * quarter, LANES)
    ratios_out = call(
        functools.partial(ratios_kernel, total, kept),
        [edge_shape] + ([store_shape] if kept else []),
        (lam_shared, mu, helmholtz, azimuth_ratios, vertical, radial),
        smem(2),
        [] if kept else [pltpu.VMEM(store_shape, F32)],
        cost=5,
        room=room,
        name="ratios",
    )
    edges, store = ratios_out[0], tuple(ratios_out[1:])
    scratch_store = [] if kept else [pltpu.VMEM(store_shape, F32)]
    (links,) = call(
        functools.partial(chain_links_kernel, chips),
        [(7, half, LANES)],
        (ports, edges),
        cost=0.5,
        room=room,
        name="links",
    )
    (response,) = call(
        functools.partial(response_kernel, total),
        [(2, total, LANES)],
        (lam_groups, weight_groups, mu_groups, helmholtz, azimuth_ratios, vertical, radial),
        smem(3),
        [
            pltpu.VMEM((total, 2 * quarter, LANES), F32),
            pltpu.VMEM((2, CELLS, total, 8, LANES), F32),
            pltpu.VMEM((2, CELLS, total, LANES), F32),
        ],
        cost=5,
        room=room,
        name="response",
    )
    (packed_ends,) = call(
        functools.partial(ends_kernel, total, kept),
        [(4, total, LANES)],
        (response, spectrum, lam, ends, mu) + scalars4 + store,
        smem(5),
        [pltpu.VMEM((2, total, 8, LANES), F32)] + scratch_store,
        cost=3,
        room=room,
        name="ends",
    )
    incoming = None
    whole_late, _ = lax.optimization_barrier((whole, packed_ends))
    for edge in range(chips // 2 - 1):
        moved = between_chips(out, [(edge, edge + 1), (chips - 1 - edge, chips - 2 - edge)])
        incoming = moved if incoming is None else incoming + moved
        (out,) = call(
            inward_kernel,
            [line],
            (whole_late, incoming, links),
            cost=0.3,
            room=room,
            name="inward",
        )

    def join(axis, bit, common, own, other):
        shape = (2 * own.shape[0] - common, total, LANES)
        (result,) = call(
            functools.partial(join_kernel, axis, bit, common),
            [shape],
            (own, other),
            cost=0.3,
            room=room,
            name="join",
        )
        return result

    gathered = packed_ends
    for bit in range(1, blocks.bit_length() - 1):
        moved = hop("rad", gathered, bit)
        gathered = join("rad", bit, 2, gathered, moved)
    gathered = join("rad", 0, 2, gathered, hop("rad", gathered, 0))
    matrix_shape = (total, total // SLABS, LANES)
    minus_matrix, alternate_matrix, plus_matrix = call(
        functools.partial(capacity_kernel, total),
        [matrix_shape] * 3,
        (azimuth, gathered),
        (0,),
        cost=4,
        room=room,
        name="capacity",
    )
    slab_ends = gathered[0:2]
    moved = hop("az", slab_ends, 0)
    slab_ends, _ = lax.optimization_barrier((slab_ends, minus_matrix))
    slab_ends = join("az", 0, 0, slab_ends, moved)
    middle_after = slab_ends
    azimuth_pair, _ = lax.optimization_barrier((azimuth, slab_ends))
    (pair_matrix,) = call(
        functools.partial(pair_kernel, total),
        [matrix_shape],
        (azimuth_pair, minus_matrix, plus_matrix),
        (0,),
        cost=3,
        room=room,
        name="pair",
    )
    moved = hop("az", slab_ends, 1)
    slab_ends, _ = lax.optimization_barrier((slab_ends, pair_matrix))
    slab_ends = join("az", 1, 0, slab_ends, moved)

    low, high = chips // 2 - 1, chips // 2
    other = between_chips(out, [(low, high), (high, low)])
    whole_last, _ = lax.optimization_barrier((whole, middle_after))
    near, far = call(
        functools.partial(middle_kernel, chips),
        [line, line],
        (whole_last, incoming, out, other, links),
        cost=0.3,
        room=room,
        name="middle",
    )
    passed = None
    for edge in range(chips // 2 - 2, -1, -1):
        moved = between_chips(far, [(edge + 1, edge), (chips - 2 - edge, chips - 1 - edge)])
        passed = moved if passed is None else passed + moved
        if edge > 0:
            (far,) = call(
                outward_kernel,
                [line],
                (whole, incoming, passed, links),
                cost=0.3,
                room=room,
                name="outward",
            )
    keep_sources, send_sources = call(
        functools.partial(slabs_kernel, total),
        [(SLABS, total, LANES)] * 2,
        (azimuth, minus_matrix, alternate_matrix, pair_matrix, slab_ends),
        (0,),
        [pltpu.VMEM((2 * SLABS, total, LANES), F32), pltpu.VMEM((8, total, LANES), F32)],
        cost=2,
        room=room,
        name="slabs",
    )
    moved = hop("az", send_sources, 1)
    keep_sources, send_sources = call(
        functools.partial(halve_kernel, "az", 0),
        [(2, total, LANES)] * 2,
        (keep_sources, moved),
        cost=0.3,
        room=room,
        name="halve",
    )
    whole_parts, _ = lax.optimization_barrier((whole, send_sources))
    own_sides, send_sides = call(
        functools.partial(parts_kernel, chips),
        [(2, half, LANES)] * 2,
        (keep, got, ports, links, whole_parts, incoming, near, passed),
        cost=0.4,
        room=room,
        name="parts",
    )
    got_sides = other_core(send_sides)
    sources = (keep_sources, hop("az", send_sources, 0))
    all_sources, extra = call(
        functools.partial(sides_kernel, total, kept),
        [(2, total, LANES), (2, length, LANES)],
        (lam, ends, mu) + scalars4 + sources + store,
        smem(3),
        scratch_store,
        cost=3,
        room=room,
        name="sides",
    )
    (pressure,) = call(
        functools.partial(backward_kernel, total),
        [(length * CELLS, LANES)],
        (
            spectrum,
            own_sides,
            got_sides,
            extra,
            all_sources,
            matrices(np.swapaxes(stage, 1, 2), basis.T),
            lam,
            ends,
            mu,
        )
        + scalars4,
        smem(9),
        [pltpu.VMEM((4,) + wide_shape, BF16)] * 2
        + [pltpu.VMEM((4,) + wide_shape, F32), pltpu.VMEM((length * CELLS, 2 * LANES), BF16)]
        + [pltpu.VMEM((length * CELLS, LANES), F32), pltpu.SemaphoreType.DMA((4,))],
        out_held=(0,),
        cost=7,
        room=room,
        name="backward",
    )
    return pressure.reshape(length, CELLS, LANES)


def solution(mesh):
    in_specs = (P("az", "rad", None), P(), P(), P(), P())
    return jax.shard_map(
        on_device,
        mesh=mesh,
        in_specs=in_specs,
        out_specs=P("az", "rad", None),
        check_vma=False,
    )
```

```python
import functools
import math

import jax
import jax.numpy as jnp
import ml_dtypes
import numpy as np
from jax import lax
from jax.experimental import pallas as pl
from jax.experimental.pallas import tpu as pltpu
from jax.sharding import PartitionSpec as P

F32 = jnp.float32
BF16 = jnp.bfloat16
CELLS = 4
SLABS = 4
LANES = 128


def two_halves(table):
    high = table.astype(np.float32).astype(ml_dtypes.bfloat16)
    low = (table - high.astype(np.float64)).astype(np.float32).astype(ml_dtypes.bfloat16)
    return high, low


def cosine_basis(depth):
    rows = np.arange(depth)
    phases = (2 * rows[:, None] + 1) * rows[None, :] % (4 * depth)
    scales = np.where(rows == 0, math.sqrt(1.0 / depth), math.sqrt(2.0 / depth))
    return np.cos(math.pi / (2 * depth) * phases) * scales[None, :]


def wide_basis(basis):
    high, low = two_halves(basis)
    top = np.concatenate([high, low], axis=1)
    bottom = np.concatenate([high, np.zeros_like(high)], axis=1)
    return np.concatenate([top, bottom], axis=0)


def slab_tables(length):
    quarter = length // 8
    half = quarter // 2
    offsets = np.arange(quarter) + 0.5
    stage = np.zeros((4, 2 * quarter, 2 * quarter))
    modes = np.zeros((4, 2 * quarter), np.int64)

    def angle(mode):
        return 2 * np.pi * (mode[:, None] * offsets[None, :] % length) / length

    def scale(mode):
        single = (mode == 0) | (mode == length // 2)
        return np.where(single, np.sqrt(1 / length), np.sqrt(2 / length))[:, None]

    steps = np.arange(half)
    for first, mode, column, wave in (
        (0, 8 * steps, 0, np.cos),
        (half, 8 * steps + 4, quarter, np.cos),
        (quarter, 8 * (steps + 1), 0, np.sin),
        (quarter + half, 8 * steps + 4, quarter, np.sin),
    ):
        stage[0, first : first + half, column : column + quarter] = scale(mode) * wave(angle(mode))
        modes[0, first : first + half] = mode
    for slot in (1, 2, 3):
        mode = slot + 8 * np.arange(quarter)
        cosine, sine = scale(mode) * np.cos(angle(mode)), scale(mode) * np.sin(angle(mode))
        stage[slot] = np.block([[cosine, sine], [sine, -cosine]])
        modes[slot] = np.concatenate([mode, mode])
    modes = modes.reshape(-1)
    parity = np.tile(np.repeat([1, -1], quarter), 4)
    single = (modes == 0) | (modes == length // 2)
    size = np.where(single, np.sqrt(1 / length), np.sqrt(2 / length))
    ends = size * np.where(parity > 0, np.cos(np.pi * modes / length), np.sin(np.pi * modes / length))
    eigen = 2.0 - 2.0 * np.cos(2 * np.pi * modes / length)
    return stage, eigen, ends, parity


def spread(column):
    return np.broadcast_to(column[..., None], column.shape + (LANES,)).astype(np.float32)


def split(values):
    high = values.astype(BF16)
    low = (values - high.astype(F32)).astype(BF16)
    return high, low


def dot(left, right):
    return jnp.dot(left, right, preferred_element_type=F32)


def times_basis(values, wide):
    high, low = split(values)
    both = dot(jnp.concatenate([high, low], axis=1), wide)
    depth = values.shape[1]
    return both[:, :depth] + both[:, depth:]


class Radial:
    def __init__(self, helmholtz, azimuth, vertical, radial, total):
        self.refs = (helmholtz, azimuth, vertical, radial)
        self.total = total

    def coupling(self, cell):
        cell = jnp.asarray(cell, jnp.int32)
        return jnp.where(cell < self.total - 1, self.refs[3][cell], 0.0)

    def previous(self, cell):
        cell = jnp.asarray(cell, jnp.int32)
        return jnp.where(cell > 0, self.refs[3][jnp.maximum(cell - 1, 0)], 0.0)

    def diagonal(self, cell, lam, mu):
        base = self.refs[0][cell] + self.coupling(cell) + self.previous(cell)
        return lam * self.refs[1][cell] + (mu * self.refs[2][cell] + base)


def inverse(values):
    return pl.reciprocal(values, approx=False)


def solve_block(radial, first, lam, mu, right, add_first=None, add_last=None):
    rows = []
    factor = values = None
    for place in range(CELLS):
        cell = first + place
        diagonal = radial.diagonal(cell, lam, mu)
        if place == 0 and add_first is not None:
            diagonal = diagonal - add_first
        if place == CELLS - 1 and add_last is not None:
            diagonal = diagonal - add_last
        if place > 0:
            before = radial.previous(cell)
            pivot = inverse(diagonal - before * factor)
            values = (right[place] + before * values) * pivot
        else:
            pivot = inverse(diagonal)
            values = right[place] * pivot
        factor = radial.coupling(cell) * pivot
        rows.append((values, factor))
    answer = [rows[-1][0]]
    for values, factor in rows[-2::-1]:
        answer.insert(0, values + factor * answer[0])
    return answer


def block_ports(radial, first, lam, mu):
    diagonals = [radial.diagonal(first + place, lam, mu) for place in range(CELLS)]
    pivot = inverse(diagonals[0])
    forward = [pivot]
    for place in range(1, CELLS):
        before = radial.previous(first + place)
        pivot = inverse(diagonals[place] - before * before * pivot)
        forward.append(pivot)
    last = forward[-1]
    cross = last
    for place in range(CELLS - 2, -1, -1):
        cross = radial.coupling(first + place) * forward[place] * cross
    backward = inverse(diagonals[-1])
    for place in range(CELLS - 2, -1, -1):
        after = radial.coupling(first + place)
        backward = inverse(diagonals[place] - after * after * backward)
    entry, leave = radial.previous(first), radial.coupling(first + CELLS - 1)
    return backward * entry, cross * leave, cross * entry, last * leave


def chip_ports(radial, first, lam, mu):
    b1, g1, b2, g2 = block_ports(radial, first, lam, mu)
    c1, h1, c2, h2 = block_ports(radial, first + CELLS, lam, mu)
    mid = inverse(1.0 - g2 * c1)
    low = c1 * b2 * mid
    high = h1 * mid
    whole = (
        b1 + g1 * low,
        g1 * high,
        c2 * (b2 + g2 * low),
        h2 + c2 * g2 * high,
    )
    return (b1, g1, b2, g2), (c1, h1, c2, h2), mid, whole


def spread_parts(x):
    root = math.sqrt(0.5)
    s = [x[n] + x[n + 4] for n in range(4)]
    d = [x[n] - x[n + 4] for n in range(4)]
    even, odd = s[0] + s[2], s[1] + s[3]
    minus, plus = root * (d[1] - d[3]), root * (d[1] + d[3])
    return (
        even + odd,
        even - odd,
        d[0] + minus,
        -plus - d[2],
        s[0] - s[2],
        s[3] - s[1],
        d[0] - minus,
        d[2] - plus,
    )


def gather_parts(y):
    root = math.sqrt(0.5)
    plus, minus = y[0] + y[1], y[0] - y[1]
    s = (plus + y[4], minus - y[5], plus - y[4], minus + y[5])
    real, imag = root * (y[2] - y[6]), root * (y[3] + y[7])
    d = (y[2] + y[6], real - imag, y[7] - y[3], -real - imag)
    return [s[n] + d[n] for n in range(4)] + [s[n] - d[n] for n in range(4)]


def forward_kernel(total, source_in, tables_in, stages_in, *rest):
    scalars_in = rest[:4]
    spectrum_out, keep, send = rest[4:7]
    source, tables, stages, s0, s1, s2, s3, wide_rows, high, low, spectrum, sems = rest[7:]
    scalars = (s0, s1, s2, s3)
    length = source.shape[0] * source.shape[1] // CELLS
    quarter = length // 8
    eighth = quarter * CELLS
    pairs = []
    for part in range(2):
        rows = pl.ds(part * eighth // 2, eighth // 2)
        pairs.append((source_in.at[:, rows, :], source.at[:, rows, :]))
    pairs += [(stages_in, stages), (tables_in, tables)]
    pairs += list(zip(scalars_in, scalars))
    copies = [
        pltpu.make_async_copy(origin, target, sems.at[place])
        for place, (origin, target) in enumerate(pairs)
    ]
    for copy in copies:
        copy.start()
    radial = Radial(*scalars, total)
    core = lax.rem(lax.axis_index("rad"), 2)
    first = lax.axis_index("rad") * CELLS
    chunk = 16
    for start in range(0, quarter, chunk):
        if start * 2 % quarter == 0:
            copies[start * 2 // quarter].wait()
        for cell in range(CELLS):
            x = [
                source[n, pl.ds(start * CELLS + cell, chunk, stride=CELLS), :] for n in range(8)
            ]
            for place, part in enumerate(spread_parts(x)):
                one, two = split(part)
                row = cell * length + place * quarter + start
                wide_rows[row : row + chunk, :LANES] = one
                wide_rows[row : row + chunk, LANES:] = two
    copies[2].wait()
    wide = stages[8 * 2 * quarter : 8 * 2 * quarter + 2 * LANES, :]
    for cell in range(CELLS):
        for slot in range(4):
            row = cell * length + slot * 2 * quarter
            both = dot(wide_rows[row : row + 2 * quarter, :], wide)
            one, two = split(both[:, :LANES] + both[:, LANES:])
            columns = slice(cell * LANES, (cell + 1) * LANES)
            high[slot, :, columns] = one
            low[slot, :, columns] = two
    leaving = []
    for slot in range(4):
        upper = stages[slot * 2 * quarter : (slot + 1) * 2 * quarter, :]
        lower = stages[(4 + slot) * 2 * quarter : (5 + slot) * 2 * quarter, :]
        result = dot(upper, high[slot]) + dot(upper, low[slot]) + dot(lower, high[slot])
        for cell in range(CELLS):
            spectrum[cell, slot * 2 * quarter : (slot + 1) * 2 * quarter, :] = result[
                :, cell * LANES : (cell + 1) * LANES
            ]
        rows = pl.ds(slot * 2 * quarter, 2 * quarter)
        leaving.append(
            pltpu.make_async_copy(
                spectrum.at[:, rows, :], spectrum_out.at[:, rows, :], sems.at[8 + slot]
            )
        )
        leaving[-1].start()
    for copy in copies[3:]:
        copy.wait()
    chunk = 64
    half = length // 2
    level = tables[length : length + 1, :]

    def step(index, _):
        ends = []
        for part in range(2):
            rows = pl.ds(pl.multiple_of(part * half + index * chunk, chunk), chunk)
            right = [spectrum[cell, rows, :] for cell in range(CELLS)]
            answer = solve_block(radial, first, tables[rows, :], level, right)
            ends.append((answer[0], answer[-1]))
        rows = pl.ds(pl.multiple_of(index * chunk, chunk), chunk)
        for place in range(2):
            keep[place, rows, :] = jnp.where(core == 0, ends[0][place], ends[1][place])
            send[place, rows, :] = jnp.where(core == 0, ends[1][place], ends[0][place])
        return 0

    lax.fori_loop(0, half // chunk, step, 0)
    for copy in leaving:
        copy.wait()


def shared_row(slot, kind, quarter):
    return pl.multiple_of(jnp.where(slot == 0, kind, slot + 1) * quarter, quarter)


def pair_ports_kernel(total, lam, mu, *rest):
    radial = Radial(*rest[:4], total)
    (out,) = rest[4:]
    half = out.shape[1]
    quarter = half // 4
    chips = total // (2 * CELLS)
    core = lax.rem(lax.axis_index("rad"), 2)
    chip = lax.axis_index("rad") // 2
    left_side = chip < chips // 2
    first = chip * (2 * CELLS)
    level = mu[...][:1]
    chunk = min(64, quarter)

    def step(index, _):
        rows = pl.ds(pl.multiple_of(index * chunk, chunk), chunk)
        spot = pl.ds(pl.multiple_of(core * half + index * chunk, chunk), chunk)
        (b1, g1, b2, g2), (c1, h1, c2, h2), mid, (w1, w2, w3, w4) = chip_ports(
            radial, first, lam[spot, :], level
        )
        rff, rnn = jnp.where(left_side, w1, w4), jnp.where(left_side, w4, w1)
        rfn, rnf = jnp.where(left_side, w2, w3), jnp.where(left_side, w3, w2)
        for place, value in enumerate((g1, b2, g2, c1, h1, c2, mid, rff, rfn, rnf, rnn)):
            out[place, rows, :] = value
        return 0

    lax.fori_loop(0, half // chunk, step, 0)


def chain_links_kernel(chips, ports, edges, out):
    half = out.shape[1]
    quarter = half // 4
    core = lax.rem(lax.axis_index("rad"), 2)
    left_side = lax.axis_index("rad") // 2 < chips // 2
    chunk = min(64, quarter)

    def step(index, _):
        rows = pl.ds(pl.multiple_of(index * chunk, chunk), chunk)
        block = index * chunk // quarter
        start = shared_row(core * 2 + block // 2, lax.rem(block, 2), quarter)
        spot = pl.ds(pl.multiple_of(start + lax.rem(index * chunk, quarter), chunk), chunk)
        rff, rfn, rnf, rnn = (ports[7 + place, rows, :] for place in range(4))
        left, right = edges[0, spot, :], edges[1, spot, :]
        far, near = jnp.where(left_side, left, right), jnp.where(left_side, right, left)
        pivot = inverse(1.0 - rff * far)
        onward = rnn + rnf * far * rfn * pivot
        for place, value in enumerate(
            (rff, pivot, rfn * pivot, rnf, far, near, inverse(1.0 - near * onward))
        ):
            out[place, rows, :] = value
        return 0

    lax.fori_loop(0, half // chunk, step, 0)


def merge_kernel(chips, keep, got, ports, whole, out):
    half = keep.shape[1]
    core = lax.rem(lax.axis_index("rad"), 2)
    left_side = lax.axis_index("rad") // 2 < chips // 2
    chunk = 32

    def step(index, _):
        rows = pl.ds(pl.multiple_of(index * chunk, chunk), chunk)
        g1, b2, g2, c1, h1, c2, mid = (ports[place, rows, :] for place in range(7))
        mine = [keep[place, rows, :] for place in range(2)]
        other = [got[place, rows, :] for place in range(2)]
        low = [jnp.where(core == 0, m, o) for m, o in zip(mine, other)]
        high = [jnp.where(core == 0, o, m) for m, o in zip(mine, other)]
        upper = (high[0] + c1 * low[1]) * mid
        first = low[0] + g1 * upper
        last = high[1] + c2 * (low[1] + g2 * upper)
        near = jnp.where(left_side, last, first)
        whole[0, rows, :] = jnp.where(left_side, first, last)
        whole[1, rows, :] = near
        out[rows, :] = near
        return 0

    lax.fori_loop(0, half // chunk, step, 0)


def inward_kernel(whole, incoming, links, out):
    half = out.shape[0]
    chunk = 32

    def step(index, _):
        rows = pl.ds(pl.multiple_of(index * chunk, chunk), chunk)
        rff, pivot, _rfn, rnf, far = (links[place, rows, :] for place in range(5))
        value = incoming[rows, :]
        origin = (whole[0, rows, :] + rff * value) * pivot
        out[rows, :] = whole[1, rows, :] + rnf * (value + far * origin)
        return 0

    lax.fori_loop(0, half // chunk, step, 0)


def middle_kernel(chips, whole, incoming, own, other, links, near_out, far_out):
    half = far_out.shape[0]
    chip = lax.axis_index("rad") // 2
    inner = (chip == chips // 2) | (chip == chips // 2 - 1)
    chunk = 32

    def step(index, _):
        rows = pl.ds(pl.multiple_of(index * chunk, chunk), chunk)
        rff, pivot, hold, _rnf, _far, near, close = (
            links[place, rows, :] for place in range(7)
        )
        value = (other[rows, :] + near * own[rows, :]) * close
        value = jnp.where(inner, value, 0.0)
        origin = (whole[0, rows, :] + rff * incoming[rows, :]) * pivot
        near_out[rows, :] = value
        far_out[rows, :] = origin + hold * value
        return 0

    lax.fori_loop(0, half // chunk, step, 0)


def outward_kernel(whole, incoming, near_in, links, far_out):
    half = far_out.shape[0]
    chunk = 32

    def step(index, _):
        rows = pl.ds(pl.multiple_of(index * chunk, chunk), chunk)
        rff, pivot, hold = (links[place, rows, :] for place in range(3))
        origin = (whole[0, rows, :] + rff * incoming[rows, :]) * pivot
        far_out[rows, :] = origin + hold * near_in[rows, :]
        return 0

    lax.fori_loop(0, half // chunk, step, 0)


def parts_kernel(chips, keep, got, ports, links, whole, incoming, near_one, near_two, own, send):
    half = keep.shape[1]
    core = lax.rem(lax.axis_index("rad"), 2)
    left_side = lax.axis_index("rad") // 2 < chips // 2
    chunk = 32

    def step(index, _):
        rows = pl.ds(pl.multiple_of(index * chunk, chunk), chunk)
        _g1, b2, g2, c1, h1, _c2, mid = (ports[place, rows, :] for place in range(7))
        rff, pivot, hold, _rnf, far = (links[place, rows, :] for place in range(5))
        near = near_one[rows, :] + near_two[rows, :]
        value = incoming[rows, :]
        outer = value + far * ((whole[0, rows, :] + rff * value) * pivot + hold * near)
        left, right = jnp.where(left_side, outer, near), jnp.where(left_side, near, outer)
        last = jnp.where(core == 0, keep[1, rows, :], got[1, rows, :]) + b2 * left
        opening = jnp.where(core == 0, got[0, rows, :], keep[0, rows, :]) + h1 * right
        upper = (opening + c1 * last) * mid
        lower = last + g2 * upper
        own[0, rows, :] = jnp.where(core == 0, left, lower)
        own[1, rows, :] = jnp.where(core == 0, upper, right)
        send[0, rows, :] = jnp.where(core == 0, lower, left)
        send[1, rows, :] = jnp.where(core == 0, right, upper)
        return 0

    lax.fori_loop(0, half // chunk, step, 0)


def fold_rows(values):
    parts = [values[start : start + 8] for start in range(0, values.shape[0], 8)]
    while len(parts) > 1:
        parts = [a + b for a, b in zip(parts[::2], parts[1::2])]
    return parts[0]


def by_blocks(count, body, carry):
    def block(index, carry):
        for place in range(CELLS):
            carry = body(index * CELLS + place, carry)
        return carry

    return lax.fori_loop(0, lax.div(count, CELLS), block, carry)


def ratios(radial, first, lam, mu, left_store, right_store):
    total = radial.total
    shape = lam.shape

    def leftward(cell, factor):
        pivot = inverse(radial.diagonal(cell, lam, mu) - radial.previous(cell) * factor)
        factor = radial.coupling(cell) * pivot
        left_store[cell] = factor
        return factor

    def rightward(step, factor):
        cell = total - 1 - step
        pivot = inverse(radial.diagonal(cell, lam, mu) - radial.coupling(cell) * factor)
        factor = radial.previous(cell) * pivot
        right_store[cell] = factor
        return factor

    zero = jnp.zeros(shape, F32)
    left = by_blocks(first, leftward, zero)
    right = by_blocks(total - CELLS - first, rightward, zero)
    return left, right


def ratios_kernel(total, kept, lam, mu, *rest):
    radial = Radial(*rest[:4], total)
    edges, store = rest[4:]
    first = lax.axis_index("rad") * CELLS
    opening = lax.axis_index("rad") // 2 * (2 * CELLS)
    level = mu[...][:1]
    chunk = lam.shape[0] // (2 if kept else 5)

    def step(index, _):
        rows = pl.ds(pl.multiple_of(index * chunk, chunk), chunk)
        view = store.at[:, rows, :] if kept else store
        ratios(radial, first, lam[rows, :], level, view, view)
        left = view[jnp.maximum(opening - 1, 0)]
        right = view[jnp.minimum(opening + 2 * CELLS, total - 1)]
        edges[0, rows, :] = jnp.where(opening > 0, left, 0.0)
        edges[1, rows, :] = jnp.where(opening + 2 * CELLS < total, right, 0.0)
        return 0

    lax.fori_loop(0, lam.shape[0] // chunk, step, 0)


def outside(view, first, total):
    left = jnp.where(first > 0, view[jnp.maximum(first - 1, 0)], 0.0)
    right = view[jnp.minimum(first + CELLS, total - 1)]
    return left, jnp.where(first + CELLS < total, right, 0.0)


def stored_view(store, index, chunk):
    start = shared_row(index // 2, lax.rem(index, 2), chunk)
    return store.at[:, pl.ds(start, chunk), :]


def ends_kernel(total, kept, response, spectrum, lam, ends, mu, *rest):
    radial = Radial(*rest[:4], total)
    if kept:
        store, out, sums = rest[4:]
    else:
        out, sums, store = rest[4:]
    first = lax.axis_index("rad") * CELLS
    level = mu[...][:1]
    chunk = spectrum.shape[1] // 8
    sums[...] = jnp.zeros_like(sums)

    def start(kind, index, view, left, right):
        rows = pl.ds(pl.multiple_of(index * chunk, chunk), chunk)
        weight = 2.0 * ends[rows, :]
        answer = solve_block(
            radial,
            first,
            lam[rows, :],
            level,
            [weight * spectrum[cell, rows, :] for cell in range(CELLS)],
            radial.previous(first) * left,
            radial.coupling(first + CELLS - 1) * right,
        )
        for place in range(CELLS):
            sums[kind, first + place] += fold_rows(answer[place])
        return answer

    def spread_out(kinds, views, answers):
        def onward(cell, values):
            values = [view[cell] * value for view, value in zip(views, values)]
            for kind, value in zip(kinds, values):
                sums[kind, cell] += fold_rows(value)
            return tuple(values)

        by_blocks(
            first,
            lambda move, values: onward(first - 1 - move, values),
            tuple(answer[0] for answer in answers),
        )
        by_blocks(
            total - CELLS - first,
            lambda move, values: onward(first + CELLS + move, values),
            tuple(answer[-1] for answer in answers),
        )

    if kept:

        def step(slot, _):
            views = [stored_view(store, 2 * slot + kind, chunk) for kind in range(2)]
            answers = [
                start(kind, 2 * slot + kind, views[kind], *outside(views[kind], first, total))
                for kind in range(2)
            ]
            spread_out((0, 1), views, answers)
            return 0

        lax.fori_loop(0, 4, step, 0)
    else:

        def step(index, _):
            kind = lax.rem(index, 2)
            rows = pl.ds(pl.multiple_of(index * chunk, chunk), chunk)
            left, right = ratios(radial, first, lam[rows, :], level, store, store)
            spread_out((kind,), (store,), [start(kind, index, store, left, right)])
            return 0

        lax.fori_loop(0, 8, step, 0)
    for kind in range(2):
        for cell in range(total):
            out[kind, cell : cell + 1, :] = jnp.sum(sums[kind, cell], axis=0, keepdims=True)
    out[2:4] = response[...]


def join_kernel(axis, bit, common, own, other, out):
    high = lax.rem(lax.div(lax.axis_index(axis), 1 << bit), 2)
    count = own.shape[0] - common
    if common:
        out[0:common] = own[0:common] + other[0:common]
    out[pl.ds(common + high * count, count)] = own[common:]
    out[pl.ds(common + (1 - high) * count, count)] = other[common:]


def halve_kernel(axis, bit, own, other, keep, send):
    high = lax.rem(lax.div(lax.axis_index(axis), 1 << bit), 2)
    count = keep.shape[0]
    keep[...] = own[pl.ds(high * count, count)] + other[pl.ds(high * count, count)]
    there = pl.ds((1 - high) * count, count)
    send[...] = own[there] + other[there]


def response_kernel(total, lam, weight, mu, *rest):
    radial = Radial(*rest[:4], total)
    out, store, sums, lines = rest[4:]
    first = lax.axis_index("rad") * CELLS
    level = mu[pl.ds(lax.axis_index("az"), 1), :]
    group = LANES // SLABS
    chunk = lam.shape[0] // 2
    sums[...] = jnp.zeros_like(sums)
    lefts, rights = ratios(radial, first, lam[...], level, store, store)

    for kind in range(2):
        rows = slice(kind * chunk, (kind + 1) * chunk)
        source = weight[rows, :]
        zero = jnp.zeros_like(source)
        openings, closings = [], []
        for place in range(CELLS):
            answer = solve_block(
                radial,
                first,
                lam[rows, :],
                level,
                [source if cell == place else zero for cell in range(CELLS)],
                radial.previous(first) * lefts[rows],
                radial.coupling(first + CELLS - 1) * rights[rows],
            )
            for cell in range(CELLS):
                sums[kind, place, first + cell] += fold_rows(answer[cell])
            openings.append(answer[0])
            closings.append(answer[-1])

        def outward(cell, factor, edges):
            factor = store[cell, rows, :] * factor
            for place in range(CELLS):
                sums[kind, place, cell] += fold_rows(factor * edges[place])
            return factor

        one = jnp.ones_like(source)
        by_blocks(first, lambda move, factor: outward(first - 1 - move, factor, openings), one)
        by_blocks(
            total - CELLS - first,
            lambda move, factor: outward(first + CELLS + move, factor, closings),
            one,
        )

    lane = lax.broadcasted_iota(jnp.int32, (1, LANES), 1) // group

    def close(cell, _):
        for kind in range(2):
            for place in range(CELLS):
                lines[kind, place, pl.ds(cell, 1), :] = jnp.sum(
                    sums[kind, place, cell], axis=0, keepdims=True
                )
        return 0

    lax.fori_loop(0, total, close, 0, unroll=8)
    for kind in range(2):
        result = jnp.zeros((total, LANES), F32)
        for place in range(CELLS):
            line = lines[kind, place]
            line = line + pltpu.roll(line, 2 * group, 1)
            line = line + pltpu.roll(line, group, 1)
            result = jnp.where(lane == place, line, result)
        out[kind] = result


def lane_groups():
    return lax.broadcasted_iota(jnp.int32, (1, LANES), 1) // (LANES // SLABS)


def to_all_groups(values, group):
    width = LANES // SLABS
    values = jnp.where(lane_groups() == group, values, 0.0)
    values = values + pltpu.roll(values, 2 * width, 1)
    return values + pltpu.roll(values, width, 1)


def fold_cells(values):
    width = values.shape[0] // SLABS
    result = values[:width]
    for group in range(1, SLABS):
        part = values[group * width : (group + 1) * width]
        result = jnp.where(lane_groups() == group, part, result)
    return result


def unfold_cells(values):
    return jnp.concatenate([to_all_groups(values, group) for group in range(SLABS)])


def invert(matrices, total):
    width = total // SLABS
    step_size = 8
    rows = lax.broadcasted_iota(jnp.int32, (width, LANES), 0)
    cells = rows + lane_groups() * width

    def step(panel, _):
        base = pl.multiple_of(panel * step_size, step_size)
        group = lax.div(base, width)
        spot_rows = pl.ds(pl.multiple_of(lax.rem(base, width), step_size), step_size)
        inside = (cells >= base) & (cells < base + step_size)
        state = []
        for matrix in matrices:
            lines = [matrix[base + place] for place in range(step_size)]
            corners = [
                to_all_groups(matrix[base + place, spot_rows, :], group)
                for place in range(step_size)
            ]
            state.append((lines, corners))
        for place in range(step_size):
            mark = cells == base + place
            spot = lax.broadcasted_iota(jnp.int32, (step_size, LANES), 0) == place
            for lines, corners in state:
                scale = inverse(corners[place][place : place + 1])
                line = jnp.where(mark, 1.0, lines[place]) * scale
                corner = jnp.where(spot, 1.0, corners[place]) * scale
                for row in range(step_size):
                    if row == place:
                        continue
                    factor = corners[row][place : place + 1]
                    lines[row] = jnp.where(mark, 0.0, lines[row]) - factor * line
                    corners[row] = jnp.where(spot, 0.0, corners[row]) - factor * corner
                lines[place], corners[place] = line, corner

        batch = 32

        def update(index, _):
            for matrix, (lines, _corners) in zip(matrices, state):
                spots = [index * batch + place for place in range(batch)]
                corners = [to_all_groups(matrix[spot, spot_rows, :], group) for spot in spots]
                values = [jnp.where(inside, 0.0, matrix[spot]) for spot in spots]
                for place in range(step_size):
                    values = [
                        value - corner[place : place + 1] * lines[place]
                        for value, corner in zip(values, corners)
                    ]
                for spot, value in zip(spots, values):
                    matrix[spot] = value
            return 0

        lax.fori_loop(0, total // batch, update, 0)
        for matrix, (lines, _corners) in zip(matrices, state):
            for place in range(step_size):
                matrix[base + place] = lines[place]
        return 0

    lax.fori_loop(0, total // step_size, step, 0)


def per_cell(total, azimuth, top):
    width = total // SLABS
    cells = lax.broadcasted_iota(jnp.int32, (width, LANES), 0) + lane_groups() * width

    def column(cell, value):
        return jnp.where(cells == cell, azimuth[cell], value)

    return top * inverse(lax.fori_loop(0, total, column, jnp.ones((width, LANES), F32), unroll=8))


def capacity_kernel(total, azimuth, responses, *outs):
    minus_out, alternate_out, pair_out = outs
    chips = total // (2 * CELLS)
    width = total // SLABS
    shift = LANES // SLABS
    lane = lane_groups()
    cells = lax.broadcasted_iota(jnp.int32, (width, LANES), 0) + lane * width
    half = per_cell(total, azimuth, 0.5)
    for block in range(2 * chips):
        start = 2 + 2 * (block % 2 * chips + block // 2)
        for kind in range(2):
            parts = [
                responses[start + kind, group * width : (group + 1) * width, :]
                for group in range(SLABS)
            ]
            for place in range(CELLS):
                row = jnp.zeros((width, LANES), F32)
                for group, part in enumerate(parts):
                    turn = (group - place) % SLABS
                    part = pltpu.roll(part, turn * shift, 1) if turn else part
                    row = jnp.where(lane == group, part, row)
                cell = block * CELLS + place
                own = jnp.where(cells == cell, half, 0.0)
                if kind == 0:
                    alternate_out[cell] = own + row
                    pair_out[cell] = own + row
                else:
                    minus_out[cell] = own - row
    invert([minus_out, alternate_out], total)


def pair_kernel(total, azimuth, minus_matrix, plus_matrix, pair_out):
    scale = per_cell(total, azimuth, 0.25)

    def add(cell, _):
        own = inverse(jnp.full((1, LANES), azimuth[cell], F32))
        pair_out[cell] = plus_matrix[cell] + minus_matrix[cell] * (scale * own)
        return 0

    lax.fori_loop(0, total, add, 0, unroll=8)
    invert([pair_out], total)


def apply_matrix(matrix, store, slots):
    total = matrix.shape[0]
    results = [[None] * 4 for _ in slots]
    for cell in range(total):
        line = matrix[cell]
        for place, slot in enumerate(slots):
            term = line * store[slot, cell : cell + 1, :]
            before = results[place][cell % 4]
            results[place][cell % 4] = term if before is None else before + term
    return [(r[0] + r[1]) + (r[2] + r[3]) for r in results]


def slabs_kernel(total, azimuth, minus_matrix, alternate_matrix, pair_matrix, *rest):
    values, keep, send, results, store = rest
    slab = lax.axis_index("az")
    width = total // SLABS
    shift = LANES // SLABS
    lane = lane_groups()

    def channels(kind):
        u = [values[2 * place + kind] for place in range(SLABS)]
        mixed = (u[0] - u[2], u[3] - u[1], (u[0] + u[2]) - (u[1] + u[3]))
        return [to_all_groups(value, slab) for value in mixed]

    sums, differences = channels(0), channels(1)
    half = per_cell(total, azimuth, 0.5)
    for place in range(3):
        store[place] = differences[place]
    store[3] = -sums[2]
    lead_real, lead_imag, minus_alternate = apply_matrix(minus_matrix, store, (0, 1, 2))
    (plus_alternate,) = apply_matrix(alternate_matrix, store, (3,))
    store[4] = unfold_cells(-half * lead_imag - fold_cells(sums[0]))
    store[5] = unfold_cells(half * lead_real - fold_cells(sums[1]))
    plus_real, plus_imag = apply_matrix(pair_matrix, store, (4, 5))
    store[6] = unfold_cells(-half * plus_imag)
    store[7] = unfold_cells(half * plus_real)
    more_real, more_imag = apply_matrix(minus_matrix, store, (6, 7))
    found = (
        (plus_real, plus_imag, plus_alternate),
        (lead_real + more_real, lead_imag + more_imag, minus_alternate),
    )
    for kind, (real, imag, alternate) in enumerate(found):
        folded = (
            0.25 * (2.0 * real + alternate),
            0.25 * (-2.0 * imag - alternate),
            0.25 * (alternate - 2.0 * real),
            0.25 * (2.0 * imag - alternate),
        )
        for place, value in enumerate(folded):
            for group in range(SLABS):
                turn = lax.rem(slab - group + SLABS, SLABS) * shift
                rows = slice(group * width, (group + 1) * width)
                results[2 * place + kind, rows, :] = jnp.where(
                    lane == slab, pltpu.roll(value, turn, 1), 0.0
                )
    high = lax.div(slab, SLABS // 2)
    keep[...] = results[pl.ds(high * SLABS, SLABS)]
    send[...] = results[pl.ds((1 - high) * SLABS, SLABS)]


def sides_kernel(total, kept, lam, ends, mu, *rest):
    radial = Radial(*rest[:4], total)
    own_part, other_part = rest[4:6]
    if kept:
        store, sources, out = rest[6:]
    else:
        sources, out, store = rest[6:]
    sources[...] = own_part[...] + other_part[...]
    first = lax.axis_index("rad") * CELLS
    level = mu[...][:1]
    chunk = lam.shape[0] // 8
    entry, leave = radial.previous(first), radial.coupling(first + CELLS - 1)

    def inflow(kinds, views):
        zeros = tuple(jnp.zeros((chunk, LANES), F32) for _ in kinds)

        def passed(cell, values):
            return tuple(
                view[cell] * (sources[kind, pl.ds(cell, 1), :] + value)
                for kind, view, value in zip(kinds, views, values)
            )

        from_left = by_blocks(first, passed, zeros)
        from_right = by_blocks(
            total - CELLS - first,
            lambda move, values: passed(total - 1 - move, values),
            zeros,
        )
        return from_left, from_right

    def finish(kind, index, left, right, from_left, from_right):
        rows = pl.ds(pl.multiple_of(index * chunk, chunk), chunk)
        own = [sources[kind, pl.ds(first + place, 1), :] for place in range(CELLS)]
        own[0] = own[0] + from_left
        own[-1] = own[-1] + from_right
        answer = solve_block(radial, first, lam[rows, :], level, own, entry * left, leave * right)
        weight = ends[rows, :]
        out[0, rows, :] = weight * (from_left + entry * left * answer[0])
        out[1, rows, :] = weight * (from_right + leave * right * answer[-1])

    if kept:

        def step(slot, _):
            views = [stored_view(store, 2 * slot + kind, chunk) for kind in range(2)]
            from_left, from_right = inflow((0, 1), views)
            for kind, view in enumerate(views):
                left, right = outside(view, first, total)
                finish(kind, 2 * slot + kind, left, right, from_left[kind], from_right[kind])
            return 0

        lax.fori_loop(0, 4, step, 0)
    else:

        def step(index, _):
            kind = lax.rem(index, 2)
            rows = pl.ds(pl.multiple_of(index * chunk, chunk), chunk)
            left, right = ratios(radial, first, lam[rows, :], level, store, store)
            from_left, from_right = inflow((kind,), (store,))
            finish(kind, index, left, right, from_left[0], from_right[0])
            return 0

        lax.fori_loop(0, 8, step, 0)


def backward_kernel(total, spectrum, own, got, extra, sources, stages, lam, ends, mu, *rest):
    radial = Radial(*rest[:4], total)
    out, high, low, middle, wide_rows, field, sems = rest[4:]
    length = spectrum.shape[1]
    quarter = length // 8
    core = lax.rem(lax.axis_index("rad"), 2)
    first = lax.axis_index("rad") * CELLS
    level = mu[...][:1]
    chunk = min(128, quarter)
    entry, leave = radial.previous(first), radial.coupling(first + CELLS - 1)

    for slot in range(4):

        def step(index, _):
            kind = index // (quarter // chunk)
            spot = pl.ds(pl.multiple_of(index * chunk, chunk), chunk)
            rows = pl.ds(pl.multiple_of(slot * 2 * quarter + index * chunk, chunk), chunk)
            near = pl.ds(pl.multiple_of(slot % 2 * 2 * quarter + index * chunk, chunk), chunk)
            mine = core == slot // 2
            side = [jnp.where(mine, own[place, near, :], got[place, near, :]) for place in range(2)]
            weight = ends[rows, :]
            right = [
                spectrum[cell, rows, :] + weight * sources[kind, pl.ds(first + cell, 1), :]
                for cell in range(CELLS)
            ]
            right[0] = right[0] + (entry * side[0] + extra[0, rows, :])
            right[-1] = right[-1] + (leave * side[1] + extra[1, rows, :])
            answer = solve_block(radial, first, lam[rows, :], level, right)
            for cell in range(CELLS):
                one, two = split(answer[cell])
                columns = slice(cell * LANES, (cell + 1) * LANES)
                high[slot, spot, columns] = one
                low[slot, spot, columns] = two
            return 0

        lax.fori_loop(0, 2 * quarter // chunk, step, 0)
        upper = stages[slot * 2 * quarter : (slot + 1) * 2 * quarter, :]
        lower = stages[(4 + slot) * 2 * quarter : (5 + slot) * 2 * quarter, :]
        middle[slot] = dot(upper, high[slot]) + dot(upper, low[slot]) + dot(lower, high[slot])
    chunk = 16
    wide = stages[8 * 2 * quarter : 8 * 2 * quarter + 2 * LANES, :]
    for cell in range(CELLS):
        columns = slice(cell * LANES, (cell + 1) * LANES)
        for start in range(0, quarter, chunk):
            y = [
                middle[place // 2, pl.ds(place % 2 * quarter + start, chunk), columns]
                for place in range(8)
            ]
            for place, value in enumerate(gather_parts(y)):
                one, two = split(value)
                row = cell * length + place * quarter + start
                wide_rows[row : row + chunk, :LANES] = one
                wide_rows[row : row + chunk, LANES:] = two
    copies = []
    for part in range(4):
        start = part * 2 * quarter
        for cell in range(CELLS):
            row = cell * length + start
            both = dot(wide_rows[row : row + 2 * quarter, :], wide)
            field[pl.ds(start * CELLS + cell, 2 * quarter, stride=CELLS), :] = (
                both[:, :LANES] + both[:, LANES:]
            )
        rows = pl.ds(start * CELLS, 2 * quarter * CELLS)
        copies.append(pltpu.make_async_copy(field.at[rows], out.at[rows], sems.at[part]))
        copies[-1].start()
    for copy in copies:
        copy.wait()


def call(kernel, out_shapes, args, scalars=(), scratch=(), cost=1, room=20, held=(), out_held=(), name=None):
    specs = []
    for place in range(len(args)):
        space = pltpu.SMEM if place in scalars else pltpu.HBM if place in held else pltpu.VMEM
        specs.append(pl.BlockSpec(memory_space=space))
    outs = [
        (pltpu.HBM if place in out_held else jax.ShapeDtypeStruct)(shape, F32)
        for place, shape in enumerate(out_shapes)
    ]
    args = [
        pltpu.with_memory_space_constraint(arg, pltpu.HBM) if place in held else arg
        for place, arg in enumerate(args)
    ]
    return pl.pallas_call(
        kernel,
        out_shape=outs,
        in_specs=specs,
        out_specs=[
            pl.BlockSpec(memory_space=pltpu.HBM if place in out_held else pltpu.VMEM)
            for place in range(len(outs))
        ],
        scratch_shapes=list(scratch),
        compiler_params=pltpu.CompilerParams(vmem_limit_bytes=room * 2**20),
        cost_estimate=pl.CostEstimate(
            flops=0, bytes_accessed=int(cost * 3.69e6), transcendentals=0
        ),
        name=name,
    )(*args)


def other_core(values):
    count = lax.axis_size("rad")
    return lax.ppermute(values, "rad", [(index, index ^ 1) for index in range(count)])


def between_chips(values, pairs):
    route = [(2 * a + core, 2 * b + core) for a, b in pairs for core in range(2)]
    return lax.ppermute(values, "rad", route)


def hop(axis, values, bit):
    count = lax.axis_size(axis)
    return lax.ppermute(values, axis, [(index, index ^ (1 << bit)) for index in range(count)])


def on_device(source, helmholtz, azimuth, vertical, radial):
    length, cells, depth = source.shape
    blocks = lax.axis_size("rad")
    chips = blocks // 2
    total = blocks * cells
    assert cells == CELLS and depth == LANES and lax.axis_size("az") == SLABS
    assert chips % 2 == 0
    half = length // 2
    quarter = length // 8
    scalars4 = (helmholtz, azimuth, vertical, radial)
    kept = total * 5 * quarter * LANES * 4 <= 12 * 2**20
    room = 20 if kept else 56

    basis = cosine_basis(depth)
    stage, eigen, end_weights, parity = slab_tables(length)

    def matrices(stages, last):
        high, low = two_halves(stages.reshape(-1, stages.shape[-1]))
        return jnp.asarray(np.concatenate([high, low, wide_basis(last)]))

    vertical_eigen = 2.0 - 2.0 * np.cos(math.pi / depth * np.arange(depth))
    levels = np.broadcast_to(vertical_eigen[None, :], (8, depth)).astype(np.float32)
    lam = jnp.asarray(spread(eigen))
    ends = jnp.asarray(spread(end_weights))
    mu = jnp.asarray(levels)
    tables = jnp.asarray(np.concatenate([spread(eigen), levels]))
    by_slot = eigen.reshape(4, 2, quarter)
    lam_shared = jnp.asarray(
        spread(np.concatenate([by_slot[0, 0], by_slot[0, 1], by_slot[1:, 0].reshape(-1)]))
    )
    group = depth // SLABS
    mu_groups = jnp.asarray(
        np.tile(vertical_eigen.reshape(SLABS, group), (1, SLABS)).astype(np.float32)
    )

    def packed(column):
        table = np.stack([column[parity > 0], column[parity < 0]]).reshape(2 * quarter, SLABS)
        return jnp.asarray(np.repeat(table, group, axis=1).astype(np.float32))

    lam_groups = packed(eigen)
    weight_groups = packed(2.0 * end_weights**2)

    def smem(start):
        return tuple(range(start, start + 4))

    wide_shape = (2 * quarter, CELLS * LANES)
    stages = matrices(stage, basis)
    spectrum, keep, send = call(
        functools.partial(forward_kernel, total),
        [(CELLS, length, LANES), (2, half, LANES), (2, half, LANES)],
        (source.reshape(8, quarter * CELLS, LANES), tables, stages)
        + scalars4,
        (),
        [
            pltpu.VMEM((8, quarter * CELLS, LANES), F32),
            pltpu.VMEM(tables.shape, F32),
            pltpu.VMEM(stages.shape, BF16),
        ]
        + [pltpu.SMEM((total,), F32)] * 4
        + [pltpu.VMEM((length * CELLS, 2 * LANES), BF16)]
        + [pltpu.VMEM((4,) + wide_shape, BF16)] * 2
        + [pltpu.VMEM((CELLS, length, LANES), F32), pltpu.SemaphoreType.DMA((12,))],
        cost=8,
        held=tuple(range(7)),
        out_held=(0,),
        room=room,
        name="forward",
    )
    got = other_core(send)
    azimuth_ports, _ = lax.optimization_barrier((azimuth, send))
    (ports,) = call(
        functools.partial(pair_ports_kernel, total),
        [(11, half, LANES)],
        (lam, mu, helmholtz, azimuth_ports, vertical, radial),
        smem(2),
        cost=2,
        room=room,
        name="pair_ports",
    )
    line = (half, LANES)
    whole, out = call(
        functools.partial(merge_kernel, chips),
        [(2, half, LANES), line],
        (keep, got, ports),
        cost=0.3,
        room=room,
        name="merge",
    )

    out, azimuth_ratios = lax.optimization_barrier((out, azimuth))
    store_shape = (total, (5 if kept else 1) * quarter, LANES)
    edge_shape = (2, 5 * quarter, LANES)
    ratios_out = call(
        functools.partial(ratios_kernel, total, kept),
        [edge_shape] + ([store_shape] if kept else []),
        (lam_shared, mu, helmholtz, azimuth_ratios, vertical, radial),
        smem(2),
        [] if kept else [pltpu.VMEM(store_shape, F32)],
        cost=5,
        room=room,
        name="ratios",
    )
    edges, store = ratios_out[0], tuple(ratios_out[1:])
    scratch_store = [] if kept else [pltpu.VMEM(store_shape, F32)]
    (links,) = call(
        functools.partial(chain_links_kernel, chips),
        [(7, half, LANES)],
        (ports, edges),
        cost=0.5,
        room=room,
        name="links",
    )
    (response,) = call(
        functools.partial(response_kernel, total),
        [(2, total, LANES)],
        (lam_groups, weight_groups, mu_groups, helmholtz, azimuth_ratios, vertical, radial),
        smem(3),
        [
            pltpu.VMEM((total, 2 * quarter, LANES), F32),
            pltpu.VMEM((2, CELLS, total, 8, LANES), F32),
            pltpu.VMEM((2, CELLS, total, LANES), F32),
        ],
        cost=5,
        room=room,
        name="response",
    )
    (packed_ends,) = call(
        functools.partial(ends_kernel, total, kept),
        [(4, total, LANES)],
        (response, spectrum, lam, ends, mu) + scalars4 + store,
        smem(5),
        [pltpu.VMEM((2, total, 8, LANES), F32)] + scratch_store,
        cost=3,
        room=room,
        name="ends",
    )
    incoming = None
    whole_late, _ = lax.optimization_barrier((whole, packed_ends))
    for edge in range(chips // 2 - 1):
        moved = between_chips(out, [(edge, edge + 1), (chips - 1 - edge, chips - 2 - edge)])
        incoming = moved if incoming is None else incoming + moved
        (out,) = call(
            inward_kernel,
            [line],
            (whole_late, incoming, links),
            cost=0.3,
            room=room,
            name="inward",
        )

    def join(axis, bit, common, own, other):
        shape = (2 * own.shape[0] - common, total, LANES)
        (result,) = call(
            functools.partial(join_kernel, axis, bit, common),
            [shape],
            (own, other),
            cost=0.3,
            room=room,
            name="join",
        )
        return result

    gathered = packed_ends
    for bit in range(1, blocks.bit_length() - 1):
        moved = hop("rad", gathered, bit)
        gathered = join("rad", bit, 2, gathered, moved)
    gathered = join("rad", 0, 2, gathered, hop("rad", gathered, 0))
    matrix_shape = (total, total // SLABS, LANES)
    minus_matrix, alternate_matrix, plus_matrix = call(
        functools.partial(capacity_kernel, total),
        [matrix_shape] * 3,
        (azimuth, gathered),
        (0,),
        cost=4,
        room=room,
        name="capacity",
    )
    slab_ends = gathered[0:2]
    moved = hop("az", slab_ends, 0)
    slab_ends, _ = lax.optimization_barrier((slab_ends, minus_matrix))
    slab_ends = join("az", 0, 0, slab_ends, moved)
    middle_after = slab_ends
    azimuth_pair, _ = lax.optimization_barrier((azimuth, slab_ends))
    (pair_matrix,) = call(
        functools.partial(pair_kernel, total),
        [matrix_shape],
        (azimuth_pair, minus_matrix, plus_matrix),
        (0,),
        cost=3,
        room=room,
        name="pair",
    )
    moved = hop("az", slab_ends, 1)
    slab_ends, _ = lax.optimization_barrier((slab_ends, pair_matrix))
    slab_ends = join("az", 1, 0, slab_ends, moved)

    low, high = chips // 2 - 1, chips // 2
    other = between_chips(out, [(low, high), (high, low)])
    whole_last, _ = lax.optimization_barrier((whole, middle_after))
    near, far = call(
        functools.partial(middle_kernel, chips),
        [line, line],
        (whole_last, incoming, out, other, links),
        cost=0.3,
        room=room,
        name="middle",
    )
    passed = None
    for edge in range(chips // 2 - 2, -1, -1):
        moved = between_chips(far, [(edge + 1, edge), (chips - 2 - edge, chips - 1 - edge)])
        passed = moved if passed is None else passed + moved
        if edge > 0:
            (far,) = call(
                outward_kernel,
                [line],
                (whole, incoming, passed, links),
                cost=0.3,
                room=room,
                name="outward",
            )
    keep_sources, send_sources = call(
        functools.partial(slabs_kernel, total),
        [(SLABS, total, LANES)] * 2,
        (azimuth, minus_matrix, alternate_matrix, pair_matrix, slab_ends),
        (0,),
        [pltpu.VMEM((2 * SLABS, total, LANES), F32), pltpu.VMEM((8, total, LANES), F32)],
        cost=2,
        room=room,
        name="slabs",
    )
    moved = hop("az", send_sources, 1)
    keep_sources, send_sources = call(
        functools.partial(halve_kernel, "az", 0),
        [(2, total, LANES)] * 2,
        (keep_sources, moved),
        cost=0.3,
        room=room,
        name="halve",
    )
    whole_parts, _ = lax.optimization_barrier((whole, send_sources))
    own_sides, send_sides = call(
        functools.partial(parts_kernel, chips),
        [(2, half, LANES)] * 2,
        (keep, got, ports, links, whole_parts, incoming, near, passed),
        cost=0.4,
        room=room,
        name="parts",
    )
    got_sides = other_core(send_sides)
    sources = (keep_sources, hop("az", send_sources, 0))
    all_sources, extra = call(
        functools.partial(sides_kernel, total, kept),
        [(2, total, LANES), (2, length, LANES)],
        (lam, ends, mu) + scalars4 + sources + store,
        smem(3),
        scratch_store,
        cost=3,
        room=room,
        name="sides",
    )
    (pressure,) = call(
        functools.partial(backward_kernel, total),
        [(length * CELLS, LANES)],
        (
            spectrum,
            own_sides,
            got_sides,
            extra,
            all_sources,
            matrices(np.swapaxes(stage, 1, 2), basis.T),
            lam,
            ends,
            mu,
        )
        + scalars4,
        smem(9),
        [pltpu.VMEM((4,) + wide_shape, BF16)] * 2
        + [pltpu.VMEM((4,) + wide_shape, F32), pltpu.VMEM((length * CELLS, 2 * LANES), BF16)]
        + [pltpu.VMEM((length * CELLS, LANES), F32), pltpu.SemaphoreType.DMA((4,))],
        out_held=(0,),
        cost=7,
        room=room,
        name="backward",
    )
    return pressure.reshape(length, CELLS, LANES)


def solution(mesh):
    in_specs = (P("az", "rad", None), P(), P(), P(), P())
    return jax.shard_map(
        on_device,
        mesh=mesh,
        in_specs=in_specs,
        out_specs=P("az", "rad", None),
        check_vma=False,
    )
```

```python
import functools
import math

import jax
import jax.numpy as jnp
import ml_dtypes
import numpy as np
from jax import lax
from jax.experimental import pallas as pl
from jax.experimental.pallas import tpu as pltpu
from jax.sharding import PartitionSpec as P

F32 = jnp.float32
BF16 = jnp.bfloat16
CELLS = 4
SLABS = 4
LANES = 128


def two_halves(table):
    high = table.astype(np.float32).astype(ml_dtypes.bfloat16)
    low = (table - high.astype(np.float64)).astype(np.float32).astype(ml_dtypes.bfloat16)
    return high, low


def cosine_basis(depth):
    rows = np.arange(depth)
    phases = (2 * rows[:, None] + 1) * rows[None, :] % (4 * depth)
    scales = np.where(rows == 0, math.sqrt(1.0 / depth), math.sqrt(2.0 / depth))
    return np.cos(math.pi / (2 * depth) * phases) * scales[None, :]


def wide_basis(basis):
    high, low = two_halves(basis)
    top = np.concatenate([high, low], axis=1)
    bottom = np.concatenate([high, np.zeros_like(high)], axis=1)
    return np.concatenate([top, bottom], axis=0)


def slab_tables(length):
    quarter = length // 8
    half = quarter // 2
    offsets = np.arange(quarter) + 0.5
    stage = np.zeros((4, 2 * quarter, 2 * quarter))
    modes = np.zeros((4, 2 * quarter), np.int64)

    def angle(mode):
        return 2 * np.pi * (mode[:, None] * offsets[None, :] % length) / length

    def scale(mode):
        single = (mode == 0) | (mode == length // 2)
        return np.where(single, np.sqrt(1 / length), np.sqrt(2 / length))[:, None]

    steps = np.arange(half)
    for first, mode, column, wave in (
        (0, 8 * steps, 0, np.cos),
        (half, 8 * steps + 4, quarter, np.cos),
        (quarter, 8 * (steps + 1), 0, np.sin),
        (quarter + half, 8 * steps + 4, quarter, np.sin),
    ):
        stage[0, first : first + half, column : column + quarter] = scale(mode) * wave(angle(mode))
        modes[0, first : first + half] = mode
    for slot in (1, 2, 3):
        mode = slot + 8 * np.arange(quarter)
        cosine, sine = scale(mode) * np.cos(angle(mode)), scale(mode) * np.sin(angle(mode))
        stage[slot] = np.block([[cosine, sine], [sine, -cosine]])
        modes[slot] = np.concatenate([mode, mode])
    modes = modes.reshape(-1)
    parity = np.tile(np.repeat([1, -1], quarter), 4)
    single = (modes == 0) | (modes == length // 2)
    size = np.where(single, np.sqrt(1 / length), np.sqrt(2 / length))
    ends = size * np.where(parity > 0, np.cos(np.pi * modes / length), np.sin(np.pi * modes / length))
    eigen = 2.0 - 2.0 * np.cos(2 * np.pi * modes / length)
    return stage, eigen, ends, parity


def spread(column):
    return np.broadcast_to(column[..., None], column.shape + (LANES,)).astype(np.float32)


def split(values):
    high = values.astype(BF16)
    low = (values - high.astype(F32)).astype(BF16)
    return high, low


def dot(left, right):
    return jnp.dot(left, right, preferred_element_type=F32)


def times_basis(values, wide):
    high, low = split(values)
    both = dot(jnp.concatenate([high, low], axis=1), wide)
    depth = values.shape[1]
    return both[:, :depth] + both[:, depth:]


class Radial:
    def __init__(self, helmholtz, azimuth, vertical, radial, total):
        self.refs = (helmholtz, azimuth, vertical, radial)
        self.total = total

    def coupling(self, cell):
        cell = jnp.asarray(cell, jnp.int32)
        return jnp.where(cell < self.total - 1, self.refs[3][cell], 0.0)

    def previous(self, cell):
        cell = jnp.asarray(cell, jnp.int32)
        return jnp.where(cell > 0, self.refs[3][jnp.maximum(cell - 1, 0)], 0.0)

    def diagonal(self, cell, lam, mu):
        base = self.refs[0][cell] + self.coupling(cell) + self.previous(cell)
        return lam * self.refs[1][cell] + (mu * self.refs[2][cell] + base)


def inverse(values):
    return pl.reciprocal(values, approx=False)


def solve_block(radial, first, lam, mu, right, add_first=None, add_last=None):
    rows = []
    factor = values = None
    for place in range(CELLS):
        cell = first + place
        diagonal = radial.diagonal(cell, lam, mu)
        if place == 0 and add_first is not None:
            diagonal = diagonal - add_first
        if place == CELLS - 1 and add_last is not None:
            diagonal = diagonal - add_last
        if place > 0:
            before = radial.previous(cell)
            pivot = inverse(diagonal - before * factor)
            values = (right[place] + before * values) * pivot
        else:
            pivot = inverse(diagonal)
            values = right[place] * pivot
        factor = radial.coupling(cell) * pivot
        rows.append((values, factor))
    answer = [rows[-1][0]]
    for values, factor in rows[-2::-1]:
        answer.insert(0, values + factor * answer[0])
    return answer


def block_ports(radial, first, lam, mu):
    diagonals = [radial.diagonal(first + place, lam, mu) for place in range(CELLS)]
    pivot = inverse(diagonals[0])
    forward = [pivot]
    for place in range(1, CELLS):
        before = radial.previous(first + place)
        pivot = inverse(diagonals[place] - before * before * pivot)
        forward.append(pivot)
    last = forward[-1]
    cross = last
    for place in range(CELLS - 2, -1, -1):
        cross = radial.coupling(first + place) * forward[place] * cross
    backward = inverse(diagonals[-1])
    for place in range(CELLS - 2, -1, -1):
        after = radial.coupling(first + place)
        backward = inverse(diagonals[place] - after * after * backward)
    entry, leave = radial.previous(first), radial.coupling(first + CELLS - 1)
    return backward * entry, cross * leave, cross * entry, last * leave


def chip_ports(radial, first, lam, mu):
    b1, g1, b2, g2 = block_ports(radial, first, lam, mu)
    c1, h1, c2, h2 = block_ports(radial, first + CELLS, lam, mu)
    mid = inverse(1.0 - g2 * c1)
    low = c1 * b2 * mid
    high = h1 * mid
    whole = (
        b1 + g1 * low,
        g1 * high,
        c2 * (b2 + g2 * low),
        h2 + c2 * g2 * high,
    )
    return (b1, g1, b2, g2), (c1, h1, c2, h2), mid, whole


def spread_parts(x):
    root = math.sqrt(0.5)
    s = [x[n] + x[n + 4] for n in range(4)]
    d = [x[n] - x[n + 4] for n in range(4)]
    even, odd = s[0] + s[2], s[1] + s[3]
    minus, plus = root * (d[1] - d[3]), root * (d[1] + d[3])
    return (
        even + odd,
        even - odd,
        d[0] + minus,
        -plus - d[2],
        s[0] - s[2],
        s[3] - s[1],
        d[0] - minus,
        d[2] - plus,
    )


def gather_parts(y):
    root = math.sqrt(0.5)
    plus, minus = y[0] + y[1], y[0] - y[1]
    s = (plus + y[4], minus - y[5], plus - y[4], minus + y[5])
    real, imag = root * (y[2] - y[6]), root * (y[3] + y[7])
    d = (y[2] + y[6], real - imag, y[7] - y[3], -real - imag)
    return [s[n] + d[n] for n in range(4)] + [s[n] - d[n] for n in range(4)]


def forward_kernel(total, source_in, tables_in, stages_in, *rest):
    scalars_in = rest[:4]
    spectrum_out, keep, send = rest[4:7]
    source, tables, stages, s0, s1, s2, s3, wide_rows, high, low, spectrum, sems = rest[7:]
    scalars = (s0, s1, s2, s3)
    length = source.shape[0] * source.shape[1] // CELLS
    quarter = length // 8
    eighth = quarter * CELLS
    pairs = []
    for part in range(2):
        rows = pl.ds(part * eighth // 2, eighth // 2)
        pairs.append((source_in.at[:, rows, :], source.at[:, rows, :]))
    pairs += [(stages_in, stages), (tables_in, tables)]
    pairs += list(zip(scalars_in, scalars))
    copies = [
        pltpu.make_async_copy(origin, target, sems.at[place])
        for place, (origin, target) in enumerate(pairs)
    ]
    for copy in copies:
        copy.start()
    radial = Radial(*scalars, total)
    core = lax.rem(lax.axis_index("rad"), 2)
    first = lax.axis_index("rad") * CELLS
    chunk = 16
    for start in range(0, quarter, chunk):
        if start * 2 % quarter == 0:
            copies[start * 2 // quarter].wait()
        for cell in range(CELLS):
            x = [
                source[n, pl.ds(start * CELLS + cell, chunk, stride=CELLS), :] for n in range(8)
            ]
            for place, part in enumerate(spread_parts(x)):
                one, two = split(part)
                row = cell * length + place * quarter + start
                wide_rows[row : row + chunk, :LANES] = one
                wide_rows[row : row + chunk, LANES:] = two
    copies[2].wait()
    wide = stages[8 * 2 * quarter : 8 * 2 * quarter + 2 * LANES, :]
    for cell in range(CELLS):
        for slot in range(4):
            row = cell * length + slot * 2 * quarter
            both = dot(wide_rows[row : row + 2 * quarter, :], wide)
            one, two = split(both[:, :LANES] + both[:, LANES:])
            columns = slice(cell * LANES, (cell + 1) * LANES)
            high[slot, :, columns] = one
            low[slot, :, columns] = two
    leaving = []
    for slot in range(4):
        upper = stages[slot * 2 * quarter : (slot + 1) * 2 * quarter, :]
        lower = stages[(4 + slot) * 2 * quarter : (5 + slot) * 2 * quarter, :]
        result = dot(upper, high[slot]) + dot(upper, low[slot]) + dot(lower, high[slot])
        for cell in range(CELLS):
            spectrum[cell, slot * 2 * quarter : (slot + 1) * 2 * quarter, :] = result[
                :, cell * LANES : (cell + 1) * LANES
            ]
        rows = pl.ds(slot * 2 * quarter, 2 * quarter)
        leaving.append(
            pltpu.make_async_copy(
                spectrum.at[:, rows, :], spectrum_out.at[:, rows, :], sems.at[8 + slot]
            )
        )
        leaving[-1].start()
    for copy in copies[3:]:
        copy.wait()
    chunk = 64
    half = length // 2
    level = tables[length : length + 1, :]

    def step(index, _):
        ends = []
        for part in range(2):
            rows = pl.ds(part * half + index * chunk, chunk)
            right = [spectrum[cell, rows, :] for cell in range(CELLS)]
            answer = solve_block(radial, first, tables[rows, :], level, right)
            ends.append((answer[0], answer[-1]))
        rows = pl.ds(index * chunk, chunk)
        for place in range(2):
            keep[place, rows, :] = jnp.where(core == 0, ends[0][place], ends[1][place])
            send[place, rows, :] = jnp.where(core == 0, ends[1][place], ends[0][place])
        return 0

    for index in range(half // chunk):
        step(index, 0)
    for copy in leaving:
        copy.wait()


def shared_row(slot, kind, quarter):
    return pl.multiple_of(jnp.where(slot == 0, kind, slot + 1) * quarter, quarter)


def pair_ports_kernel(total, lam, mu, *rest):
    radial = Radial(*rest[:4], total)
    (out,) = rest[4:]
    half = out.shape[1]
    quarter = half // 4
    chips = total // (2 * CELLS)
    core = lax.rem(lax.axis_index("rad"), 2)
    chip = lax.axis_index("rad") // 2
    left_side = chip < chips // 2
    first = chip * (2 * CELLS)
    level = mu[...][:1]
    chunk = min(64, quarter)

    def step(index, _):
        rows = pl.ds(pl.multiple_of(index * chunk, chunk), chunk)
        spot = pl.ds(pl.multiple_of(core * half + index * chunk, chunk), chunk)
        (b1, g1, b2, g2), (c1, h1, c2, h2), mid, (w1, w2, w3, w4) = chip_ports(
            radial, first, lam[spot, :], level
        )
        rff, rnn = jnp.where(left_side, w1, w4), jnp.where(left_side, w4, w1)
        rfn, rnf = jnp.where(left_side, w2, w3), jnp.where(left_side, w3, w2)
        for place, value in enumerate((g1, b2, g2, c1, h1, c2, mid, rff, rfn, rnf, rnn)):
            out[place, rows, :] = value
        return 0

    lax.fori_loop(0, half // chunk, step, 0)


def chain_links_kernel(chips, ports, edges, out):
    half = out.shape[1]
    quarter = half // 4
    core = lax.rem(lax.axis_index("rad"), 2)
    left_side = lax.axis_index("rad") // 2 < chips // 2
    chunk = min(64, quarter)

    def step(index, _):
        rows = pl.ds(pl.multiple_of(index * chunk, chunk), chunk)
        block = index * chunk // quarter
        start = shared_row(core * 2 + block // 2, lax.rem(block, 2), quarter)
        spot = pl.ds(pl.multiple_of(start + lax.rem(index * chunk, quarter), chunk), chunk)
        rff, rfn, rnf, rnn = (ports[7 + place, rows, :] for place in range(4))
        left, right = edges[0, spot, :], edges[1, spot, :]
        far, near = jnp.where(left_side, left, right), jnp.where(left_side, right, left)
        pivot = inverse(1.0 - rff * far)
        onward = rnn + rnf * far * rfn * pivot
        for place, value in enumerate(
            (rff, pivot, rfn * pivot, rnf, far, near, inverse(1.0 - near * onward))
        ):
            out[place, rows, :] = value
        return 0

    lax.fori_loop(0, half // chunk, step, 0)


def merge_kernel(chips, keep, got, ports, whole, out):
    half = keep.shape[1]
    core = lax.rem(lax.axis_index("rad"), 2)
    left_side = lax.axis_index("rad") // 2 < chips // 2
    chunk = 32

    def step(index, _):
        rows = pl.ds(pl.multiple_of(index * chunk, chunk), chunk)
        g1, b2, g2, c1, h1, c2, mid = (ports[place, rows, :] for place in range(7))
        mine = [keep[place, rows, :] for place in range(2)]
        other = [got[place, rows, :] for place in range(2)]
        low = [jnp.where(core == 0, m, o) for m, o in zip(mine, other)]
        high = [jnp.where(core == 0, o, m) for m, o in zip(mine, other)]
        upper = (high[0] + c1 * low[1]) * mid
        first = low[0] + g1 * upper
        last = high[1] + c2 * (low[1] + g2 * upper)
        near = jnp.where(left_side, last, first)
        whole[0, rows, :] = jnp.where(left_side, first, last)
        whole[1, rows, :] = near
        out[rows, :] = near
        return 0

    lax.fori_loop(0, half // chunk, step, 0)


def inward_kernel(whole, incoming, links, out):
    half = out.shape[0]
    chunk = 32

    def step(index, _):
        rows = pl.ds(pl.multiple_of(index * chunk, chunk), chunk)
        rff, pivot, _rfn, rnf, far = (links[place, rows, :] for place in range(5))
        value = incoming[rows, :]
        origin = (whole[0, rows, :] + rff * value) * pivot
        out[rows, :] = whole[1, rows, :] + rnf * (value + far * origin)
        return 0

    lax.fori_loop(0, half // chunk, step, 0)


def middle_kernel(chips, whole, incoming, own, other, links, near_out, far_out):
    half = far_out.shape[0]
    chip = lax.axis_index("rad") // 2
    inner = (chip == chips // 2) | (chip == chips // 2 - 1)
    chunk = 32

    def step(index, _):
        rows = pl.ds(pl.multiple_of(index * chunk, chunk), chunk)
        rff, pivot, hold, _rnf, _far, near, close = (
            links[place, rows, :] for place in range(7)
        )
        value = (other[rows, :] + near * own[rows, :]) * close
        value = jnp.where(inner, value, 0.0)
        origin = (whole[0, rows, :] + rff * incoming[rows, :]) * pivot
        near_out[rows, :] = value
        far_out[rows, :] = origin + hold * value
        return 0

    lax.fori_loop(0, half // chunk, step, 0)


def outward_kernel(whole, incoming, near_in, links, far_out):
    half = far_out.shape[0]
    chunk = 32

    def step(index, _):
        rows = pl.ds(pl.multiple_of(index * chunk, chunk), chunk)
        rff, pivot, hold = (links[place, rows, :] for place in range(3))
        origin = (whole[0, rows, :] + rff * incoming[rows, :]) * pivot
        far_out[rows, :] = origin + hold * near_in[rows, :]
        return 0

    lax.fori_loop(0, half // chunk, step, 0)


def parts_kernel(chips, keep, got, ports, links, whole, incoming, near_one, near_two, own, send):
    half = keep.shape[1]
    core = lax.rem(lax.axis_index("rad"), 2)
    left_side = lax.axis_index("rad") // 2 < chips // 2
    chunk = 32

    def step(index, _):
        rows = pl.ds(pl.multiple_of(index * chunk, chunk), chunk)
        _g1, b2, g2, c1, h1, _c2, mid = (ports[place, rows, :] for place in range(7))
        rff, pivot, hold, _rnf, far = (links[place, rows, :] for place in range(5))
        near = near_one[rows, :] + near_two[rows, :]
        value = incoming[rows, :]
        outer = value + far * ((whole[0, rows, :] + rff * value) * pivot + hold * near)
        left, right = jnp.where(left_side, outer, near), jnp.where(left_side, near, outer)
        last = jnp.where(core == 0, keep[1, rows, :], got[1, rows, :]) + b2 * left
        opening = jnp.where(core == 0, got[0, rows, :], keep[0, rows, :]) + h1 * right
        upper = (opening + c1 * last) * mid
        lower = last + g2 * upper
        own[0, rows, :] = jnp.where(core == 0, left, lower)
        own[1, rows, :] = jnp.where(core == 0, upper, right)
        send[0, rows, :] = jnp.where(core == 0, lower, left)
        send[1, rows, :] = jnp.where(core == 0, right, upper)
        return 0

    lax.fori_loop(0, half // chunk, step, 0)


def fold_rows(values):
    parts = [values[start : start + 8] for start in range(0, values.shape[0], 8)]
    while len(parts) > 1:
        parts = [a + b for a, b in zip(parts[::2], parts[1::2])]
    return parts[0]


def by_blocks(count, body, carry):
    def block(index, carry):
        for place in range(CELLS):
            carry = body(index * CELLS + place, carry)
        return carry

    return lax.fori_loop(0, lax.div(count, CELLS), block, carry)


def ratios(radial, first, lam, mu, left_store, right_store):
    total = radial.total
    shape = lam.shape

    def leftward(cell, factor):
        pivot = inverse(radial.diagonal(cell, lam, mu) - radial.previous(cell) * factor)
        factor = radial.coupling(cell) * pivot
        left_store[cell] = factor
        return factor

    def rightward(step, factor):
        cell = total - 1 - step
        pivot = inverse(radial.diagonal(cell, lam, mu) - radial.coupling(cell) * factor)
        factor = radial.previous(cell) * pivot
        right_store[cell] = factor
        return factor

    zero = jnp.zeros(shape, F32)
    left = by_blocks(first, leftward, zero)
    right = by_blocks(total - CELLS - first, rightward, zero)
    return left, right


def ratios_kernel(total, kept, lam, mu, *rest):
    radial = Radial(*rest[:4], total)
    edges, store = rest[4:]
    first = lax.axis_index("rad") * CELLS
    opening = lax.axis_index("rad") // 2 * (2 * CELLS)
    level = mu[...][:1]
    chunk = lam.shape[0] // (2 if kept else 5)

    def step(index, _):
        rows = pl.ds(pl.multiple_of(index * chunk, chunk), chunk)
        view = store.at[:, rows, :] if kept else store
        ratios(radial, first, lam[rows, :], level, view, view)
        left = view[jnp.maximum(opening - 1, 0)]
        right = view[jnp.minimum(opening + 2 * CELLS, total - 1)]
        edges[0, rows, :] = jnp.where(opening > 0, left, 0.0)
        edges[1, rows, :] = jnp.where(opening + 2 * CELLS < total, right, 0.0)
        return 0

    lax.fori_loop(0, lam.shape[0] // chunk, step, 0)


def outside(view, first, total):
    left = jnp.where(first > 0, view[jnp.maximum(first - 1, 0)], 0.0)
    right = view[jnp.minimum(first + CELLS, total - 1)]
    return left, jnp.where(first + CELLS < total, right, 0.0)


def stored_view(store, index, chunk):
    start = shared_row(index // 2, lax.rem(index, 2), chunk)
    return store.at[:, pl.ds(start, chunk), :]


def ends_kernel(total, kept, response, spectrum, lam, ends, mu, *rest):
    radial = Radial(*rest[:4], total)
    if kept:
        store, out, sums = rest[4:]
    else:
        out, sums, store = rest[4:]
    first = lax.axis_index("rad") * CELLS
    level = mu[...][:1]
    chunk = spectrum.shape[1] // 8
    sums[...] = jnp.zeros_like(sums)

    def start(kind, index, view, left, right):
        rows = pl.ds(pl.multiple_of(index * chunk, chunk), chunk)
        weight = 2.0 * ends[rows, :]
        answer = solve_block(
            radial,
            first,
            lam[rows, :],
            level,
            [weight * spectrum[cell, rows, :] for cell in range(CELLS)],
            radial.previous(first) * left,
            radial.coupling(first + CELLS - 1) * right,
        )
        for place in range(CELLS):
            sums[kind, first + place] += fold_rows(answer[place])
        return answer

    def spread_out(kinds, views, answers):
        def onward(cell, values):
            values = [view[cell] * value for view, value in zip(views, values)]
            for kind, value in zip(kinds, values):
                sums[kind, cell] += fold_rows(value)
            return tuple(values)

        by_blocks(
            first,
            lambda move, values: onward(first - 1 - move, values),
            tuple(answer[0] for answer in answers),
        )
        by_blocks(
            total - CELLS - first,
            lambda move, values: onward(first + CELLS + move, values),
            tuple(answer[-1] for answer in answers),
        )

    if kept:

        def step(slot, _):
            views = [stored_view(store, 2 * slot + kind, chunk) for kind in range(2)]
            answers = [
                start(kind, 2 * slot + kind, views[kind], *outside(views[kind], first, total))
                for kind in range(2)
            ]
            spread_out((0, 1), views, answers)
            return 0

        lax.fori_loop(0, 4, step, 0)
    else:

        def step(index, _):
            kind = lax.rem(index, 2)
            rows = pl.ds(pl.multiple_of(index * chunk, chunk), chunk)
            left, right = ratios(radial, first, lam[rows, :], level, store, store)
            spread_out((kind,), (store,), [start(kind, index, store, left, right)])
            return 0

        lax.fori_loop(0, 8, step, 0)
    for kind in range(2):
        for cell in range(total):
            out[kind, cell : cell + 1, :] = jnp.sum(sums[kind, cell], axis=0, keepdims=True)
    out[2:4] = response[...]


def join_kernel(axis, bit, common, own, other, out):
    high = lax.rem(lax.div(lax.axis_index(axis), 1 << bit), 2)
    count = own.shape[0] - common
    if common:
        out[0:common] = own[0:common] + other[0:common]
    out[pl.ds(common + high * count, count)] = own[common:]
    out[pl.ds(common + (1 - high) * count, count)] = other[common:]


def halve_kernel(axis, bit, own, other, keep, send):
    high = lax.rem(lax.div(lax.axis_index(axis), 1 << bit), 2)
    count = keep.shape[0]
    keep[...] = own[pl.ds(high * count, count)] + other[pl.ds(high * count, count)]
    there = pl.ds((1 - high) * count, count)
    send[...] = own[there] + other[there]


def response_kernel(total, lam, weight, mu, *rest):
    radial = Radial(*rest[:4], total)
    out, store, sums, lines = rest[4:]
    first = lax.axis_index("rad") * CELLS
    level = mu[pl.ds(lax.axis_index("az"), 1), :]
    group = LANES // SLABS
    chunk = lam.shape[0] // 2
    sums[...] = jnp.zeros_like(sums)
    lefts, rights = ratios(radial, first, lam[...], level, store, store)

    for kind in range(2):
        rows = slice(kind * chunk, (kind + 1) * chunk)
        source = weight[rows, :]
        zero = jnp.zeros_like(source)
        openings, closings = [], []
        for place in range(CELLS):
            answer = solve_block(
                radial,
                first,
                lam[rows, :],
                level,
                [source if cell == place else zero for cell in range(CELLS)],
                radial.previous(first) * lefts[rows],
                radial.coupling(first + CELLS - 1) * rights[rows],
            )
            for cell in range(CELLS):
                sums[kind, place, first + cell] += fold_rows(answer[cell])
            openings.append(answer[0])
            closings.append(answer[-1])

        def outward(cell, factor, edges):
            factor = store[cell, rows, :] * factor
            for place in range(CELLS):
                sums[kind, place, cell] += fold_rows(factor * edges[place])
            return factor

        one = jnp.ones_like(source)
        by_blocks(first, lambda move, factor: outward(first - 1 - move, factor, openings), one)
        by_blocks(
            total - CELLS - first,
            lambda move, factor: outward(first + CELLS + move, factor, closings),
            one,
        )

    lane = lax.broadcasted_iota(jnp.int32, (1, LANES), 1) // group

    def close(cell, _):
        for kind in range(2):
            for place in range(CELLS):
                lines[kind, place, pl.ds(cell, 1), :] = jnp.sum(
                    sums[kind, place, cell], axis=0, keepdims=True
                )
        return 0

    lax.fori_loop(0, total, close, 0, unroll=8)
    for kind in range(2):
        result = jnp.zeros((total, LANES), F32)
        for place in range(CELLS):
            line = lines[kind, place]
            line = line + pltpu.roll(line, 2 * group, 1)
            line = line + pltpu.roll(line, group, 1)
            result = jnp.where(lane == place, line, result)
        out[kind] = result


def lane_groups():
    return lax.broadcasted_iota(jnp.int32, (1, LANES), 1) // (LANES // SLABS)


def to_all_groups(values, group):
    width = LANES // SLABS
    values = jnp.where(lane_groups() == group, values, 0.0)
    values = values + pltpu.roll(values, 2 * width, 1)
    return values + pltpu.roll(values, width, 1)


def fold_cells(values):
    width = values.shape[0] // SLABS
    result = values[:width]
    for group in range(1, SLABS):
        part = values[group * width : (group + 1) * width]
        result = jnp.where(lane_groups() == group, part, result)
    return result


def unfold_cells(values):
    return jnp.concatenate([to_all_groups(values, group) for group in range(SLABS)])


def invert(matrices, total):
    width = total // SLABS
    step_size = 8
    rows = lax.broadcasted_iota(jnp.int32, (width, LANES), 0)
    cells = rows + lane_groups() * width

    def step(panel, _):
        base = pl.multiple_of(panel * step_size, step_size)
        group = lax.div(base, width)
        spot_rows = pl.ds(pl.multiple_of(lax.rem(base, width), step_size), step_size)
        inside = (cells >= base) & (cells < base + step_size)
        state = []
        for matrix in matrices:
            lines = [matrix[base + place] for place in range(step_size)]
            corners = [
                to_all_groups(matrix[base + place, spot_rows, :], group)
                for place in range(step_size)
            ]
            state.append((lines, corners))
        for place in range(step_size):
            mark = cells == base + place
            spot = lax.broadcasted_iota(jnp.int32, (step_size, LANES), 0) == place
            for lines, corners in state:
                scale = inverse(corners[place][place : place + 1])
                line = jnp.where(mark, 1.0, lines[place]) * scale
                corner = jnp.where(spot, 1.0, corners[place]) * scale
                for row in range(step_size):
                    if row == place:
                        continue
                    factor = corners[row][place : place + 1]
                    lines[row] = jnp.where(mark, 0.0, lines[row]) - factor * line
                    corners[row] = jnp.where(spot, 0.0, corners[row]) - factor * corner
                lines[place], corners[place] = line, corner

        batch = 32

        def update(index, _):
            for matrix, (lines, _corners) in zip(matrices, state):
                spots = [index * batch + place for place in range(batch)]
                corners = [to_all_groups(matrix[spot, spot_rows, :], group) for spot in spots]
                values = [jnp.where(inside, 0.0, matrix[spot]) for spot in spots]
                for place in range(step_size):
                    values = [
                        value - corner[place : place + 1] * lines[place]
                        for value, corner in zip(values, corners)
                    ]
                for spot, value in zip(spots, values):
                    matrix[spot] = value
            return 0

        lax.fori_loop(0, total // batch, update, 0)
        for matrix, (lines, _corners) in zip(matrices, state):
            for place in range(step_size):
                matrix[base + place] = lines[place]
        return 0

    lax.fori_loop(0, total // step_size, step, 0)


def per_cell(total, azimuth, top):
    width = total // SLABS
    cells = lax.broadcasted_iota(jnp.int32, (width, LANES), 0) + lane_groups() * width

    def column(cell, value):
        return jnp.where(cells == cell, azimuth[cell], value)

    return top * inverse(lax.fori_loop(0, total, column, jnp.ones((width, LANES), F32), unroll=8))


def capacity_kernel(total, azimuth, responses, *outs):
    minus_out, alternate_out, pair_out = outs
    chips = total // (2 * CELLS)
    width = total // SLABS
    shift = LANES // SLABS
    lane = lane_groups()
    cells = lax.broadcasted_iota(jnp.int32, (width, LANES), 0) + lane * width
    half = per_cell(total, azimuth, 0.5)
    for block in range(2 * chips):
        start = 2 + 2 * (block % 2 * chips + block // 2)
        for kind in range(2):
            parts = [
                responses[start + kind, group * width : (group + 1) * width, :]
                for group in range(SLABS)
            ]
            for place in range(CELLS):
                row = jnp.zeros((width, LANES), F32)
                for group, part in enumerate(parts):
                    turn = (group - place) % SLABS
                    part = pltpu.roll(part, turn * shift, 1) if turn else part
                    row = jnp.where(lane == group, part, row)
                cell = block * CELLS + place
                own = jnp.where(cells == cell, half, 0.0)
                if kind == 0:
                    alternate_out[cell] = own + row
                    pair_out[cell] = own + row
                else:
                    minus_out[cell] = own - row
    invert([minus_out, alternate_out], total)


def pair_kernel(total, azimuth, minus_matrix, plus_matrix, pair_out):
    scale = per_cell(total, azimuth, 0.25)

    def add(cell, _):
        own = inverse(jnp.full((1, LANES), azimuth[cell], F32))
        pair_out[cell] = plus_matrix[cell] + minus_matrix[cell] * (scale * own)
        return 0

    lax.fori_loop(0, total, add, 0, unroll=8)
    invert([pair_out], total)


def apply_matrix(matrix, store, slots):
    total = matrix.shape[0]
    results = [[None] * 4 for _ in slots]
    for cell in range(total):
        line = matrix[cell]
        for place, slot in enumerate(slots):
            term = line * store[slot, cell : cell + 1, :]
            before = results[place][cell % 4]
            results[place][cell % 4] = term if before is None else before + term
    return [(r[0] + r[1]) + (r[2] + r[3]) for r in results]


def slabs_kernel(total, azimuth, minus_matrix, alternate_matrix, pair_matrix, *rest):
    values, keep, send, results, store = rest
    slab = lax.axis_index("az")
    width = total // SLABS
    shift = LANES // SLABS
    lane = lane_groups()

    def channels(kind):
        u = [values[2 * place + kind] for place in range(SLABS)]
        mixed = (u[0] - u[2], u[3] - u[1], (u[0] + u[2]) - (u[1] + u[3]))
        return [to_all_groups(value, slab) for value in mixed]

    sums, differences = channels(0), channels(1)
    half = per_cell(total, azimuth, 0.5)
    for place in range(3):
        store[place] = differences[place]
    store[3] = -sums[2]
    lead_real, lead_imag, minus_alternate = apply_matrix(minus_matrix, store, (0, 1, 2))
    (plus_alternate,) = apply_matrix(alternate_matrix, store, (3,))
    store[4] = unfold_cells(-half * lead_imag - fold_cells(sums[0]))
    store[5] = unfold_cells(half * lead_real - fold_cells(sums[1]))
    plus_real, plus_imag = apply_matrix(pair_matrix, store, (4, 5))
    store[6] = unfold_cells(-half * plus_imag)
    store[7] = unfold_cells(half * plus_real)
    more_real, more_imag = apply_matrix(minus_matrix, store, (6, 7))
    found = (
        (plus_real, plus_imag, plus_alternate),
        (lead_real + more_real, lead_imag + more_imag, minus_alternate),
    )
    for kind, (real, imag, alternate) in enumerate(found):
        folded = (
            0.25 * (2.0 * real + alternate),
            0.25 * (-2.0 * imag - alternate),
            0.25 * (alternate - 2.0 * real),
            0.25 * (2.0 * imag - alternate),
        )
        for place, value in enumerate(folded):
            for group in range(SLABS):
                turn = lax.rem(slab - group + SLABS, SLABS) * shift
                rows = slice(group * width, (group + 1) * width)
                results[2 * place + kind, rows, :] = jnp.where(
                    lane == slab, pltpu.roll(value, turn, 1), 0.0
                )
    high = lax.div(slab, SLABS // 2)
    keep[...] = results[pl.ds(high * SLABS, SLABS)]
    send[...] = results[pl.ds((1 - high) * SLABS, SLABS)]


def sides_kernel(total, kept, lam, ends, mu, *rest):
    radial = Radial(*rest[:4], total)
    own_part, other_part = rest[4:6]
    if kept:
        store, sources, out = rest[6:]
    else:
        sources, out, store = rest[6:]
    sources[...] = own_part[...] + other_part[...]
    first = lax.axis_index("rad") * CELLS
    level = mu[...][:1]
    chunk = lam.shape[0] // 8
    entry, leave = radial.previous(first), radial.coupling(first + CELLS - 1)

    def inflow(kinds, views):
        zeros = tuple(jnp.zeros((chunk, LANES), F32) for _ in kinds)

        def passed(cell, values):
            return tuple(
                view[cell] * (sources[kind, pl.ds(cell, 1), :] + value)
                for kind, view, value in zip(kinds, views, values)
            )

        from_left = by_blocks(first, passed, zeros)
        from_right = by_blocks(
            total - CELLS - first,
            lambda move, values: passed(total - 1 - move, values),
            zeros,
        )
        return from_left, from_right

    def finish(kind, index, left, right, from_left, from_right):
        rows = pl.ds(pl.multiple_of(index * chunk, chunk), chunk)
        own = [sources[kind, pl.ds(first + place, 1), :] for place in range(CELLS)]
        own[0] = own[0] + from_left
        own[-1] = own[-1] + from_right
        answer = solve_block(radial, first, lam[rows, :], level, own, entry * left, leave * right)
        weight = ends[rows, :]
        out[0, rows, :] = weight * (from_left + entry * left * answer[0])
        out[1, rows, :] = weight * (from_right + leave * right * answer[-1])

    if kept:

        def step(slot, _):
            views = [stored_view(store, 2 * slot + kind, chunk) for kind in range(2)]
            from_left, from_right = inflow((0, 1), views)
            for kind, view in enumerate(views):
                left, right = outside(view, first, total)
                finish(kind, 2 * slot + kind, left, right, from_left[kind], from_right[kind])
            return 0

        lax.fori_loop(0, 4, step, 0)
    else:

        def step(index, _):
            kind = lax.rem(index, 2)
            rows = pl.ds(pl.multiple_of(index * chunk, chunk), chunk)
            left, right = ratios(radial, first, lam[rows, :], level, store, store)
            from_left, from_right = inflow((kind,), (store,))
            finish(kind, index, left, right, from_left[0], from_right[0])
            return 0

        lax.fori_loop(0, 8, step, 0)


def backward_kernel(total, spectrum, own, got, extra, sources, stages, lam, ends, mu, *rest):
    radial = Radial(*rest[:4], total)
    out, high, low, middle, wide_rows, field, sems = rest[4:]
    length = spectrum.shape[1]
    quarter = length // 8
    core = lax.rem(lax.axis_index("rad"), 2)
    first = lax.axis_index("rad") * CELLS
    level = mu[...][:1]
    chunk = min(64, quarter)
    entry, leave = radial.previous(first), radial.coupling(first + CELLS - 1)

    for slot in range(4):

        def step(index, _):
            kind = index // (quarter // chunk)
            spot = pl.ds(index * chunk, chunk)
            rows = pl.ds(slot * 2 * quarter + index * chunk, chunk)
            near = pl.ds(slot % 2 * 2 * quarter + index * chunk, chunk)
            mine = core == slot // 2
            side = [jnp.where(mine, own[place, near, :], got[place, near, :]) for place in range(2)]
            weight = ends[rows, :]
            right = [
                spectrum[cell, rows, :] + weight * sources[kind, pl.ds(first + cell, 1), :]
                for cell in range(CELLS)
            ]
            right[0] = right[0] + (entry * side[0] + extra[0, rows, :])
            right[-1] = right[-1] + (leave * side[1] + extra[1, rows, :])
            answer = solve_block(radial, first, lam[rows, :], level, right)
            for cell in range(CELLS):
                one, two = split(answer[cell])
                columns = slice(cell * LANES, (cell + 1) * LANES)
                high[slot, spot, columns] = one
                low[slot, spot, columns] = two
            return 0

        for index in range(2 * quarter // chunk):
            step(index, 0)
        upper = stages[slot * 2 * quarter : (slot + 1) * 2 * quarter, :]
        lower = stages[(4 + slot) * 2 * quarter : (5 + slot) * 2 * quarter, :]
        middle[slot] = dot(upper, high[slot]) + dot(upper, low[slot]) + dot(lower, high[slot])
    chunk = 16
    wide = stages[8 * 2 * quarter : 8 * 2 * quarter + 2 * LANES, :]
    for cell in range(CELLS):
        columns = slice(cell * LANES, (cell + 1) * LANES)
        for start in range(0, quarter, chunk):
            y = [
                middle[place // 2, pl.ds(place % 2 * quarter + start, chunk), columns]
                for place in range(8)
            ]
            for place, value in enumerate(gather_parts(y)):
                one, two = split(value)
                row = cell * length + place * quarter + start
                wide_rows[row : row + chunk, :LANES] = one
                wide_rows[row : row + chunk, LANES:] = two
    copies = []
    for part in range(4):
        start = part * 2 * quarter
        for cell in range(CELLS):
            row = cell * length + start
            both = dot(wide_rows[row : row + 2 * quarter, :], wide)
            field[pl.ds(start * CELLS + cell, 2 * quarter, stride=CELLS), :] = (
                both[:, :LANES] + both[:, LANES:]
            )
        rows = pl.ds(start * CELLS, 2 * quarter * CELLS)
        copies.append(pltpu.make_async_copy(field.at[rows], out.at[rows], sems.at[part]))
        copies[-1].start()
    for copy in copies:
        copy.wait()


def call(kernel, out_shapes, args, scalars=(), scratch=(), cost=1, room=20, held=(), out_held=(), name=None):
    specs = []
    for place in range(len(args)):
        space = pltpu.SMEM if place in scalars else pltpu.HBM if place in held else pltpu.VMEM
        specs.append(pl.BlockSpec(memory_space=space))
    outs = [
        (pltpu.HBM if place in out_held else jax.ShapeDtypeStruct)(shape, F32)
        for place, shape in enumerate(out_shapes)
    ]
    args = [
        pltpu.with_memory_space_constraint(arg, pltpu.HBM) if place in held else arg
        for place, arg in enumerate(args)
    ]
    return pl.pallas_call(
        kernel,
        out_shape=outs,
        in_specs=specs,
        out_specs=[
            pl.BlockSpec(memory_space=pltpu.HBM if place in out_held else pltpu.VMEM)
            for place in range(len(outs))
        ],
        scratch_shapes=list(scratch),
        compiler_params=pltpu.CompilerParams(vmem_limit_bytes=room * 2**20),
        cost_estimate=pl.CostEstimate(
            flops=0, bytes_accessed=int(cost * 3.69e6), transcendentals=0
        ),
        name=name,
    )(*args)


def other_core(values):
    count = lax.axis_size("rad")
    return lax.ppermute(values, "rad", [(index, index ^ 1) for index in range(count)])


def between_chips(values, pairs):
    route = [(2 * a + core, 2 * b + core) for a, b in pairs for core in range(2)]
    return lax.ppermute(values, "rad", route)


def hop(axis, values, bit):
    count = lax.axis_size(axis)
    return lax.ppermute(values, axis, [(index, index ^ (1 << bit)) for index in range(count)])


def on_device(source, helmholtz, azimuth, vertical, radial):
    length, cells, depth = source.shape
    blocks = lax.axis_size("rad")
    chips = blocks // 2
    total = blocks * cells
    assert cells == CELLS and depth == LANES and lax.axis_size("az") == SLABS
    assert chips % 2 == 0
    half = length // 2
    quarter = length // 8
    scalars4 = (helmholtz, azimuth, vertical, radial)
    kept = total * 5 * quarter * LANES * 4 <= 12 * 2**20
    room = 20 if kept else 56

    basis = cosine_basis(depth)
    stage, eigen, end_weights, parity = slab_tables(length)

    def matrices(stages, last):
        high, low = two_halves(stages.reshape(-1, stages.shape[-1]))
        return jnp.asarray(np.concatenate([high, low, wide_basis(last)]))

    vertical_eigen = 2.0 - 2.0 * np.cos(math.pi / depth * np.arange(depth))
    levels = np.broadcast_to(vertical_eigen[None, :], (8, depth)).astype(np.float32)
    lam = jnp.asarray(spread(eigen))
    ends = jnp.asarray(spread(end_weights))
    mu = jnp.asarray(levels)
    tables = jnp.asarray(np.concatenate([spread(eigen), levels]))
    by_slot = eigen.reshape(4, 2, quarter)
    lam_shared = jnp.asarray(
        spread(np.concatenate([by_slot[0, 0], by_slot[0, 1], by_slot[1:, 0].reshape(-1)]))
    )
    group = depth // SLABS
    mu_groups = jnp.asarray(
        np.tile(vertical_eigen.reshape(SLABS, group), (1, SLABS)).astype(np.float32)
    )

    def packed(column):
        table = np.stack([column[parity > 0], column[parity < 0]]).reshape(2 * quarter, SLABS)
        return jnp.asarray(np.repeat(table, group, axis=1).astype(np.float32))

    lam_groups = packed(eigen)
    weight_groups = packed(2.0 * end_weights**2)

    def smem(start):
        return tuple(range(start, start + 4))

    wide_shape = (2 * quarter, CELLS * LANES)
    stages = matrices(stage, basis)
    spectrum, keep, send = call(
        functools.partial(forward_kernel, total),
        [(CELLS, length, LANES), (2, half, LANES), (2, half, LANES)],
        (source.reshape(8, quarter * CELLS, LANES), tables, stages)
        + scalars4,
        (),
        [
            pltpu.VMEM((8, quarter * CELLS, LANES), F32),
            pltpu.VMEM(tables.shape, F32),
            pltpu.VMEM(stages.shape, BF16),
        ]
        + [pltpu.SMEM((total,), F32)] * 4
        + [pltpu.VMEM((length * CELLS, 2 * LANES), BF16)]
        + [pltpu.VMEM((4,) + wide_shape, BF16)] * 2
        + [pltpu.VMEM((CELLS, length, LANES), F32), pltpu.SemaphoreType.DMA((12,))],
        cost=8,
        held=tuple(range(7)),
        out_held=(0,),
        room=room,
        name="forward",
    )
    got = other_core(send)
    azimuth_ports, _ = lax.optimization_barrier((azimuth, send))
    (ports,) = call(
        functools.partial(pair_ports_kernel, total),
        [(11, half, LANES)],
        (lam, mu, helmholtz, azimuth_ports, vertical, radial),
        smem(2),
        cost=2,
        room=room,
        name="pair_ports",
    )
    line = (half, LANES)
    whole, out = call(
        functools.partial(merge_kernel, chips),
        [(2, half, LANES), line],
        (keep, got, ports),
        cost=0.3,
        room=room,
        name="merge",
    )

    out, azimuth_ratios = lax.optimization_barrier((out, azimuth))
    store_shape = (total, (5 if kept else 1) * quarter, LANES)
    edge_shape = (2, 5 * quarter, LANES)
    ratios_out = call(
        functools.partial(ratios_kernel, total, kept),
        [edge_shape] + ([store_shape] if kept else []),
        (lam_shared, mu, helmholtz, azimuth_ratios, vertical, radial),
        smem(2),
        [] if kept else [pltpu.VMEM(store_shape, F32)],
        cost=5,
        room=room,
        name="ratios",
    )
    edges, store = ratios_out[0], tuple(ratios_out[1:])
    scratch_store = [] if kept else [pltpu.VMEM(store_shape, F32)]
    (links,) = call(
        functools.partial(chain_links_kernel, chips),
        [(7, half, LANES)],
        (ports, edges),
        cost=0.5,
        room=room,
        name="links",
    )
    (response,) = call(
        functools.partial(response_kernel, total),
        [(2, total, LANES)],
        (lam_groups, weight_groups, mu_groups, helmholtz, azimuth_ratios, vertical, radial),
        smem(3),
        [
            pltpu.VMEM((total, 2 * quarter, LANES), F32),
            pltpu.VMEM((2, CELLS, total, 8, LANES), F32),
            pltpu.VMEM((2, CELLS, total, LANES), F32),
        ],
        cost=5,
        room=room,
        name="response",
    )
    (packed_ends,) = call(
        functools.partial(ends_kernel, total, kept),
        [(4, total, LANES)],
        (response, spectrum, lam, ends, mu) + scalars4 + store,
        smem(5),
        [pltpu.VMEM((2, total, 8, LANES), F32)] + scratch_store,
        cost=3,
        room=room,
        name="ends",
    )
    incoming = None
    whole_late, _ = lax.optimization_barrier((whole, packed_ends))
    for edge in range(chips // 2 - 1):
        moved = between_chips(out, [(edge, edge + 1), (chips - 1 - edge, chips - 2 - edge)])
        incoming = moved if incoming is None else incoming + moved
        (out,) = call(
            inward_kernel,
            [line],
            (whole_late, incoming, links),
            cost=0.3,
            room=room,
            name="inward",
        )

    def join(axis, bit, common, own, other):
        shape = (2 * own.shape[0] - common, total, LANES)
        (result,) = call(
            functools.partial(join_kernel, axis, bit, common),
            [shape],
            (own, other),
            cost=0.3,
            room=room,
            name="join",
        )
        return result

    gathered = packed_ends
    for bit in range(1, blocks.bit_length() - 1):
        moved = hop("rad", gathered, bit)
        gathered = join("rad", bit, 2, gathered, moved)
    gathered = join("rad", 0, 2, gathered, hop("rad", gathered, 0))
    matrix_shape = (total, total // SLABS, LANES)
    minus_matrix, alternate_matrix, plus_matrix = call(
        functools.partial(capacity_kernel, total),
        [matrix_shape] * 3,
        (azimuth, gathered),
        (0,),
        cost=4,
        room=room,
        name="capacity",
    )
    slab_ends = gathered[0:2]
    moved = hop("az", slab_ends, 0)
    slab_ends, _ = lax.optimization_barrier((slab_ends, minus_matrix))
    slab_ends = join("az", 0, 0, slab_ends, moved)
    middle_after = slab_ends
    azimuth_pair, _ = lax.optimization_barrier((azimuth, slab_ends))
    (pair_matrix,) = call(
        functools.partial(pair_kernel, total),
        [matrix_shape],
        (azimuth_pair, minus_matrix, plus_matrix),
        (0,),
        cost=3,
        room=room,
        name="pair",
    )
    moved = hop("az", slab_ends, 1)
    slab_ends, _ = lax.optimization_barrier((slab_ends, pair_matrix))
    slab_ends = join("az", 1, 0, slab_ends, moved)

    low, high = chips // 2 - 1, chips // 2
    other = between_chips(out, [(low, high), (high, low)])
    whole_last, _ = lax.optimization_barrier((whole, middle_after))
    near, far = call(
        functools.partial(middle_kernel, chips),
        [line, line],
        (whole_last, incoming, out, other, links),
        cost=0.3,
        room=room,
        name="middle",
    )
    passed = None
    for edge in range(chips // 2 - 2, -1, -1):
        moved = between_chips(far, [(edge + 1, edge), (chips - 2 - edge, chips - 1 - edge)])
        passed = moved if passed is None else passed + moved
        if edge > 0:
            (far,) = call(
                outward_kernel,
                [line],
                (whole, incoming, passed, links),
                cost=0.3,
                room=room,
                name="outward",
            )
    keep_sources, send_sources = call(
        functools.partial(slabs_kernel, total),
        [(SLABS, total, LANES)] * 2,
        (azimuth, minus_matrix, alternate_matrix, pair_matrix, slab_ends),
        (0,),
        [pltpu.VMEM((2 * SLABS, total, LANES), F32), pltpu.VMEM((8, total, LANES), F32)],
        cost=2,
        room=room,
        name="slabs",
    )
    moved = hop("az", send_sources, 1)
    keep_sources, send_sources = call(
        functools.partial(halve_kernel, "az", 0),
        [(2, total, LANES)] * 2,
        (keep_sources, moved),
        cost=0.3,
        room=room,
        name="halve",
    )
    whole_parts, _ = lax.optimization_barrier((whole, send_sources))
    own_sides, send_sides = call(
        functools.partial(parts_kernel, chips),
        [(2, half, LANES)] * 2,
        (keep, got, ports, links, whole_parts, incoming, near, passed),
        cost=0.4,
        room=room,
        name="parts",
    )
    got_sides = other_core(send_sides)
    sources = (keep_sources, hop("az", send_sources, 0))
    all_sources, extra = call(
        functools.partial(sides_kernel, total, kept),
        [(2, total, LANES), (2, length, LANES)],
        (lam, ends, mu) + scalars4 + sources + store,
        smem(3),
        scratch_store,
        cost=3,
        room=room,
        name="sides",
    )
    (pressure,) = call(
        functools.partial(backward_kernel, total),
        [(length * CELLS, LANES)],
        (
            spectrum,
            own_sides,
            got_sides,
            extra,
            all_sources,
            matrices(np.swapaxes(stage, 1, 2), basis.T),
            lam,
            ends,
            mu,
        )
        + scalars4,
        smem(9),
        [pltpu.VMEM((4,) + wide_shape, BF16)] * 2
        + [pltpu.VMEM((4,) + wide_shape, F32), pltpu.VMEM((length * CELLS, 2 * LANES), BF16)]
        + [pltpu.VMEM((length * CELLS, LANES), F32), pltpu.SemaphoreType.DMA((4,))],
        out_held=(0,),
        cost=7,
        room=room,
        name="backward",
    )
    return pressure.reshape(length, CELLS, LANES)


def solution(mesh):
    in_specs = (P("az", "rad", None), P(), P(), P(), P())
    return jax.shard_map(
        on_device,
        mesh=mesh,
        in_specs=in_specs,
        out_specs=P("az", "rad", None),
        check_vma=False,
    )
```
